32 devices in a mesh: dp: 8 (over z, y), mp: 4 (over x, core).
Axes of the slice: x: 2, y: 2, z: 4, core: 2. Of those that a mesh axis runs over, the one named last changes fastest.
Arguments:
- pixels: bfloat16 [8192, 3072], P('dp', 'mp'), may hold values from -6 to 6
- lengths: int32 [8, 8], P('dp'), may hold values from 25 to 576, as said below
- valid_mask: int32 [8192], P('dp'), may hold values from 0 to 1, as said below
- teacher_logits: float32 [64, 1000], P('dp'), may hold values from -12 to 12
- teacher_map: int32 [8], replicated, may hold values from 0 to 7, each once
- attend_in: float32 [3, 3, 768, 768], P(None, None, 'dp', 'mp'), may hold values from -0.21875 to 0.21875
- attend_out: float32 [3, 768, 768], P(None, 'mp', 'dp'), may hold values from -0.625 to 0.625
- hidden_up: float32 [3, 768, 3072], P(None, 'dp', 'mp'), may hold values from -0.21875 to 0.21875
- hidden_down: float32 [3, 3072, 768], P(None, 'mp', 'dp'), may hold values from -0.109375 to 0.109375
- patch_embed: float32 [3072, 768], P('mp', 'dp'), may hold values from -0.109375 to 0.109375
- class_head: float32 [768, 1000], P('dp'), may hold values from -0.21875 to 0.21875
- norm_params: float32 [7, 2, 768], P(None, None, 'dp'), may hold values from -0.9 to 2.2
- attend_in_first: float32 [3, 3, 768, 768], P(None, None, 'dp', 'mp'), may hold values from -7.1525574e-07 to 7.1525574e-07
- attend_out_first: float32 [3, 768, 768], P(None, 'mp', 'dp'), may hold values from -7.1525574e-07 to 7.1525574e-07
- hidden_up_first: float32 [3, 768, 3072], P(None, 'dp', 'mp'), may hold values from -7.1525574e-07 to 7.1525574e-07
- hidden_down_first: float32 [3, 3072, 768], P(None, 'mp', 'dp'), may hold values from -7.1525574e-07 to 7.1525574e-07
- patch_embed_first: float32 [3072, 768], P('mp', 'dp'), may hold values from -7.1525574e-07 to 7.1525574e-07
- class_head_first: float32 [768, 1000], P('dp'), may hold values from -7.1525574e-07 to 7.1525574e-07
- norm_params_first: float32 [7, 2, 768], P(None, None, 'dp'), may hold values from -1.9073486e-06 to 1.9073486e-06
- attend_in_second: float32 [3, 3, 768, 768], P(None, None, 'dp', 'mp'), may hold values from 1.0262321e-15 to 4.1049283e-15
- attend_out_second: float32 [3, 768, 768], P(None, 'mp', 'dp'), may hold values from 1.0262321e-15 to 4.1049283e-15
- hidden_up_second: float32 [3, 768, 3072], P(None, 'dp', 'mp'), may hold values from 1.0262321e-15 to 4.1049283e-15
- hidden_down_second: float32 [3, 3072, 768], P(None, 'mp', 'dp'), may hold values from 1.0262321e-15 to 4.1049283e-15
- patch_embed_second: float32 [3072, 768], P('mp', 'dp'), may hold values from 1.0262321e-15 to 4.1049283e-15
- class_head_second: float32 [768, 1000], P('dp'), may hold values from 1.0262321e-15 to 4.1049283e-15
- norm_params_second: float32 [7, 2, 768], P(None, None, 'dp'), may hold values from 9.23609e-15 to 3.694436e-14
Outputs:
- loss: float32 [], replicated
- grad_norm: float32 [], replicated
- attend_in_first_next: float32 [3, 3, 768, 768], P(None, None, 'dp', 'mp')
- attend_out_first_next: float32 [3, 768, 768], P(None, 'mp', 'dp')
- hidden_up_first_next: float32 [3, 768, 3072], P(None, 'dp', 'mp')
- hidden_down_first_next: float32 [3, 3072, 768], P(None, 'mp', 'dp')
- patch_embed_first_next: float32 [3072, 768], P('mp', 'dp')
- class_head_first_next: float32 [768, 1000], P('dp')
- norm_params_first_next: float32 [7, 2, 768], P(None, None, 'dp')
- attend_in_second_next: float32 [3, 3, 768, 768], P(None, None, 'dp', 'mp')
- attend_out_second_next: float32 [3, 768, 768], P(None, 'mp', 'dp')
- hidden_up_second_next: float32 [3, 768, 3072], P(None, 'dp', 'mp')
- hidden_down_second_next: float32 [3, 3072, 768], P(None, 'mp', 'dp')
- patch_embed_second_next: float32 [3072, 768], P('mp', 'dp')
- class_head_second_next: float32 [768, 1000], P('dp')
- norm_params_second_next: float32 [7, 2, 768], P(None, None, 'dp')
- attend_in_next: float32 [3, 3, 768, 768], P(None, None, 'dp', 'mp')
- attend_out_next: float32 [3, 768, 768], P(None, 'mp', 'dp')
- hidden_up_next: float32 [3, 768, 3072], P(None, 'dp', 'mp')
- hidden_down_next: float32 [3, 3072, 768], P(None, 'mp', 'dp')
- patch_embed_next: float32 [3072, 768], P('mp', 'dp')
- class_head_next: float32 [768, 1000], P('dp')
- norm_params_next: float32 [7, 2, 768], P(None, None, 'dp')
The draws below stay inside these ranges and needn't reach their ends.
Inputs may be any that keep to these rules, and one draw needn't show every extreme that they name: `lengths`: each row sums to 1024; one image of every device has exactly 576 tokens. `teacher_map`: a permutation of the dp indices. `valid_mask`: all tokens of one image of one device are 0.
All inputs are finite; a program needn't handle non-finite values.
Results may differ from the reference program's by a relative error of at most 0.018.
Values may be sent and summed in bfloat16 or wider, within the bound.
No kernel may reach another device: no remote copies, remote signals or barrier semaphores. Data moves between devices by JAX's collectives and lax.ppermute only.
A program may use at most 192 MiB of HBM per device.

```python
import math
import jax
import jax.numpy as jnp
from jax import lax

D = 768
HEADS = 12
HEAD_DIM = 64
FF = 3072
CLASSES = 1000
PIX = 3072
LAYERS = 3
TOK_DEV = 1024
IMG_DEV = 8
STEP = 10
MOST = 576
LEAST = 25
NORMS = 7
TOKENS = 8192
IMAGES = 64
N_DP = 8


def lengths_and_place(key):
    first, second = jax.random.split(key)
    extra = TOK_DEV - MOST - (IMG_DEV - 1) * LEAST
    cuts = jnp.sort(jax.random.randint(first, (N_DP, IMG_DEV - 2), 0, extra + 1), axis=1)
    bounds = jnp.concatenate([jnp.zeros((N_DP, 1), jnp.int32), cuts.astype(jnp.int32), jnp.full((N_DP, 1), extra, jnp.int32)], 1)
    pieces = bounds[:, 1:] - bounds[:, :-1] + LEAST
    place = jax.random.randint(second, (N_DP, 1), 0, IMG_DEV)
    slots = jnp.arange(IMG_DEV, dtype=jnp.int32)[None, :]
    source = jnp.clip(slots - (slots > place).astype(jnp.int32), 0, IMG_DEV - 2)
    others = jnp.take_along_axis(pieces, source, 1)
    lengths = jnp.where(slots == place, MOST, others).astype(jnp.int32)
    return (lengths, place)


def draw_lengths(key, part):
    lengths, place = lengths_and_place(key)
    return lengths


def draw_valid_mask(key, part):
    lengths, place = lengths_and_place(key)
    key = jax.random.fold_in(key, 7)
    first, second, third = jax.random.split(key, 3)
    kept = (jax.random.randint(first, (N_DP, TOK_DEV), 0, 8) < 7).astype(jnp.int32)
    device = jax.random.randint(second, (), 0, N_DP)
    image = (place[device, 0] + 1 + jax.random.randint(third, (), 0, IMG_DEV - 1)) % IMG_DEV
    ends = jnp.cumsum(lengths, 1)
    position = jnp.arange(TOK_DEV, dtype=jnp.int32)
    segment = jnp.sum((position[None, :, None] >= ends[:, None, :]).astype(jnp.int32), 2)
    empty = (jnp.arange(N_DP, dtype=jnp.int32)[:, None] == device) & (segment == image)
    return jnp.where(empty, 0, kept).astype(jnp.int32).reshape(TOKENS)


def draw_teacher_logits(key, part):
    key = jax.random.fold_in(key, 11)
    rows = jnp.arange(IMAGES, dtype=jnp.float32)[:, None]
    ramp = 1.0 + 2.0 * rows / max(IMAGES - 1, 1)
    base = jnp.clip(jax.random.normal(key, (IMAGES, CLASSES), jnp.float32), -4.0, 4.0)
    return base * ramp


def draw_norm_params(key, part):
    key = jax.random.fold_in(key, 5)
    first, second = jax.random.split(key)
    columns = jnp.arange(D, dtype=jnp.float32)[None, :] / D
    gain = (0.6 + 1.2 * columns) * jax.random.uniform(first, (NORMS, D), jnp.float32, 0.8, 1.2)
    bias = 0.3 * jnp.clip(jax.random.normal(second, (NORMS, D), jnp.float32), -3.0, 3.0)
    return jnp.stack([gain, bias], 1)


def block_scale(rng, dims, cuts, low, largest):
    level = 1.0
    for dim, parts in cuts:
        draws = jax.random.uniform(jax.random.fold_in(jax.random.fold_in(rng, 6), dim), (parts,), jnp.float32, low / len(cuts), largest / len(cuts))
        level = level * jnp.repeat(jnp.exp(draws), dims[dim] // parts).reshape((-1,) + (1,) * (len(dims) - 1 - dim))
    return level


def gaussian(key, extent, spread, bound, cuts=(), kind=jnp.bfloat16):
    level = block_scale(key, extent, cuts, -0.22, 0.18) if cuts else 1.0
    result = jax.random.normal(key, extent, jnp.float32) * spread * level
    return jnp.minimum(jnp.maximum(result, -bound), bound).astype(kind)


def setup_inputs(seed: int = 0) -> dict:
    arg_keys = jax.random.split(jax.random.key(seed), 27)
    pixels = gaussian(arg_keys[0], (TOKENS, PIX), 1.0, 6.0, ((0, 8), (1, 4)))
    lengths = draw_lengths(jax.random.fold_in(arg_keys[26], 71), 0)
    valid_mask = draw_valid_mask(jax.random.fold_in(arg_keys[26], 71), 0)
    teacher_logits = draw_teacher_logits(jax.random.fold_in(arg_keys[26], 71), 0)
    teacher_map = jax.random.permutation(arg_keys[4], N_DP).astype(jnp.int32)
    attend_in = gaussian(arg_keys[5], (LAYERS, 3, D, D), D ** -0.5, 0.21875, ((2, 8), (3, 4)), jnp.float32)
    attend_out = gaussian(arg_keys[6], (LAYERS, D, D), (D // 8) ** -0.5, 0.625, ((1, 4), (2, 8)), jnp.float32)
    hidden_up = gaussian(arg_keys[7], (LAYERS, D, FF), D ** -0.5, 0.21875, ((1, 8), (2, 4)), jnp.float32)
    hidden_down = gaussian(arg_keys[8], (LAYERS, FF, D), FF ** -0.5, 0.109375, ((1, 4), (2, 8)), jnp.float32)
    patch_embed = gaussian(arg_keys[9], (PIX, D), PIX ** -0.5, 0.109375, ((0, 4), (1, 8)), jnp.float32)
    class_head = gaussian(arg_keys[10], (D, CLASSES), D ** -0.5, 0.21875, ((0, 8),), jnp.float32)
    norm_params = draw_norm_params(jax.random.fold_in(arg_keys[26], 71), 0)
    attend_in_first = gaussian(arg_keys[12], (LAYERS, 3, D, D), (0.11 * (0.000025 / (LAYERS * (4 * D * D + 2 * D * FF) + PIX * D + D * CLASSES)) ** 0.5), 7.152557373046875e-07, ((2, 8), (3, 4)), jnp.float32)
    attend_out_first = gaussian(arg_keys[13], (LAYERS, D, D), (0.11 * (0.000025 / (LAYERS * (4 * D * D + 2 * D * FF) + PIX * D + D * CLASSES)) ** 0.5), 7.152557373046875e-07, ((1, 4), (2, 8)), jnp.float32)
    hidden_up_first = gaussian(arg_keys[14], (LAYERS, D, FF), (0.11 * (0.000025 / (LAYERS * (4 * D * D + 2 * D * FF) + PIX * D + D * CLASSES)) ** 0.5), 7.152557373046875e-07, ((1, 8), (2, 4)), jnp.float32)
    hidden_down_first = gaussian(arg_keys[15], (LAYERS, FF, D), (0.11 * (0.000025 / (LAYERS * (4 * D * D + 2 * D * FF) + PIX * D + D * CLASSES)) ** 0.5), 7.152557373046875e-07, ((1, 4), (2, 8)), jnp.float32)
    patch_embed_first = gaussian(arg_keys[16], (PIX, D), (0.11 * (0.000025 / (LAYERS * (4 * D * D + 2 * D * FF) + PIX * D + D * CLASSES)) ** 0.5), 7.152557373046875e-07, ((0, 4), (1, 8)), jnp.float32)
    class_head_first = gaussian(arg_keys[17], (D, CLASSES), (0.11 * (0.000025 / (LAYERS * (4 * D * D + 2 * D * FF) + PIX * D + D * CLASSES)) ** 0.5), 7.152557373046875e-07, ((0, 8),), jnp.float32)
    norm_params_first = gaussian(arg_keys[18], (NORMS, 2, D), (0.33 * (0.000025 / (LAYERS * (4 * D * D + 2 * D * FF) + PIX * D + D * CLASSES)) ** 0.5), 1.9073486328125e-06, ((2, 8),), jnp.float32)
    attend_in_second = jnp.clip(jnp.exp(math.log(4.1049283384334695e-15) - 1.3862944 * jax.random.uniform(arg_keys[19], (LAYERS, 3, D, D), jnp.float32) ** block_scale(arg_keys[19], (LAYERS, 3, D, D), ((2, 8), (3, 4)), -0.2, 0.2)), 1.0262320846083674e-15, 4.1049283384334695e-15)
    attend_out_second = jnp.clip(jnp.exp(math.log(4.1049283384334695e-15) - 1.3862944 * jax.random.uniform(arg_keys[20], (LAYERS, D, D), jnp.float32) ** block_scale(arg_keys[20], (LAYERS, D, D), ((1, 4), (2, 8)), -0.2, 0.2)), 1.0262320846083674e-15, 4.1049283384334695e-15)
    hidden_up_second = jnp.clip(jnp.exp(math.log(4.1049283384334695e-15) - 1.3862944 * jax.random.uniform(arg_keys[21], (LAYERS, D, FF), jnp.float32) ** block_scale(arg_keys[21], (LAYERS, D, FF), ((1, 8), (2, 4)), -0.2, 0.2)), 1.0262320846083674e-15, 4.1049283384334695e-15)
    hidden_down_second = jnp.clip(jnp.exp(math.log(4.1049283384334695e-15) - 1.3862944 * jax.random.uniform(arg_keys[22], (LAYERS, FF, D), jnp.float32) ** block_scale(arg_keys[22], (LAYERS, FF, D), ((1, 4), (2, 8)), -0.2, 0.2)), 1.0262320846083674e-15, 4.1049283384334695e-15)
    patch_embed_second = jnp.clip(jnp.exp(math.log(4.1049283384334695e-15) - 1.3862944 * jax.random.uniform(arg_keys[23], (PIX, D), jnp.float32) ** block_scale(arg_keys[23], (PIX, D), ((0, 4), (1, 8)), -0.2, 0.2)), 1.0262320846083674e-15, 4.1049283384334695e-15)
    class_head_second = jnp.clip(jnp.exp(math.log(4.1049283384334695e-15) - 1.3862944 * jax.random.uniform(arg_keys[24], (D, CLASSES), jnp.float32) ** block_scale(arg_keys[24], (D, CLASSES), ((0, 8),), -0.2, 0.2)), 1.0262320846083674e-15, 4.1049283384334695e-15)
    norm_params_second = jnp.clip(jnp.exp(math.log(3.6944358434033014e-14) - 1.3862944 * jax.random.uniform(arg_keys[25], (NORMS, 2, D), jnp.float32) ** block_scale(arg_keys[25], (NORMS, 2, D), ((2, 8),), -0.2, 0.2)), 9.236089608508254e-15, 3.6944358434033014e-14)
    return dict(pixels=pixels, lengths=lengths, valid_mask=valid_mask, teacher_logits=teacher_logits, teacher_map=teacher_map, attend_in=attend_in, attend_out=attend_out, hidden_up=hidden_up, hidden_down=hidden_down, patch_embed=patch_embed, class_head=class_head, norm_params=norm_params, attend_in_first=attend_in_first, attend_out_first=attend_out_first, hidden_up_first=hidden_up_first, hidden_down_first=hidden_down_first, patch_embed_first=patch_embed_first, class_head_first=class_head_first, norm_params_first=norm_params_first, attend_in_second=attend_in_second, attend_out_second=attend_out_second, hidden_up_second=hidden_up_second, hidden_down_second=hidden_down_second, patch_embed_second=patch_embed_second, class_head_second=class_head_second, norm_params_second=norm_params_second)


EPSILON = 1e-06
MASKED = -30000.0
CLIP = 0.005
BETA_ONE = 0.9
BETA_TWO = 0.999
ADAM_EPS = 1e-08
RATES = (0.02, 0.06, 0.02, 0.02, 0.02, 0.02, 0.5)
DECAYS = (0.05, 0.05, 0.05, 0.05, 0.05, 0.05, 0.0)
HIGH = lax.Precision.HIGHEST

@jax.custom_vjp
def low(v):
    return lax.optimization_barrier(v.astype(jnp.bfloat16)).astype(jnp.float32)

@jax.custom_vjp
def low_back(v):
    return v

def low_keep(v):
    return (low(v), None)

def low_pass(kept, grad):
    return (grad,)

def back_keep(v):
    return (v, None)

def back_low(kept, grad):
    return (low(grad),)
low.defvjp(low_keep, low_pass)
low_back.defvjp(back_keep, back_low)

def layer_norm(value, gain, bias):
    centred = value - lax.optimization_barrier(jnp.mean(value, -1, keepdims=True))
    variance = lax.optimization_barrier(jnp.mean(centred * centred, -1, keepdims=True))
    return centred * lax.rsqrt(variance + EPSILON) * gain + bias

def matmul(left, right):
    return jnp.dot(left, right, precision=HIGH)

def block_loss(weights, pixels, lengths, valid, teacher):
    attend_in, attend_out, hidden_up, hidden_down, patch_embed, class_head, norm_params = weights
    ntok = pixels.shape[0]
    position = jnp.arange(ntok, dtype=jnp.int32)
    ends = jnp.cumsum(lengths).astype(jnp.int32)
    segment = lax.optimization_barrier(jnp.sum((position[:, None] >= ends[None, :]).astype(jnp.int32), 1))
    keep = (segment[:, None] == segment[None, :]) & (valid[None, :] > 0)
    scale = HEAD_DIM ** (-0.5)
    x = low_back(matmul(pixels, patch_embed))
    for layer in range(LAYERS):
        normed = low(layer_norm(x, norm_params[2 * layer, 0], norm_params[2 * layer, 1]))
        mixed = jnp.einsum('td,jde->jte', normed, attend_in[layer], precision=HIGH)
        mixed = low(low_back(mixed))
        split = mixed.reshape(3, ntok, HEADS, HEAD_DIM).transpose(0, 2, 1, 3)
        scores = low_back(jnp.einsum('htc,hsc->hts', split[0], split[1], precision=HIGH) * scale)
        scores = jnp.where(keep[None], scores, MASKED)
        probs = low(jax.nn.softmax(scores, -1))
        attended = jnp.einsum('hts,hsc->htc', probs, split[2], precision=HIGH)
        attended = low(low_back(attended.transpose(1, 0, 2).reshape(ntok, D)))
        middle = x + low_back(matmul(attended, attend_out[layer]))
        normed_two = low(layer_norm(middle, norm_params[2 * layer + 1, 0], norm_params[2 * layer + 1, 1]))
        up_value = low_back(matmul(normed_two, hidden_up[layer]))
        active = low(jax.nn.gelu(up_value, approximate=False))
        x = middle + low_back(matmul(active, hidden_down[layer]))
    member = (segment[None, :] == jnp.arange(IMG_DEV, dtype=jnp.int32)[:, None]) & (valid[None, :] > 0)
    member = member.astype(jnp.float32)
    count = lax.optimization_barrier(jnp.sum(member, 1, keepdims=True))
    pooled = matmul(member, x) / jnp.maximum(count, 1.0)
    pooled_normed = low(layer_norm(pooled, norm_params[NORMS - 1, 0], norm_params[NORMS - 1, 1]))
    logits = low_back(matmul(pooled_normed, class_head))
    student = jax.nn.log_softmax(logits, -1)
    teach = jax.nn.log_softmax(teacher, -1)
    return jnp.sum(jnp.exp(teach) * (teach - student))

def adam(weight, grad, first, second, rate, decay):
    first = BETA_ONE * first + (1.0 - BETA_ONE) * grad
    second = BETA_TWO * second + (1.0 - BETA_TWO) * grad * grad
    update = first / (1.0 - BETA_ONE ** STEP) / (jnp.sqrt(second / (1.0 - BETA_TWO ** STEP)) + ADAM_EPS)
    return (first, second, weight - rate * (update + decay * weight))

def reference(pixels, lengths, valid_mask, teacher_logits, teacher_map, attend_in, attend_out, hidden_up, hidden_down, patch_embed, class_head, norm_params, attend_in_first, attend_out_first, hidden_up_first, hidden_down_first, patch_embed_first, class_head_first, norm_params_first, attend_in_second, attend_out_second, hidden_up_second, hidden_down_second, patch_embed_second, class_head_second, norm_params_second):
    masters = (attend_in, attend_out, hidden_up, hidden_down, patch_embed, class_head, norm_params)
    firsts = (attend_in_first, attend_out_first, hidden_up_first, hidden_down_first, patch_embed_first, class_head_first, norm_params_first)
    seconds = (attend_in_second, attend_out_second, hidden_up_second, hidden_down_second, patch_embed_second, class_head_second, norm_params_second)
    inverse = jnp.zeros((N_DP,), jnp.int32).at[teacher_map].set(jnp.arange(N_DP, dtype=jnp.int32))
    teacher = teacher_logits.reshape(N_DP, IMG_DEV, CLASSES)[inverse]
    blocks = (pixels.astype(jnp.float32).reshape(N_DP, TOK_DEV, PIX), lengths, valid_mask.reshape(N_DP, TOK_DEV), teacher)

    def total_loss(params):
        weights = tuple((low(w) for w in params))
        step = jax.checkpoint(lambda item: block_loss(weights, item[0], item[1], item[2], item[3]))
        return jnp.sum(lax.map(step, blocks))
    loss_sum, pull = jax.vjp(total_loss, masters)
    grads = pull(jnp.full((), 1.0 / IMAGES, jnp.float32))[0]
    grad_norm = jnp.sqrt(sum((jnp.sum(g * g) for g in grads)))
    clip = jnp.minimum(1.0, CLIP / grad_norm)
    results = []
    for kind in range(7):
        results.append(adam(masters[kind], grads[kind] * clip, firsts[kind], seconds[kind], RATES[kind], DECAYS[kind]))
    return (loss_sum, grad_norm, results[0][0], results[1][0], results[2][0], results[3][0], results[4][0], results[5][0], results[6][0], results[0][1], results[1][1], results[2][1], results[3][1], results[4][1], results[5][1], results[6][1], results[0][2], results[1][2], results[2][2], results[3][2], results[4][2], results[5][2], results[6][2])
```

```python
import jax
import jax.numpy as jnp
from jax import lax
from jax.sharding import PartitionSpec as P

HEAD_DIM = 64
LAYERS = 3
STEP = 10
MOST = 576

EPSILON = 1e-06
MASKED = -30000.0
CLIP = 0.005
BETA_ONE = 0.9
BETA_TWO = 0.999
ADAM_EPS = 1e-08
RATES = (0.02, 0.06, 0.02, 0.02, 0.02, 0.02, 0.5)
DECAYS = (0.05, 0.05, 0.05, 0.05, 0.05, 0.05, 0.0)
SQRT_HALF = 0.7071067811865476
INV_ROOT = 0.3989422804014327
HIGH = lax.Precision.HIGHEST
BF = jnp.bfloat16
F32 = jnp.float32

AXES = ("dp", "mp")
INNER = ("mp", 1)
OUTER = ("mp", 2)


def swap(value, bit):
    axis, mask = bit
    size = lax.axis_size(axis)
    return lax.ppermute(value, axis, [(i, i ^ mask) for i in range(size)])


def dp_bits():
    size = lax.axis_size("dp")
    bits = []
    mask = 1
    while mask < size:
        bits.append(("dp", mask))
        mask *= 2
    return bits


def dims_of(bits):
    return {bit: i for i, bit in enumerate([OUTER] + bits[::-1])}


def gather(value, order, dims):
    value = value.reshape((1,) * len(dims) + value.shape)
    for bit in order:
        value = jnp.concatenate([value, swap(value, bit)], dims[bit])
    return value


def scatter(value, order, dims):
    for bit in order:
        dim = dims[bit]
        keep = lax.index_in_dim(value, 0, dim)
        send = lax.index_in_dim(value, 1, dim)
        value = keep.astype(F32) + swap(send.astype(BF), bit).astype(F32)
        if bit is not order[-1]:
            value = value.astype(BF)
    return value.reshape(value.shape[len(dims) :])


def both(part):
    return part + swap(part.astype(BF), INNER).astype(F32)


def dot(left, right, contract):
    return lax.dot_general(left, right, ((contract[0:1], contract[1:2]), ((), ())), preferred_element_type=F32)


def nn(left, right):
    return dot(left, right, (1, 0))


def nt(left, right):
    return dot(left, right, (1, 1))


def tn(left, right):
    return dot(left, right, (0, 0))


def norm_stats(value):
    centred = value - jnp.mean(value, -1, keepdims=True)
    variance = jnp.mean(centred * centred, -1, keepdims=True)
    rstd = lax.rsqrt(variance + EPSILON)
    return centred * rstd, rstd


def layer_norm(value, norm):
    return norm_stats(value)[0] * norm[0] + norm[1]


def norm_back(value, norm, d_out):
    hat, rstd = norm_stats(value)
    d_hat = d_out * norm[0]
    d_value = rstd * (
        d_hat - jnp.mean(d_hat, -1, keepdims=True) - hat * jnp.mean(d_hat * hat, -1, keepdims=True)
    )
    return d_value, jnp.stack([jnp.sum(d_out * hat, 0), jnp.sum(d_out, 0)])


def split_heads(value):
    return value.reshape(value.shape[0], -1, HEAD_DIM).transpose(1, 0, 2)


def join_heads(value):
    return value.transpose(1, 0, 2).reshape(value.shape[1], -1)


def softmax_scores(query, key, keep):
    scores = jnp.einsum("htc,hsc->hts", query, key, preferred_element_type=F32) * HEAD_DIM ** (-0.5)
    return jax.nn.softmax(jnp.where(keep[None], scores, MASKED), -1)


def attend(query, key, value, keep):
    probs = softmax_scores(query, key, keep)
    return jnp.einsum("hts,hsc->htc", probs.astype(BF), value, preferred_element_type=F32)


def attend_back(query, key, value, d_out, keep):
    probs = softmax_scores(query, key, keep)
    d_probs = jnp.einsum("htc,hsc->hts", d_out, value, preferred_element_type=F32)
    delta = jnp.sum(probs * d_probs, -1, keepdims=True)
    d_scores = jnp.where(keep[None], probs * (d_probs - delta), 0.0).astype(BF)
    scale = HEAD_DIM ** (-0.5)
    d_query = jnp.einsum("hts,hsc->htc", d_scores, key, preferred_element_type=F32) * scale
    d_key = jnp.einsum("hts,htc->hsc", d_scores, query, preferred_element_type=F32) * scale
    d_value = jnp.einsum("hts,htc->hsc", probs.astype(BF), d_out, preferred_element_type=F32)
    return d_query.astype(BF), d_key.astype(BF), d_value.astype(BF)


def layer_forward(x, attn, ff, norms, keep):
    width = attn.shape[2] // 4
    normed = layer_norm(x, norms[0]).astype(BF)
    mixed = [
        jnp.concatenate([nn(normed, attn[o][:, j * width : (j + 1) * width]) for o in range(2)], 1).astype(BF)
        for j in range(3)
    ]
    heads = [split_heads(m) for m in mixed]
    attended = join_heads(attend(*heads, keep)).astype(BF)
    part = sum(nt(attended[:, o * width : (o + 1) * width], attn[o][:, 3 * width :]) for o in range(2))
    middle = x + both(part)
    hidden = ff.shape[2] // 2
    normed_two = layer_norm(middle, norms[1]).astype(BF)
    up = [nn(normed_two, ff[o][:, :hidden]) for o in range(2)]
    active = [jax.nn.gelu(u, approximate=False).astype(BF) for u in up]
    part = sum(nt(active[o], ff[o][:, hidden:]) for o in range(2))
    return middle + both(part), (x, middle, normed, heads, attended, normed_two, up, active)


def layer_backward(d_x, saved, attn, ff, norms, keep):
    x, middle, normed, heads, attended, normed_two, up, active = saved
    width = attn.shape[2] // 4
    hidden = ff.shape[2] // 2
    d_z = d_x.astype(BF)
    d_up = []
    g_ff = []
    for o in range(2):
        d_active = nn(d_z, ff[o][:, hidden:])
        slope = 0.5 * (1.0 + lax.erf(up[o] * SQRT_HALF)) + up[o] * jnp.exp(-0.5 * up[o] * up[o]) * INV_ROOT
        d_up.append((d_active * slope).astype(BF))
        g_ff.append(jnp.concatenate([tn(normed_two, d_up[o]).astype(BF), tn(d_z, active[o]).astype(BF)], 1))
    part = sum(nt(d_up[o], ff[o][:, :hidden]) for o in range(2))
    d_mid, g_norm_two = norm_back(middle, norms[1], both(part))
    d_mid = d_x + d_mid
    d_y = d_mid.astype(BF)
    d_att = jnp.concatenate([nn(d_y, attn[o][:, 3 * width :]) for o in range(2)], 1).astype(BF)
    d_heads = attend_back(*heads, split_heads(d_att), keep)
    d_mixed = [join_heads(h) for h in d_heads]
    g_attn = []
    part = 0.0
    for o in range(2):
        cols = slice(o * width, (o + 1) * width)
        g_attn.append(
            jnp.concatenate(
                [tn(normed, d_mixed[j][:, cols]).astype(BF) for j in range(3)] + [tn(d_y, attended[:, cols]).astype(BF)], 1
            )
        )
        for j in range(3):
            part = part + nt(d_mixed[j][:, cols], attn[o][:, j * width : (j + 1) * width])
    d_low, g_norm_one = norm_back(x, norms[0], both(part))
    return d_mid + d_low, jnp.stack(g_attn), jnp.stack(g_ff), jnp.stack([g_norm_one, g_norm_two])


def adam(weight, grad, first, second, rate, decay):
    first = BETA_ONE * first + (1.0 - BETA_ONE) * grad
    second = BETA_TWO * second + (1.0 - BETA_TWO) * grad * grad
    update = first / (1.0 - BETA_ONE**STEP) / (jnp.sqrt(second / (1.0 - BETA_TWO**STEP)) + ADAM_EPS)
    return (first, second, weight - rate * (update + decay * weight))


def body(pixels, lengths, valid_mask, teacher_logits, teacher_map, *state):
    masters, firsts, seconds = state[:7], state[7:14], state[14:]
    attend_in, attend_out, hidden_up, hidden_down, patch_embed, class_head, norm_params = masters
    bits = dp_bits()
    dims = dims_of(bits)
    low, high = bits[0], bits[1:]
    outer_last = high + [low, OUTER]
    low_last = high + [OUTER, low]
    rows = patch_embed.shape[1]
    inner = lax.axis_index("mp") % 2
    outer = lax.axis_index("mp") // 2
    images = lengths.shape[1]
    tokens = pixels.shape[0]
    total_images = images * lax.axis_size("dp")

    def cols(value):
        return value.astype(BF)

    patch_unit = cols(patch_embed.T)
    attn_units = [
        jnp.concatenate([cols(attend_in[l, j]) for j in range(3)] + [cols(attend_out[l].T)], 1) for l in range(LAYERS)
    ]
    ff_units = [jnp.concatenate([cols(hidden_up[l]), cols(hidden_down[l].T)], 1) for l in range(LAYERS)]
    half = class_head.shape[1] // 2
    head_unit = lax.dynamic_slice_in_dim(cols(class_head), inner * half, half, 1)

    def whole(unit, order):
        got = gather(unit, order, dims)
        return got.reshape(got.shape[0], -1, got.shape[-1])

    row = lengths[0]
    ends = jnp.cumsum(row)
    longest = jnp.argmax(row)
    start = ends[longest] - row[longest]
    place = jnp.arange(MOST, dtype=jnp.int32)

    def mine(value, which):
        twice = jnp.concatenate([value, value], 0)
        return lax.dynamic_slice_in_dim(twice, start + MOST * which, MOST, 0)

    pix = [mine(pixels, outer)]
    pix.append(swap(mine(pixels, 1 - outer), OUTER))
    held = jnp.where(outer == 0, MOST, tokens - MOST)
    position = (start + MOST * outer + place) % tokens
    segment = jnp.sum((position[:, None] >= ends[None, :]).astype(jnp.int32), 1)
    valid = jnp.where(place < held, mine(valid_mask, outer), 0) > 0
    keep = (segment[:, None] == segment[None, :]) & valid[None, :]
    image_ids = jnp.arange(images, dtype=jnp.int32)
    member = ((segment[None, :] == image_ids[:, None]) & valid[None, :]).astype(F32)
    owned = ((image_ids == longest) == (outer == 0)).astype(F32)[:, None]
    count = jnp.sum(member, 1)

    norms = gather(norm_params.astype(BF).reshape(-1, rows), high + [low], dims)
    norms = jnp.moveaxis(norms.reshape(-1, 7, 2, rows), 0, 2).reshape(7, 2, -1).astype(F32)

    patch = whole(patch_unit, outer_last)
    attn, ff = [], []
    for l in range(LAYERS):
        attn.append(whole(attn_units[l], low_last))
        ff.append(whole(ff_units[l], outer_last if l == 1 else low_last))
    head = whole(head_unit, high + [low])[0]

    teach_log = jax.nn.log_softmax(teacher_logits, -1)
    teach_log = gather(lax.dynamic_slice_in_dim(teach_log, inner * half, half, 1), high + [low], dims)
    teach_log = teach_log.reshape(-1, images, half)
    me = lax.axis_index("dp")
    source = jnp.sum(jnp.where(teacher_map == me, jnp.arange(teacher_map.shape[0], dtype=jnp.int32), 0))
    teach_log = lax.dynamic_index_in_dim(teach_log, jnp.bitwise_xor(source, me), 0, False)

    x = both(sum(nt(pix[o], patch[o]) for o in range(2)))
    saved = []
    for l in range(LAYERS):
        x, kept = layer_forward(x, attn[l], ff[l], norms[2 * l : 2 * l + 2], keep)
        saved.append(kept)

    divisor = jnp.maximum(count, 1.0)[:, None]
    pooled = jnp.dot(member, x, precision=HIGH) / divisor
    pooled_normed = layer_norm(pooled, norms[-1]).astype(BF)
    logits = nn(pooled_normed, head)
    theirs = swap(logits, INNER)
    peak = jnp.maximum(jnp.max(logits, -1, keepdims=True), jnp.max(theirs, -1, keepdims=True))
    total = jnp.sum(jnp.exp(logits - peak), -1, keepdims=True) + jnp.sum(jnp.exp(theirs - peak), -1, keepdims=True)
    student_log = logits - peak - jnp.log(total)
    loss_local = jnp.sum(owned * jnp.exp(teach_log) * (teach_log - student_log))
    d_logits = (owned * (jnp.exp(student_log) - jnp.exp(teach_log)) / total_images).astype(BF)
    g_head = tn(pooled_normed, d_logits).astype(BF)
    d_pooled, g_final = norm_back(pooled, norms[-1], both(nt(d_logits, head)))
    d_x = lax.dot_general(member, d_pooled / divisor, (((0,), (0,)), ((), ())), precision=HIGH)

    shape = (2,) * (1 + len(bits))

    def split(grad, order):
        return scatter(grad.reshape(shape + (rows, grad.shape[-1])), order[::-1], dims)

    g_attn, g_ff, g_norms = [None] * LAYERS, [None] * LAYERS, [None] * LAYERS
    g_head = scatter(g_head.reshape((1,) + shape[1:] + (rows, half)), (high + [low])[::-1], dims)
    for l in reversed(range(LAYERS)):
        d_x, g_a, g_f, g_norms[l] = layer_backward(d_x, saved[l], attn[l], ff[l], norms[2 * l : 2 * l + 2], keep)
        g_attn[l] = split(g_a, low_last)
        g_ff[l] = split(g_f, outer_last if l == 1 else low_last)
    d_x0 = d_x.astype(BF)
    g_patch = split(jnp.stack([tn(d_x0, p).astype(BF) for p in pix]), outer_last)

    g_head = g_head + swap(g_head, OUTER)
    other_half = swap(g_head, INNER)
    g_head = jnp.where(inner == 0, jnp.concatenate([g_head, other_half], 1), jnp.concatenate([other_half, g_head], 1))
    g_norm = jnp.concatenate(g_norms + [g_final[None]], 0).reshape(14, -1, rows)
    g_norm = jnp.moveaxis(g_norm, 1, 0).reshape((1,) + shape[1:] + (14, rows))
    for bit in (high + [low])[::-1]:
        g_norm = lax.index_in_dim(g_norm, 0, dims[bit]) + swap(lax.index_in_dim(g_norm, 1, dims[bit]), bit)
    g_norm = g_norm.reshape(14, rows)
    g_norm = g_norm + swap(g_norm, OUTER)
    other_norm = swap(g_norm, INNER)
    g_norm = (0.5 * (g_norm + other_norm)).reshape(7, 2, rows)

    width = attend_out.shape[1]
    hidden = hidden_up.shape[2]
    grads = (
        jnp.stack([jnp.stack([g[:, j * width : (j + 1) * width] for j in range(3)]) for g in g_attn]),
        jnp.stack([g[:, 3 * width :].T for g in g_attn]),
        jnp.stack([g[:, :hidden] for g in g_ff]),
        jnp.stack([g[:, hidden:].T for g in g_ff]),
        g_patch.T,
        g_head,
        g_norm,
    )
    first_model = (lax.axis_index("mp") == 0).astype(F32)
    squares = sum(jnp.sum(g * g) for g in g_attn + g_ff + [g_patch]) + first_model * (
        jnp.sum(g_head * g_head) + jnp.sum(g_norm * g_norm)
    )
    sums = jnp.stack([squares, loss_local * (outer >= 0)])
    for bit in [INNER, OUTER] + bits:
        sums = sums + swap(sums, bit)
    loss = sums[1]
    grad_norm = jnp.sqrt(sums[0])
    clip = jnp.minimum(1.0, CLIP / grad_norm)
    results = []
    for kind in range(7):
        results.append(
            adam(masters[kind], grads[kind] * clip, firsts[kind], seconds[kind], RATES[kind], DECAYS[kind])
        )
    return (loss, grad_norm) + tuple(r[i] for i in range(3) for r in results)


def solution(mesh):
    weights = (
        P(None, None, "dp", "mp"),
        P(None, "mp", "dp"),
        P(None, "dp", "mp"),
        P(None, "mp", "dp"),
        P("mp", "dp"),
        P("dp", None),
        P(None, None, "dp"),
    )
    placed = (P("dp", "mp"), P("dp", None), P("dp"), P("dp", None), P()) + weights * 3
    return jax.shard_map(
        body, mesh=mesh, in_specs=placed, out_specs=(P(), P()) + weights * 3, check_vma=False
    )
```

```python
import functools

import jax
import jax.numpy as jnp
from jax import lax
from jax.experimental import pallas as pl
from jax.experimental.pallas import tpu as pltpu
from jax.sharding import PartitionSpec as P

HEAD_DIM = 64
LAYERS = 3
STEP = 10
MOST = 576
FF_BLOCK = 256

EPSILON = 1e-06
MASKED = -30000.0
CLIP = 0.005
BETA_ONE = 0.9
BETA_TWO = 0.999
ADAM_EPS = 1e-08
RATES = (0.02, 0.06, 0.02, 0.02, 0.02, 0.02, 0.5)
DECAYS = (0.05, 0.05, 0.05, 0.05, 0.05, 0.05, 0.0)
SQRT_HALF = 0.7071067811865476
INV_ROOT = 0.3989422804014327
HIGH = lax.Precision.HIGHEST
BF = jnp.bfloat16
F32 = jnp.float32

AXES = ("dp", "mp")
INNER = ("mp", 1)
OUTER = ("mp", 2)


def swap(value, bit):
    axis, mask = bit
    size = lax.axis_size(axis)
    return lax.ppermute(value, axis, [(i, i ^ mask) for i in range(size)])


def dp_bits():
    size = lax.axis_size("dp")
    bits = []
    mask = 1
    while mask < size:
        bits.append(("dp", mask))
        mask *= 2
    return bits


def dims_of(bits):
    return {bit: i for i, bit in enumerate([OUTER, bits[0]] + bits[:0:-1])}


def gather(value, order, dims):
    value = value.reshape((1,) * len(dims) + value.shape)
    for bit in order:
        value = jnp.concatenate([value, swap(value, bit)], dims[bit])
    return value


def scatter(keep, send, order, dims):
    for bit, after in zip(order, order[1:] + [None]):
        value = keep.astype(F32) + swap(send.astype(BF), bit).astype(F32)
        if after is None:
            return value.reshape(value.shape[len(dims) :])
        value = value.astype(BF)
        keep = lax.index_in_dim(value, 0, dims[after])
        send = lax.index_in_dim(value, 1, dims[after])


def both(part):
    return part + swap(part.astype(BF), INNER).astype(F32)


def dot(left, right, contract):
    return lax.dot_general(left, right, ((contract[0:1], contract[1:2]), ((), ())), preferred_element_type=F32)


def nn(left, right):
    return dot(left, right, (1, 0))


def nt(left, right):
    return dot(left, right, (1, 1))


def tn(left, right):
    return dot(left, right, (0, 0))


def norm_stats(value):
    centred = value - jnp.mean(value, -1, keepdims=True)
    variance = jnp.mean(centred * centred, -1, keepdims=True)
    rstd = lax.rsqrt(variance + EPSILON)
    return centred * rstd, rstd


def layer_norm(value, norm):
    return norm_stats(value)[0] * norm[0:1] + norm[1:2]


def norm_back(value, norm, d_out):
    hat, rstd = norm_stats(value)
    d_hat = d_out * norm[0:1]
    d_value = rstd * (
        d_hat - jnp.mean(d_hat, -1, keepdims=True) - hat * jnp.mean(d_hat * hat, -1, keepdims=True)
    )
    return d_value, jnp.concatenate([jnp.sum(d_out * hat, 0, keepdims=True), jnp.sum(d_out, 0, keepdims=True)], 0)


def load_weight(w, a_ref, b_ref, half, by_outer):
    step = pl.program_id(0)
    rows = w.shape[0] // 2
    if by_outer:

        @pl.when(step < half)
        def _():
            w[:rows] = a_ref[0]
            w[rows:] = a_ref[1]

        @pl.when(step >= half)
        def _():
            w[:rows] = b_ref[0]
            w[rows:] = b_ref[1]

    else:
        w[:rows] = a_ref[0]
        w[rows:] = b_ref[0]


def store_grad(parts, a_ref, b_ref, half, by_outer):
    step = pl.program_id(0)

    def put(target, which, top):
        at = 0
        for part in parts:
            rows = part.shape[0] // 2
            value = part[:rows] if top else part[rows:]
            target[which, :, at : at + part.shape[1]] = value.astype(BF)
            at += part.shape[1]

    if by_outer:

        @pl.when(step < half)
        def _():
            put(a_ref, 0, True)
            put(a_ref, 1, False)

        @pl.when(step >= half)
        def _():
            put(b_ref, 0, True)
            put(b_ref, 1, False)

    else:
        put(a_ref, 0, True)
        put(b_ref, 0, False)


def half_specs(weight, columns, by_outer):
    half = weight.shape[2] // columns
    rows = weight.shape[1]
    if by_outer:
        return half, [
            pl.BlockSpec((2, rows, columns), lambda i: (0, 0, jnp.minimum(i, half - 1))),
            pl.BlockSpec((2, rows, columns), lambda i: (0, 0, jnp.maximum(i - half, 0))),
        ]
    return half, [pl.BlockSpec((1, rows, columns), lambda i: (i // half, 0, i % half))] * 2


def full(value):
    return pl.BlockSpec(value.shape, lambda i: (0,) * len(value.shape))


def spec_of(shape):
    return pl.BlockSpec(shape, lambda i: (0,) * len(shape))


def params():
    return pltpu.CompilerParams(dimension_semantics=("arbitrary",), vmem_limit_bytes=56 * 1024 * 1024)


def masked_probs(query, key, keep):
    scores = jnp.where(keep, nt(query, key) * HEAD_DIM ** (-0.5), MASKED)
    weight = jnp.exp(scores - jnp.max(scores, -1, keepdims=True))
    return weight / jnp.sum(weight, -1, keepdims=True)


def attn_fwd_kernel(count, half, by_outer, *refs):
    adds = refs[:count]
    norm, segq, segk, a_ref, b_ref, x_ref, mix_ref, part_ref, normed, w, acc = refs[count:]
    step = pl.program_id(0)

    @pl.when(step == 0)
    def _():
        x = adds[0][...]
        for other in adds[1:]:
            x = x + other[...].astype(F32)
        x_ref[...] = x
        normed[...] = layer_norm(x, norm[...]).astype(BF)
        acc[...] = jnp.zeros_like(acc)

    load_weight(w, a_ref, b_ref, half, by_outer)
    mixed = nn(normed[...], w[...]).astype(BF)
    c = HEAD_DIM
    keep = segq[...] == segk[...]
    probs = masked_probs(mixed[:, :c], mixed[:, c : 2 * c], keep)
    out = nn(probs.astype(BF), mixed[:, 2 * c : 3 * c]).astype(BF)
    mix_ref[0] = jnp.concatenate([mixed[:, : 3 * c], out], 1)
    acc[...] += nt(out, w[:, 3 * c :])

    @pl.when(step == pl.num_programs(0) - 1)
    def _():
        part_ref[...] = acc[...].astype(BF)


def attn_forward(adds, norm, segq, segk, pair, by_outer):
    tokens, width = adds[0].shape
    columns = 4 * HEAD_DIM
    half, halves = half_specs(pair[0], columns, by_outer)
    return pl.pallas_call(
        functools.partial(attn_fwd_kernel, len(adds), half, by_outer),
        grid=(2 * half,),
        in_specs=[full(v) for v in adds] + [full(norm), full(segq), full(segk)] + halves,
        out_specs=[
            spec_of((tokens, width)),
            pl.BlockSpec((1, tokens, columns), lambda i: (i, 0, 0)),
            spec_of((tokens, width)),
        ],
        out_shape=[
            jax.ShapeDtypeStruct((tokens, width), F32),
            jax.ShapeDtypeStruct((2 * half, tokens, columns), BF),
            jax.ShapeDtypeStruct((tokens, width), BF),
        ],
        scratch_shapes=[
            pltpu.VMEM((tokens, width), BF),
            pltpu.VMEM((width, columns), BF),
            pltpu.VMEM((tokens, width), F32),
        ],
        compiler_params=params(),
        cost_estimate=pl.CostEstimate(flops=16 * 10**9, bytes_accessed=10**7, transcendentals=10**6),
        name="attn_forward",
    )(*adds, norm, segq, segk, *pair)


def ff_fwd_kernel(count, half, by_outer, *refs):
    adds = refs[:count]
    norm, a_ref, b_ref, x_ref, part_ref, normed, w, acc = refs[count:]
    step = pl.program_id(0)

    @pl.when(step == 0)
    def _():
        x = adds[0][...]
        for other in adds[1:]:
            x = x + other[...].astype(F32)
        x_ref[...] = x
        normed[...] = layer_norm(x, norm[...]).astype(BF)
        acc[...] = jnp.zeros_like(acc)

    load_weight(w, a_ref, b_ref, half, by_outer)
    columns = w.shape[1] // 2
    up = nn(normed[...], w[:, :columns])
    active = (0.5 * up * (1.0 + lax.erf(up * SQRT_HALF))).astype(BF)
    acc[...] += nt(active, w[:, columns:])

    @pl.when(step == pl.num_programs(0) - 1)
    def _():
        part_ref[...] = acc[...].astype(BF)


def ff_forward(adds, norm, pair, by_outer):
    tokens, width = adds[0].shape
    columns = FF_BLOCK * 2
    half, halves = half_specs(pair[0], columns, by_outer)
    return pl.pallas_call(
        functools.partial(ff_fwd_kernel, len(adds), half, by_outer),
        grid=(2 * half,),
        in_specs=[full(v) for v in adds] + [full(norm)] + halves,
        out_specs=[spec_of((tokens, width)), spec_of((tokens, width))],
        out_shape=[
            jax.ShapeDtypeStruct((tokens, width), F32),
            jax.ShapeDtypeStruct((tokens, width), BF),
        ],
        scratch_shapes=[
            pltpu.VMEM((tokens, width), BF),
            pltpu.VMEM((width, columns), BF),
            pltpu.VMEM((tokens, width), F32),
        ],
        compiler_params=params(),
        cost_estimate=pl.CostEstimate(flops=10 * 10**9, bytes_accessed=10**7, transcendentals=10**6),
        name="ff_forward",
    )(*adds, norm, *pair)


def back_prologue(back, d_ref, g_ref):
    d_base = back[0][...]
    if len(back) == 1:
        d_ref[...] = d_base
        return d_base
    value, norm, own, other = back[1:]
    d_value, g_ref[...] = norm_back(value[...], norm[...], own[...].astype(F32) + other[...].astype(F32))
    d_all = d_base + d_value
    d_ref[...] = d_all
    return d_all


def ff_back_kernel(count, half, by_outer, *refs):
    back = refs[:count]
    value, norm, a_ref, b_ref, d_ref, ga_ref, gb_ref, part_ref, g_ref = refs[count : count + 9]
    normed, normed_t, dz, dz_t, w, acc = refs[count + 9 :]
    step = pl.program_id(0)

    @pl.when(step == 0)
    def _():
        d_all = back_prologue(back, d_ref, g_ref)
        dz[...] = d_all.astype(BF)
        dz_t[...] = d_all.T.astype(BF)
        here = layer_norm(value[...], norm[...])
        normed[...] = here.astype(BF)
        normed_t[...] = here.T.astype(BF)
        acc[...] = jnp.zeros_like(acc)

    load_weight(w, a_ref, b_ref, half, by_outer)
    columns = w.shape[1] // 2
    up = nn(normed[...], w[:, :columns])
    phi = 0.5 * (1.0 + lax.erf(up * SQRT_HALF))
    active = (up * phi).astype(BF)
    slope = phi + up * jnp.exp(-0.5 * up * up) * INV_ROOT
    d_up = (nn(dz[...], w[:, columns:]) * slope).astype(BF)
    acc[...] += nt(d_up, w[:, :columns])
    store_grad([nn(normed_t[...], d_up), nn(dz_t[...], active)], ga_ref, gb_ref, half, by_outer)

    @pl.when(step == pl.num_programs(0) - 1)
    def _():
        part_ref[...] = acc[...].astype(BF)


def back_out(tokens, width, pair, halves):
    specs = [spec_of((tokens, width))] + halves + [spec_of((tokens, width)), spec_of((2, width))]
    shapes = [
        jax.ShapeDtypeStruct((tokens, width), F32),
        jax.ShapeDtypeStruct(pair[0].shape, BF),
        jax.ShapeDtypeStruct(pair[0].shape, BF),
        jax.ShapeDtypeStruct((tokens, width), BF),
        jax.ShapeDtypeStruct((2, width), F32),
    ]
    return specs, shapes


def ff_backward(back, value, norm, pair, by_outer):
    tokens, width = value.shape
    columns = FF_BLOCK * 2
    half, halves = half_specs(pair[0], columns, by_outer)
    specs, shapes = back_out(tokens, width, pair, halves)
    return pl.pallas_call(
        functools.partial(ff_back_kernel, len(back), half, by_outer),
        grid=(2 * half,),
        in_specs=[full(v) for v in back] + [full(value), full(norm)] + halves,
        out_specs=specs,
        out_shape=shapes,
        scratch_shapes=[
            pltpu.VMEM((tokens, width), BF),
            pltpu.VMEM((width, tokens), BF),
            pltpu.VMEM((tokens, width), BF),
            pltpu.VMEM((width, tokens), BF),
            pltpu.VMEM((width, columns), BF),
            pltpu.VMEM((tokens, width), F32),
        ],
        compiler_params=params(),
        cost_estimate=pl.CostEstimate(flops=18 * 10**9, bytes_accessed=10**7, transcendentals=10**6),
        name="ff_backward",
    )(*back, value, norm, *pair)


def attn_back_kernel(count, half, by_outer, *refs):
    back = refs[:count]
    value, norm, segq, segk, mix_ref, a_ref, b_ref, d_ref, ga_ref, gb_ref, part_ref, g_ref = refs[count : count + 12]
    normed_t, dy, dy_t, w, acc = refs[count + 12 :]
    step = pl.program_id(0)

    @pl.when(step == 0)
    def _():
        d_all = back_prologue(back, d_ref, g_ref)
        dy[...] = d_all.astype(BF)
        dy_t[...] = d_all.T.astype(BF)
        normed_t[...] = layer_norm(value[...], norm[...]).T.astype(BF)
        acc[...] = jnp.zeros_like(acc)

    load_weight(w, a_ref, b_ref, half, by_outer)
    c = HEAD_DIM
    scale = HEAD_DIM ** (-0.5)
    query, key, val = (mix_ref[0, :, j * c : (j + 1) * c] for j in range(3))
    d_out = nn(dy[...], w[:, 3 * c :]).astype(BF)
    keep = segq[...] == segk[...]
    probs = masked_probs(query, key, keep)
    d_probs = nt(d_out, val)
    delta = jnp.sum(probs * d_probs, -1, keepdims=True)
    d_scores = jnp.where(keep, probs * (d_probs - delta), 0.0).astype(BF)
    d_query = (nn(d_scores, key) * scale).astype(BF)
    d_key = (tn(d_scores, query) * scale).astype(BF)
    d_val = tn(probs.astype(BF), d_out).astype(BF)
    d_left = jnp.concatenate([d_query, d_key], 1)
    zero = jnp.zeros_like(d_val)
    d_right = jnp.concatenate([d_val, zero], 1)
    out = jnp.concatenate([zero, mix_ref[0, :, 3 * c :]], 1)
    acc[...] += nt(d_left, w[:, : 2 * c]) + nt(d_right, w[:, 2 * c :])
    left = nn(normed_t[...], d_left)
    right = nn(normed_t[...], d_right) + nn(dy_t[...], out)
    store_grad([left, right], ga_ref, gb_ref, half, by_outer)

    @pl.when(step == pl.num_programs(0) - 1)
    def _():
        part_ref[...] = acc[...].astype(BF)


def attn_backward(back, value, norm, segq, segk, mix, pair, by_outer):
    tokens, width = value.shape
    columns = 4 * HEAD_DIM
    half, halves = half_specs(pair[0], columns, by_outer)
    specs, shapes = back_out(tokens, width, pair, halves)
    return pl.pallas_call(
        functools.partial(attn_back_kernel, len(back), half, by_outer),
        grid=(2 * half,),
        in_specs=[full(v) for v in back]
        + [full(value), full(norm), full(segq), full(segk)]
        + [pl.BlockSpec((1, tokens, columns), lambda i: (i, 0, 0))]
        + halves,
        out_specs=specs,
        out_shape=shapes,
        scratch_shapes=[
            pltpu.VMEM((width, tokens), BF),
            pltpu.VMEM((tokens, width), BF),
            pltpu.VMEM((width, tokens), BF),
            pltpu.VMEM((width, columns), BF),
            pltpu.VMEM((tokens, width), F32),
        ],
        compiler_params=params(),
        cost_estimate=pl.CostEstimate(flops=30 * 10**9, bytes_accessed=10**7, transcendentals=10**6),
        name="attn_backward",
    )(*back, value, norm, segq, segk, mix, *pair)


def adam(weight, grad, first, second, rate, decay):
    first = BETA_ONE * first + (1.0 - BETA_ONE) * grad
    second = BETA_TWO * second + (1.0 - BETA_TWO) * grad * grad
    update = first / (1.0 - BETA_ONE**STEP) / (jnp.sqrt(second / (1.0 - BETA_TWO**STEP)) + ADAM_EPS)
    return (first, second, weight - rate * (update + decay * weight))


def body(pixels, lengths, valid_mask, teacher_logits, teacher_map, *state):
    masters, firsts, seconds = state[:7], state[7:14], state[14:]
    attend_in, attend_out, hidden_up, hidden_down, patch_embed, class_head, norm_params = masters
    bits = dp_bits()
    dims = dims_of(bits)
    low, high = bits[0], bits[1:]
    outer_last = high + [low, OUTER]
    low_last = high + [OUTER, low]
    rows = patch_embed.shape[1]
    inner = lax.axis_index("mp") % 2
    outer = lax.axis_index("mp") // 2
    images = lengths.shape[1]
    tokens = pixels.shape[0]
    total_images = images * lax.axis_size("dp")

    heads = attend_in.shape[3] // HEAD_DIM
    hidden = hidden_up.shape[2]
    width = attend_out.shape[2] * lax.axis_size("dp")

    def attn_unit(l):
        into = attend_in[l].astype(BF).reshape(3, rows, heads, HEAD_DIM)
        out = attend_out[l].T.astype(BF).reshape(1, rows, heads, HEAD_DIM)
        return jnp.concatenate([into, out], 0).transpose(1, 2, 0, 3).reshape(rows, -1)

    def ff_unit(l):
        up = hidden_up[l].astype(BF).reshape(rows, -1, 1, FF_BLOCK)
        down = hidden_down[l].T.astype(BF).reshape(rows, -1, 1, FF_BLOCK)
        return jnp.concatenate([up, down], 2).reshape(rows, -1)

    half = class_head.shape[1] // 2
    head_unit = lax.dynamic_slice_in_dim(class_head.astype(BF), inner * half, half, 1)

    def pair_of(unit, order):
        own = gather(unit, order[:-1], dims)
        other = swap(own, order[-1])
        return tuple(v.reshape(2, width // 2, v.shape[-1]) for v in (own, other))

    row = lengths[0]
    ends = jnp.cumsum(row)
    longest = jnp.argmax(row)
    start = ends[longest] - row[longest]
    place = jnp.arange(MOST, dtype=jnp.int32)

    def mine(value, which):
        twice = jnp.concatenate([value, value], 0)
        return lax.dynamic_slice_in_dim(twice, start + MOST * which, MOST, 0)

    pix = [mine(pixels, outer), mine(pixels, 1 - outer)]
    held = jnp.where(outer == 0, MOST, tokens - MOST)
    position = (start + MOST * outer + place) % tokens
    segment = jnp.sum((position[:, None] >= ends[None, :]).astype(jnp.int32), 1)
    valid = jnp.where(place < held, mine(valid_mask, outer), 0) > 0
    segq = segment[:, None]
    segk = jnp.where(valid, segment, -1)[None, :]
    image_ids = jnp.arange(images, dtype=jnp.int32)
    member = ((segment[None, :] == image_ids[:, None]) & valid[None, :]).astype(F32)
    owned = ((image_ids == longest) == (outer == 0)).astype(F32)[:, None]
    count = jnp.sum(member, 1)

    norms = gather(norm_params.astype(BF).reshape(-1, rows), high + [low], dims)
    norms = jnp.moveaxis(norms.reshape(-1, 7, 2, rows), 0, 2).reshape(7, 2, -1).astype(F32)

    patch = gather(patch_embed.T.astype(BF), high + [low], dims).reshape(width, -1)
    attn_outer = [True, False, True]
    ff_outer = [False, True, False]
    orders = {True: outer_last, False: low_last}
    attn, ff = [], []
    for l in range(LAYERS):
        attn.append(pair_of(attn_unit(l), orders[attn_outer[l]]))
        ff.append(pair_of(ff_unit(l), orders[ff_outer[l]]))
    head = gather(head_unit, high + [low], dims).reshape(width, half)

    teach_log = jax.nn.log_softmax(teacher_logits, -1)
    teach_log = gather(lax.dynamic_slice_in_dim(teach_log, inner * half, half, 1), high + [low], dims)
    teach_log = jnp.swapaxes(teach_log.reshape((2, -1, images, half)), 0, 1).reshape(-1, images, half)
    me = lax.axis_index("dp")
    source = jnp.sum(jnp.where(teacher_map == me, jnp.arange(teacher_map.shape[0], dtype=jnp.int32), 0))
    teach_log = lax.dynamic_index_in_dim(teach_log, jnp.bitwise_xor(source, me), 0, False)

    mid = width // 2

    def of_inner(value, which):
        return jnp.where(which == 0, value[..., :mid], value[..., mid:])

    part = nt(jnp.concatenate(pix, 0), patch).astype(BF)
    part = of_inner(part, inner).astype(F32) + swap(of_inner(part, 1 - inner), INNER).astype(F32)
    part = part[:MOST] + swap(part[MOST:].astype(BF), OUTER).astype(F32)
    other = swap(part, INNER)
    x = jnp.where(inner == 0, jnp.concatenate([part, other], 1), jnp.concatenate([other, part], 1))

    adds = [x]
    xs, middles, mixes = [], [], []
    for l in range(LAYERS):
        x, mix, own = attn_forward(adds, norms[2 * l], segq, segk, attn[l], attn_outer[l])
        middle, own = ff_forward([x, own, swap(own, INNER)], norms[2 * l + 1], ff[l], ff_outer[l])
        adds = [middle, own, swap(own, INNER)]
        xs.append(x)
        middles.append(middle)
        mixes.append(mix)
    x = sum(v.astype(F32) for v in adds)

    divisor = jnp.maximum(count, 1.0)[:, None]
    pooled = jnp.dot(member, x, precision=HIGH) / divisor
    pooled_normed = layer_norm(pooled, norms[-1]).astype(BF)
    logits = nn(pooled_normed, head)
    theirs = swap(logits, INNER)
    peak = jnp.maximum(jnp.max(logits, -1, keepdims=True), jnp.max(theirs, -1, keepdims=True))
    total = jnp.sum(jnp.exp(logits - peak), -1, keepdims=True) + jnp.sum(jnp.exp(theirs - peak), -1, keepdims=True)
    student_log = logits - peak - jnp.log(total)
    loss_local = jnp.sum(owned * jnp.exp(teach_log) * (teach_log - student_log))
    d_logits = (owned * (jnp.exp(student_log) - jnp.exp(teach_log)) / total_images).astype(BF)
    g_head = tn(pooled_normed, d_logits).astype(BF)
    d_pooled, g_final = norm_back(pooled, norms[-1], both(nt(d_logits, head)))
    d_x = lax.dot_general(member, d_pooled / divisor, (((0,), (0,)), ((), ())), precision=HIGH)

    shape = (1,) + (2,) * len(bits)

    def halved(grad):
        grad = grad.reshape(shape + (rows, grad.shape[-1]))
        return lax.index_in_dim(grad, 0, dims[low]), lax.index_in_dim(grad, 1, dims[low])

    def split(keep, send, by_outer):
        order = orders[by_outer][::-1]
        lead = list((2,) * (1 + len(bits)))
        lead[dims[order[0]]] = 1
        keep, send = (v.reshape(tuple(lead) + (rows, v.shape[-1])) for v in (keep, send))
        return scatter(keep, send, order, dims)

    dp_order = (high + [low])[::-1]
    g_attn, g_ff, g_norms = [None] * LAYERS, [None] * LAYERS, [None] * LAYERS
    g_head = scatter(*halved(g_head), dp_order, dims)
    back = [d_x]
    for l in reversed(range(LAYERS)):
        d_x, keep, send, own, g_above = ff_backward(back, middles[l], norms[2 * l + 1], ff[l], ff_outer[l])
        if l < LAYERS - 1:
            g_norms[l + 1].insert(0, g_above)
        g_ff[l] = split(keep, send, ff_outer[l])
        back = [d_x, middles[l], norms[2 * l + 1], own, swap(own, INNER)]
        d_mid, keep, send, own, g_two = attn_backward(
            back, xs[l], norms[2 * l], segq, segk, mixes[l], attn[l], attn_outer[l]
        )
        g_norms[l] = [g_two]
        g_attn[l] = split(keep, send, attn_outer[l])
        back = [d_mid, xs[l], norms[2 * l], own, swap(own, INNER)]
    d_low, g_one = norm_back(xs[0], norms[0], back[3].astype(F32) + back[4].astype(F32))
    g_norms[0].insert(0, g_one)
    d_x0 = (back[0] + d_low).astype(BF)
    theirs = swap(of_inner(d_x0, inner), OUTER)
    other = swap(theirs, INNER)
    theirs = jnp.where(inner == 0, jnp.concatenate([theirs, other], 1), jnp.concatenate([other, theirs], 1))
    g_patch = tn(jnp.concatenate([d_x0, theirs], 0), jnp.concatenate(pix, 0)).astype(BF)
    g_patch = scatter(*halved(g_patch), dp_order, dims)

    g_head = g_head + swap(g_head, OUTER)
    other_half = swap(g_head, INNER)
    g_head = jnp.where(inner == 0, jnp.concatenate([g_head, other_half], 1), jnp.concatenate([other_half, g_head], 1))
    g_norm = jnp.stack([g for pair in g_norms for g in pair] + [g_final]).reshape(14, -1, rows)
    g_norm = jnp.moveaxis(g_norm, 1, 0).reshape(shape + (14, rows))
    for bit in dp_order:
        g_norm = lax.index_in_dim(g_norm, 0, dims[bit]) + swap(lax.index_in_dim(g_norm, 1, dims[bit]), bit)
    g_norm = g_norm.reshape(14, rows)
    g_norm = g_norm + swap(g_norm, OUTER)
    other_norm = swap(g_norm, INNER)
    g_norm = (0.5 * (g_norm + other_norm)).reshape(7, 2, rows)

    g_attn_heads = [g.reshape(rows, heads, 4, HEAD_DIM) for g in g_attn]
    g_ff_blocks = [g.reshape(rows, -1, 2, FF_BLOCK) for g in g_ff]
    grads = (
        jnp.stack([jnp.stack([g[:, :, j].reshape(rows, -1) for j in range(3)]) for g in g_attn_heads]),
        jnp.stack([g[:, :, 3].reshape(rows, -1).T for g in g_attn_heads]),
        jnp.stack([g[:, :, 0].reshape(rows, -1) for g in g_ff_blocks]),
        jnp.stack([g[:, :, 1].reshape(rows, -1).T for g in g_ff_blocks]),
        g_patch.T,
        g_head,
        g_norm,
    )
    first_model = (lax.axis_index("mp") == 0).astype(F32)
    squares = sum(jnp.sum(g * g) for g in g_attn + g_ff + [g_patch]) + first_model * (
        jnp.sum(g_head * g_head) + jnp.sum(g_norm * g_norm)
    )
    sums = jnp.stack([squares, loss_local * (outer >= 0)])
    for bit in [INNER, OUTER] + bits:
        sums = sums + swap(sums, bit)
    loss = sums[1]
    grad_norm = jnp.sqrt(sums[0])
    clip = jnp.minimum(1.0, CLIP / grad_norm)
    results = []
    for kind in range(7):
        results.append(
            adam(masters[kind], grads[kind] * clip, firsts[kind], seconds[kind], RATES[kind], DECAYS[kind])
        )
    return (loss, grad_norm) + tuple(r[i] for i in range(3) for r in results)


def solution(mesh):
    weights = (
        P(None, None, "dp", "mp"),
        P(None, "mp", "dp"),
        P(None, "dp", "mp"),
        P(None, "mp", "dp"),
        P("mp", "dp"),
        P("dp", None),
        P(None, None, "dp"),
    )
    placed = (P("dp", "mp"), P("dp", None), P("dp"), P("dp", None), P()) + weights * 3
    return jax.shard_map(
        body, mesh=mesh, in_specs=placed, out_specs=(P(), P()) + weights * 3, check_vma=False
    )
```

```python
import functools

import jax
import jax.numpy as jnp
from jax import lax
from jax.experimental import pallas as pl
from jax.experimental.pallas import tpu as pltpu
from jax.sharding import PartitionSpec as P

HEAD_DIM = 64
LAYERS = 3
STEP = 10
MOST = 576
FF_BLOCK = 256

EPSILON = 1e-06
MASKED = -30000.0
CLIP = 0.005
BETA_ONE = 0.9
BETA_TWO = 0.999
ADAM_EPS = 1e-08
RATES = (0.02, 0.06, 0.02, 0.02, 0.02, 0.02, 0.5)
DECAYS = (0.05, 0.05, 0.05, 0.05, 0.05, 0.05, 0.0)
SQRT_HALF = 0.7071067811865476
INV_ROOT = 0.3989422804014327
HIGH = lax.Precision.HIGHEST
BF = jnp.bfloat16
F32 = jnp.float32

AXES = ("dp", "mp")
INNER = ("mp", 1)
OUTER = ("mp", 2)
LOW = ("dp", 1)
FIRST = (LOW, OUTER)
SECOND = (OUTER, LOW)


def swap(value, bit):
    n_dp, n_mp = (lax.axis_size(axis) for axis in AXES)
    pairs = []
    for dp in range(n_dp):
        for mp in range(n_mp):
            axis, mask = bit if isinstance(bit[0], str) else bit[mp % 2]
            to = (dp ^ mask) * n_mp + mp if axis == "dp" else dp * n_mp + (mp ^ mask)
            pairs.append((dp * n_mp + mp, to))
    return lax.ppermute(value, AXES, pairs)


class Steps:
    def __init__(self):
        self.before = []
        self.made = []

    def next(self):
        self.before, self.made = self.made, []

    def tie(self, value):
        if not self.before:
            return value
        return lax.optimization_barrier((value, *self.before))[0]

    def add(self, value):
        self.made.append(value)
        return value

    def swap(self, value, bit):
        return self.add(swap(self.tie(value), bit))


def dp_bits():
    size = lax.axis_size("dp")
    bits = []
    mask = 1
    while mask < size:
        bits.append(("dp", mask))
        mask *= 2
    return bits


def both(part):
    return part + swap(part.astype(BF), INNER).astype(F32)


def dot(left, right, contract):
    return lax.dot_general(left, right, ((contract[0:1], contract[1:2]), ((), ())), preferred_element_type=F32)


def nn(left, right):
    return dot(left, right, (1, 0))


def nt(left, right):
    return dot(left, right, (1, 1))


def tn(left, right):
    return dot(left, right, (0, 0))


def norm_stats(value):
    centred = value - jnp.mean(value, -1, keepdims=True)
    variance = jnp.mean(centred * centred, -1, keepdims=True)
    rstd = lax.rsqrt(variance + EPSILON)
    return centred * rstd, rstd


def layer_norm(value, norm):
    return norm_stats(value)[0] * norm[0:1] + norm[1:2]


def norm_back(value, norm, d_out):
    hat, rstd = norm_stats(value)
    d_hat = d_out * norm[0:1]
    d_value = rstd * (
        d_hat - jnp.mean(d_hat, -1, keepdims=True) - hat * jnp.mean(d_hat * hat, -1, keepdims=True)
    )
    return d_value, jnp.concatenate([jnp.sum(d_out * hat, 0, keepdims=True), jnp.sum(d_out, 0, keepdims=True)], 0)


def load_weight(w, flag, own, near, across, both_ways):
    outer = pl.program_id(0) % 2
    rows = w.shape[0] // 2

    @pl.when(outer == 0)
    def _():
        w[:rows] = own[...]

    @pl.when(outer == 1)
    def _():
        w[rows:] = both_ways[...]

    @pl.when((outer == 0) & (flag[0] == 0))
    def _():
        w[rows:] = across[...]

    @pl.when((outer == 0) & (flag[0] == 1))
    def _():
        w[rows:] = near[...]

    @pl.when((outer == 1) & (flag[0] == 0))
    def _():
        w[:rows] = near[...]

    @pl.when((outer == 1) & (flag[0] == 1))
    def _():
        w[:rows] = across[...]


def store_grad(parts, flag, own, near, across, both_ways):
    outer = pl.program_id(0) % 2

    def put(target, top):
        at = 0
        for part in parts:
            rows = part.shape[0] // 2
            value = part[:rows] if top else part[rows:]
            target[:, at : at + part.shape[1]] = value.astype(BF)
            at += part.shape[1]

    @pl.when(outer == 0)
    def _():
        put(own, True)

    @pl.when(outer == 1)
    def _():
        put(both_ways, False)

    @pl.when((outer == 0) & (flag[0] == 0))
    def _():
        put(across, False)

    @pl.when((outer == 0) & (flag[0] == 1))
    def _():
        put(near, False)

    @pl.when((outer == 1) & (flag[0] == 0))
    def _():
        put(near, True)

    @pl.when((outer == 1) & (flag[0] == 1))
    def _():
        put(across, True)


def quarter_specs(weight, columns):
    steps = 2 * (weight.shape[1] // columns)
    return steps, [pl.BlockSpec((weight.shape[0], columns), lambda i: (0, i // 2))] * 4


def full(value):
    return pl.BlockSpec(value.shape, lambda i: (0,) * len(value.shape))


def spec_of(shape):
    return pl.BlockSpec(shape, lambda i: (0,) * len(shape))


FLAG = pl.BlockSpec(memory_space=pltpu.SMEM)
NO_COST = pl.CostEstimate(flops=10**6, bytes_accessed=10**4, transcendentals=0)


def params():
    return pltpu.CompilerParams(dimension_semantics=("arbitrary",), vmem_limit_bytes=56 * 1024 * 1024)


def masked_probs(scaled_query, key, keep):
    scores = jnp.where(keep, nt(scaled_query, key), MASKED)
    weight = jnp.exp(scores - jnp.max(scores, -1, keepdims=True))
    return weight * (1.0 / jnp.sum(weight, -1, keepdims=True))


def attn_fwd_kernel(count, *refs):
    flag = refs[0]
    adds = refs[1 : count + 1]
    norm, segq, segk, *weight, x_ref, mix_ref, part_ref, normed, w, acc = refs[count + 1 :]
    step = pl.program_id(0)

    @pl.when(step == 0)
    def _():
        x = adds[0][...]
        for other in adds[1:]:
            x = x + other[...].astype(F32)
        x_ref[...] = x
        normed[...] = layer_norm(x, norm[...]).astype(BF)
        acc[...] = jnp.zeros_like(acc)

    load_weight(w, flag, *weight)
    mixed = nn(normed[...], w[...]).astype(BF)
    c = HEAD_DIM
    keep = segq[...] == segk[...]
    probs = masked_probs(mixed[:, :c] * HEAD_DIM ** (-0.5), mixed[:, c : 2 * c], keep)
    out = nn(probs.astype(BF), mixed[:, 2 * c : 3 * c]).astype(BF)
    mix_ref[0] = jnp.concatenate([mixed[:, : 3 * c], out], 1)
    acc[...] += nt(out, w[:, 3 * c :])

    @pl.when(step == pl.num_programs(0) - 1)
    def _():
        part_ref[...] = acc[...].astype(BF)


def attn_forward(adds, norm, segq, segk, pieces, flag):
    tokens, width = adds[0].shape
    columns = 4 * HEAD_DIM
    steps, quarters = quarter_specs(pieces[0], columns)
    return pl.pallas_call(
        functools.partial(attn_fwd_kernel, len(adds)),
        grid=(steps,),
        in_specs=[FLAG] + [full(v) for v in adds] + [full(norm), full(segq), full(segk)] + quarters,
        out_specs=[
            spec_of((tokens, width)),
            pl.BlockSpec((1, tokens, columns), lambda i: (i, 0, 0)),
            spec_of((tokens, width)),
        ],
        out_shape=[
            jax.ShapeDtypeStruct((tokens, width), F32),
            jax.ShapeDtypeStruct((steps, tokens, columns), BF),
            jax.ShapeDtypeStruct((tokens, width), BF),
        ],
        scratch_shapes=[
            pltpu.VMEM((tokens, width), BF),
            pltpu.VMEM((width, columns), BF),
            pltpu.VMEM((tokens, width), F32),
        ],
        compiler_params=params(),
        cost_estimate=NO_COST,
        name="attn_forward",
    )(flag, *adds, norm, segq, segk, *pieces)


def ff_fwd_kernel(count, *refs):
    flag = refs[0]
    adds = refs[1 : count + 1]
    norm, *weight, x_ref, part_ref, normed, w, acc = refs[count + 1 :]
    step = pl.program_id(0)

    @pl.when(step == 0)
    def _():
        x = adds[0][...]
        for other in adds[1:]:
            x = x + other[...].astype(F32)
        x_ref[...] = x
        normed[...] = layer_norm(x, norm[...]).astype(BF)
        acc[...] = jnp.zeros_like(acc)

    load_weight(w, flag, *weight)
    columns = w.shape[1] // 2
    up = nn(normed[...], w[:, :columns])
    active = (0.5 * up * (1.0 + lax.erf(up * SQRT_HALF))).astype(BF)
    acc[...] += nt(active, w[:, columns:])

    @pl.when(step == pl.num_programs(0) - 1)
    def _():
        part_ref[...] = acc[...].astype(BF)


def ff_forward(adds, norm, pieces, flag):
    tokens, width = adds[0].shape
    columns = FF_BLOCK * 2
    steps, quarters = quarter_specs(pieces[0], columns)
    return pl.pallas_call(
        functools.partial(ff_fwd_kernel, len(adds)),
        grid=(steps,),
        in_specs=[FLAG] + [full(v) for v in adds] + [full(norm)] + quarters,
        out_specs=[spec_of((tokens, width)), spec_of((tokens, width))],
        out_shape=[
            jax.ShapeDtypeStruct((tokens, width), F32),
            jax.ShapeDtypeStruct((tokens, width), BF),
        ],
        scratch_shapes=[
            pltpu.VMEM((tokens, width), BF),
            pltpu.VMEM((width, columns), BF),
            pltpu.VMEM((tokens, width), F32),
        ],
        compiler_params=params(),
        cost_estimate=NO_COST,
        name="ff_forward",
    )(flag, *adds, norm, *pieces)


def back_prologue(back, d_ref, g_ref):
    d_base = back[0][...]
    if len(back) == 1:
        d_ref[...] = d_base
        return d_base
    value, norm, own, other = back[1:]
    d_value, g_ref[...] = norm_back(value[...], norm[...], own[...].astype(F32) + other[...].astype(F32))
    d_all = d_base + d_value
    d_ref[...] = d_all
    return d_all


def ff_back_kernel(count, *refs):
    flag = refs[0]
    back = refs[1 : count + 1]
    value, norm = refs[count + 1 : count + 3]
    weight, d_ref, grad = refs[count + 3 : count + 7], refs[count + 7], refs[count + 8 : count + 12]
    part_ref, g_ref, normed, normed_t, dz, dz_t, w, acc = refs[count + 12 :]
    step = pl.program_id(0)

    @pl.when(step == 0)
    def _():
        d_all = back_prologue(back, d_ref, g_ref)
        dz[...] = d_all.astype(BF)
        dz_t[...] = d_all.T.astype(BF)
        here = layer_norm(value[...], norm[...])
        normed[...] = here.astype(BF)
        normed_t[...] = here.T.astype(BF)
        acc[...] = jnp.zeros_like(acc)

    load_weight(w, flag, *weight)
    columns = w.shape[1] // 2
    up = nn(normed[...], w[:, :columns])
    phi = 0.5 * (1.0 + lax.erf(up * SQRT_HALF))
    active = (up * phi).astype(BF)
    slope = phi + up * jnp.exp(-0.5 * up * up) * INV_ROOT
    d_up = (nn(dz[...], w[:, columns:]) * slope).astype(BF)
    acc[...] += nt(d_up, w[:, :columns])
    store_grad([nn(normed_t[...], d_up), nn(dz_t[...], active)], flag, *grad)

    @pl.when(step == pl.num_programs(0) - 1)
    def _():
        part_ref[...] = acc[...].astype(BF)


def back_out(tokens, width, pieces, quarters):
    specs = [spec_of((tokens, width))] + quarters + [spec_of((tokens, width)), spec_of((2, width))]
    shapes = [
        jax.ShapeDtypeStruct((tokens, width), F32),
        *[jax.ShapeDtypeStruct(piece.shape, BF) for piece in pieces],
        jax.ShapeDtypeStruct((tokens, width), BF),
        jax.ShapeDtypeStruct((2, width), F32),
    ]
    return specs, shapes


def ff_backward(back, value, norm, pieces, flag):
    tokens, width = value.shape
    columns = FF_BLOCK * 2
    steps, quarters = quarter_specs(pieces[0], columns)
    specs, shapes = back_out(tokens, width, pieces, quarters)
    return pl.pallas_call(
        functools.partial(ff_back_kernel, len(back)),
        grid=(steps,),
        in_specs=[FLAG] + [full(v) for v in back] + [full(value), full(norm)] + quarters,
        out_specs=specs,
        out_shape=shapes,
        scratch_shapes=[
            pltpu.VMEM((tokens, width), BF),
            pltpu.VMEM((width, tokens), BF),
            pltpu.VMEM((tokens, width), BF),
            pltpu.VMEM((width, tokens), BF),
            pltpu.VMEM((width, columns), BF),
            pltpu.VMEM((tokens, width), F32),
        ],
        compiler_params=params(),
        cost_estimate=NO_COST,
        name="ff_backward",
    )(flag, *back, value, norm, *pieces)


def attn_back_kernel(count, *refs):
    flag = refs[0]
    back = refs[1 : count + 1]
    value, norm, segq, segk, mix_ref = refs[count + 1 : count + 6]
    weight, d_ref, grad = refs[count + 6 : count + 10], refs[count + 10], refs[count + 11 : count + 15]
    part_ref, g_ref, normed_t, dy, dy_t, w, acc = refs[count + 15 :]
    step = pl.program_id(0)

    @pl.when(step == 0)
    def _():
        d_all = back_prologue(back, d_ref, g_ref)
        dy[...] = d_all.astype(BF)
        dy_t[...] = d_all.T.astype(BF)
        normed_t[...] = layer_norm(value[...], norm[...]).T.astype(BF)
        acc[...] = jnp.zeros_like(acc)

    load_weight(w, flag, *weight)
    c = HEAD_DIM
    scale = HEAD_DIM ** (-0.5)
    query, key, val = (mix_ref[0, :, j * c : (j + 1) * c] for j in range(3))
    query = query * scale
    d_out = nn(dy[...], w[:, 3 * c :]).astype(BF)
    keep = segq[...] == segk[...]
    probs = masked_probs(query, key, keep)
    d_probs = nt(d_out, val)
    delta = jnp.sum(probs * d_probs, -1, keepdims=True)
    d_scores = jnp.where(keep, probs * (d_probs - delta), 0.0).astype(BF)
    d_query = (nn(d_scores, key) * scale).astype(BF)
    d_key = tn(d_scores, query).astype(BF)
    d_val = tn(probs.astype(BF), d_out).astype(BF)
    d_left = jnp.concatenate([d_query, d_key], 1)
    zero = jnp.zeros_like(d_val)
    d_right = jnp.concatenate([d_val, zero], 1)
    out = jnp.concatenate([zero, mix_ref[0, :, 3 * c :]], 1)
    acc[...] += nt(d_left, w[:, : 2 * c]) + nt(d_right, w[:, 2 * c :])
    left = nn(normed_t[...], d_left)
    right = nn(normed_t[...], d_right) + nn(dy_t[...], out)
    store_grad([left, right], flag, *grad)

    @pl.when(step == pl.num_programs(0) - 1)
    def _():
        part_ref[...] = acc[...].astype(BF)


def attn_backward(back, value, norm, segq, segk, mix, pieces, flag):
    tokens, width = value.shape
    columns = 4 * HEAD_DIM
    steps, quarters = quarter_specs(pieces[0], columns)
    specs, shapes = back_out(tokens, width, pieces, quarters)
    return pl.pallas_call(
        functools.partial(attn_back_kernel, len(back)),
        grid=(steps,),
        in_specs=[FLAG] + [full(v) for v in back]
        + [full(value), full(norm), full(segq), full(segk)]
        + [pl.BlockSpec((1, tokens, columns), lambda i: (i, 0, 0))]
        + quarters,
        out_specs=specs,
        out_shape=shapes,
        scratch_shapes=[
            pltpu.VMEM((width, tokens), BF),
            pltpu.VMEM((tokens, width), BF),
            pltpu.VMEM((width, tokens), BF),
            pltpu.VMEM((width, columns), BF),
            pltpu.VMEM((tokens, width), F32),
        ],
        compiler_params=params(),
        cost_estimate=NO_COST,
        name="attn_backward",
    )(flag, *back, value, norm, segq, segk, mix, *pieces)


def last_kernel(base, value, norm, own, other, d_ref, g_ref):
    d_value, g_ref[...] = norm_back(value[...], norm[...], own[...].astype(F32) + other[...].astype(F32))
    d_ref[...] = (base[...] + d_value).astype(BF)


def input_gradient(back):
    tokens, width = back[0].shape
    return pl.pallas_call(
        last_kernel,
        grid=(1,),
        in_specs=[full(v) for v in back],
        out_specs=[spec_of((tokens, width)), spec_of((2, width))],
        out_shape=[
            jax.ShapeDtypeStruct((tokens, width), BF),
            jax.ShapeDtypeStruct((2, width), F32),
        ],
        compiler_params=params(),
        cost_estimate=NO_COST,
        name="input_gradient",
    )(*back)


def finish_kernel(token, *refs):
    a_keep, a_got, f_keep, f_got, into, out, up, down, square = refs
    c = HEAD_DIM
    g = a_keep[...].astype(F32) + a_got[...].astype(F32)
    total = jnp.sum(g * g, 0, keepdims=True).sum(1, keepdims=True)
    heads = g.shape[1] // (4 * c)
    parts = [[g[:, (4 * h + j) * c : (4 * h + j + 1) * c] for h in range(heads)] for j in range(4)]
    for j in range(3):
        into[j] = jnp.concatenate(parts[j], 1)
    out[...] = jnp.concatenate(parts[3], 1).T
    g = f_keep[...].astype(F32) + f_got[...].astype(F32)
    total = total + jnp.sum(g * g, 0, keepdims=True).sum(1, keepdims=True)
    for i in range(g.shape[1] // (2 * FF_BLOCK)):
        here = slice(i * FF_BLOCK, (i + 1) * FF_BLOCK)
        up[:, here] = g[:, 2 * i * FF_BLOCK : (2 * i + 1) * FF_BLOCK]
        down[here] = g[:, (2 * i + 1) * FF_BLOCK : (2 * i + 2) * FF_BLOCK].T
    square[...] = total


def finish(a_pair, f_pair, token):
    rows, width = a_pair[0].shape
    hidden = f_pair[0].shape[1] // 2
    values = (*a_pair, *f_pair)
    outs = [(3, rows, width // 4), (width // 4, rows), (rows, hidden), (hidden, rows), (1, 1)]
    return pl.pallas_call(
        finish_kernel,
        grid=(1,),
        in_specs=[pl.BlockSpec(memory_space=pl.ANY)] + [full(v) for v in values],
        out_specs=[spec_of(o) for o in outs],
        out_shape=[jax.ShapeDtypeStruct(o, F32) for o in outs],
        compiler_params=params(),
        cost_estimate=NO_COST,
        name="finish",
    )(token, *values)


def adam(weight, grad, first, second, rate, decay):
    first = BETA_ONE * first + (1.0 - BETA_ONE) * grad
    second = BETA_TWO * second + (1.0 - BETA_TWO) * grad * grad
    update = first / (1.0 - BETA_ONE**STEP) / (jnp.sqrt(second / (1.0 - BETA_TWO**STEP)) + ADAM_EPS)
    return (first, second, weight - rate * (update + decay * weight))


def body(pixels, lengths, valid_mask, teacher_logits, teacher_map, *state):
    masters, firsts, seconds = state[:7], state[7:14], state[14:]
    attend_in, attend_out, hidden_up, hidden_down, patch_embed, class_head, norm_params = masters
    bits = dp_bits()
    low, high = bits[0], bits[1:]
    steps = Steps()
    rows = patch_embed.shape[1]
    inner = lax.axis_index("mp") % 2
    outer = lax.axis_index("mp") // 2
    images = lengths.shape[1]
    tokens = pixels.shape[0]
    total_images = images * lax.axis_size("dp")

    heads = attend_in.shape[3] // HEAD_DIM
    hidden = hidden_up.shape[2]
    width = attend_out.shape[2] * lax.axis_size("dp")

    def attn_unit(l):
        into = attend_in[l].astype(BF).reshape(3, rows, heads, HEAD_DIM)
        out = attend_out[l].T.astype(BF).reshape(1, rows, heads, HEAD_DIM)
        return jnp.concatenate([into, out], 0).transpose(1, 2, 0, 3).reshape(rows, -1)

    def ff_unit(l):
        up = hidden_up[l].astype(BF).reshape(rows, -1, 1, FF_BLOCK)
        down = hidden_down[l].T.astype(BF).reshape(rows, -1, 1, FF_BLOCK)
        return jnp.concatenate([up, down], 2).reshape(rows, -1)

    half = class_head.shape[1] // 2
    head_unit = lax.dynamic_slice_in_dim(class_head.astype(BF), inner * half, half, 1)

    flag = inner.reshape(1)

    def over(unit, bits):
        for bit in bits:
            unit = jnp.stack([unit, steps.swap(unit, bit)])
        return unit

    def over_high(unit):
        if len(high) != 2:
            return over(unit, high)
        (axis, a), (_, b) = high
        return jnp.stack([unit] + [steps.swap(unit, (axis, mask)) for mask in (a, b, a | b)])

    def near(own):
        return [own, steps.swap(own, SECOND), steps.swap(own, FIRST)]

    def across(held):
        return held + [steps.swap(held[1], FIRST)]

    def far(unit):
        unit = over_high(unit)
        return unit.reshape(-1, unit.shape[-1])

    row = lengths[0]
    ends = jnp.cumsum(row)
    longest = jnp.argmax(row)
    start = ends[longest] - row[longest]
    place = jnp.arange(MOST, dtype=jnp.int32)

    def mine(value, which):
        twice = jnp.concatenate([value, value], 0)
        return lax.dynamic_slice_in_dim(twice, start + MOST * which, MOST, 0)

    pix = [mine(pixels, outer), mine(pixels, 1 - outer)]
    held = jnp.where(outer == 0, MOST, tokens - MOST)
    position = (start + MOST * outer + place) % tokens
    segment = jnp.sum((position[:, None] >= ends[None, :]).astype(jnp.int32), 1)
    valid = jnp.where(place < held, mine(valid_mask, outer), 0) > 0
    segq = segment[:, None]
    segk = jnp.where(valid, segment, -1)[None, :]
    image_ids = jnp.arange(images, dtype=jnp.int32)
    member = ((segment[None, :] == image_ids[:, None]) & valid[None, :]).astype(F32)
    owned = ((image_ids == longest) == (outer == 0)).astype(F32)[:, None]
    count = jnp.sum(member, 1)

    mid = width // 2

    def of_inner(value, which):
        return jnp.where(which == 0, value[..., :mid], value[..., mid:])

    def halves(own, other):
        return jnp.where(inner == 0, jnp.concatenate([own, other], 1), jnp.concatenate([other, own], 1))

    dp_order = high + [low]
    teach = jax.nn.log_softmax(teacher_logits, -1)
    teach = lax.dynamic_slice_in_dim(teach, inner * half, half, 1)
    attn = [attn_unit(l) for l in range(LAYERS)]
    ff = [ff_unit(l) for l in range(LAYERS)]

    one, two = high[:1], high[1:]

    def flat(unit):
        return unit.reshape(-1, unit.shape[-1])

    for unit in attn + ff + [head_unit]:
        steps.add(unit)
    pixel_count = patch_embed.shape[0]
    patch = jnp.concatenate([patch_embed.astype(BF), norm_params.astype(BF).reshape(-1, rows)], 0).T
    patch = far(patch)
    attn[0] = over(attn[0], one)
    steps.next()
    attn[0] = flat(over(attn[0], two))
    ff[0] = over(ff[0], one)
    patch = over(patch, [low]).reshape(width, -1)
    steps.next()
    ff[0] = flat(over(ff[0], two))
    attn[1] = over(attn[1], one)
    attn[0] = near(attn[0])
    patch = steps.tie(patch)
    norms = patch[:, pixel_count:].T.astype(F32).reshape(7, 2, width)
    part = nt(jnp.concatenate(pix, 0), patch[:, :pixel_count]).astype(BF)
    part = of_inner(part, inner).astype(F32) + swap(of_inner(part, 1 - inner), INNER).astype(F32)
    part, theirs = part[:MOST], steps.add(part[MOST:].astype(BF))
    steps.next()
    part = part + steps.swap(theirs, OUTER).astype(F32)
    attn[0] = across(attn[0])
    ff[0] = near(ff[0])
    attn[1] = flat(over(attn[1], two))
    ff[1] = over(ff[1], one)
    x = steps.add(halves(part, swap(part, INNER)))
    steps.next()
    xs, middles, mixes = [], [], []

    def run_attn(l, adds):
        x, mix, own = attn_forward([steps.tie(adds[0])] + adds[1:], norms[2 * l], segq, segk, attn[l], flag)
        xs.append(x)
        mixes.append(mix)
        steps.add(own)
        return [x, own, swap(own, INNER)]

    def run_ff(l, adds):
        middle, own = ff_forward([steps.tie(adds[0])] + adds[1:], norms[2 * l + 1], ff[l], flag)
        middles.append(middle)
        steps.add(own)
        return [middle, own, swap(own, INNER)]

    ff[0] = across(ff[0])
    attn[1] = near(attn[1])
    ff[1] = flat(over(ff[1], two))
    attn[2] = over(attn[2], one)
    adds = run_attn(0, [x])
    steps.next()
    attn[1] = across(attn[1])
    ff[1] = near(ff[1])
    attn[2] = flat(over(attn[2], two))
    ff[2] = over(ff[2], one)
    adds = run_ff(0, adds)
    steps.next()
    ff[1] = across(ff[1])
    attn[2] = near(attn[2])
    ff[2] = flat(over(ff[2], two))
    adds = run_attn(1, adds)
    steps.next()
    attn[2] = across(attn[2])
    ff[2] = near(ff[2])
    head = over(head_unit, one)
    adds = run_ff(1, adds)
    steps.next()
    ff[2] = across(ff[2])
    teach = over(teach, one)
    head = over(head, two)
    adds = run_attn(2, adds)
    steps.next()
    teach = over(over(teach, two), [low])
    head = over(head, [low]).reshape(width, half)
    adds = run_ff(2, adds)
    x = sum(v.astype(F32) for v in adds)

    teach = jnp.swapaxes(teach.reshape((2, -1, images, half)), 0, 1).reshape(-1, images, half)
    me = lax.axis_index("dp")
    source = jnp.sum(jnp.where(teacher_map == me, jnp.arange(teacher_map.shape[0], dtype=jnp.int32), 0))
    teach_log = lax.dynamic_index_in_dim(teach, jnp.bitwise_xor(source, me), 0, False)

    divisor = jnp.maximum(count, 1.0)[:, None]
    pooled = jnp.dot(member, x, precision=HIGH) / divisor
    pooled_normed = layer_norm(pooled, norms[-1]).astype(BF)
    logits = nn(pooled_normed, head)
    theirs = swap(logits, INNER)
    peak = jnp.maximum(jnp.max(logits, -1, keepdims=True), jnp.max(theirs, -1, keepdims=True))
    total = jnp.sum(jnp.exp(logits - peak), -1, keepdims=True) + jnp.sum(jnp.exp(theirs - peak), -1, keepdims=True)
    student_log = logits - peak - jnp.log(total)
    loss_local = jnp.sum(owned * jnp.exp(teach_log) * (teach_log - student_log))
    d_logits = (owned * (jnp.exp(student_log) - jnp.exp(teach_log)) / total_images).astype(BF)
    g_head = tn(pooled_normed, d_logits).astype(BF)
    d_pooled, g_final = norm_back(pooled, norms[-1], both(nt(d_logits, head)))
    d_x = lax.dot_general(member, d_pooled / divisor, (((0,), (0,)), ((), ())), precision=HIGH)

    steps = Steps()
    g, g_norms = {}, {}

    def near(name):
        own, near, across, both_ways = g[name]
        near = near.astype(F32) + steps.swap(both_ways, FIRST).astype(F32)
        g[name] = own, near.astype(BF), steps.swap(across, FIRST)

    def blocks_of(value):
        value = value.astype(BF).reshape((-1, rows, value.shape[-1]))
        return [value[i] for i in range(value.shape[0])]

    def near_last(name):
        own, near, received = g[name]
        value = own.astype(F32) + received.astype(F32) + steps.swap(near, SECOND).astype(F32)
        g[name] = blocks_of(value)

    def near_low(name):
        keep, send = g[name]
        g[name] = blocks_of(keep.astype(F32) + steps.swap(send, low).astype(F32))

    def far_first(*names):
        for bit in high[:0:-1]:
            half = len(g[names[0]]) // 2
            got = steps.swap(jnp.stack([v for name in names for v in g[name][half:]]), bit)
            for k, name in enumerate(names):
                g[name] = [
                    (g[name][i].astype(F32) + got[k * half + i].astype(F32)).astype(BF) for i in range(half)
                ]

    def far_last(*names):
        got = steps.swap(jnp.stack([g[name][1] for name in names]), high[0])
        for k, name in enumerate(names):
            g[name] = (g[name][0], got[k])

    def back_ff(l, back):
        back = [steps.tie(back[0])] + back[1:]
        d_x, *grad, own, g_above = ff_backward(back, middles[l], norms[2 * l + 1], ff[l], flag)
        g["ff", l] = grad
        if l < LAYERS - 1:
            g_norms[2 * l + 2] = g_above
        steps.add(own)
        return [d_x, middles[l], norms[2 * l + 1], own, swap(own, INNER)]

    def back_attn(l, back):
        back = [steps.tie(back[0])] + back[1:]
        d_mid, *grad, own, g_above = attn_backward(
            back, xs[l], norms[2 * l], segq, segk, mixes[l], attn[l], flag
        )
        g["attn", l] = grad
        g_norms[2 * l + 1] = g_above
        steps.add(own)
        return [d_mid, xs[l], norms[2 * l], own, swap(own, INNER)]

    g["head"] = (g_head[:mid], g_head[mid:])
    near_low("head")
    back = back_ff(2, [d_x])
    steps.next()
    near(("ff", 2))
    far_first("head")
    back = back_attn(2, back)
    steps.next()
    near(("attn", 2))
    near_last(("ff", 2))
    far_last("head")
    back = back_ff(1, back)
    steps.next()
    near(("ff", 1))
    near_last(("attn", 2))
    far_first(("ff", 2))
    back = back_attn(1, back)
    steps.next()
    near(("attn", 1))
    near_last(("ff", 1))
    far_first(("attn", 2))
    far_last(("ff", 2))
    back = back_ff(0, back)
    steps.next()
    near(("ff", 0))
    near_last(("attn", 1))
    far_first(("ff", 1))
    far_last(("attn", 2))
    back = back_attn(0, back)
    steps.next()
    d_x0, g_norms[0] = input_gradient([steps.tie(back[0])] + back[1:])
    theirs = steps.swap(of_inner(d_x0, inner), OUTER)
    near(("attn", 0))
    near_last(("ff", 0))
    far_first(("attn", 1))
    far_last(("ff", 1))
    theirs = halves(theirs, swap(theirs, INNER))
    g_patch = tn(jnp.concatenate([d_x0, theirs], 0), jnp.concatenate(pix, 0)).astype(BF)
    steps.add(g_patch)
    g["patch"] = (g_patch[:mid], g_patch[mid:])
    token = g_norms[0]
    done = [None] * LAYERS
    done[2] = finish(g["attn", 2], g["ff", 2], token)
    steps.next()
    near_low("patch")
    near_last(("attn", 0))
    far_first(("ff", 0))
    far_last(("attn", 1))
    g_head = steps.tie(g["head"][0]).astype(F32) + g["head"][1].astype(F32)
    g_head = g_head + steps.swap(g_head, OUTER)
    g_norm = steps.tie(jnp.concatenate([g_norms[i] for i in range(6)] + [g_final], 0))
    g_norm = 0.5 * (g_norm + swap(g_norm, INNER))
    done[1] = finish(g["attn", 1], g["ff", 1], g_patch)
    steps.next()
    far_first(("attn", 0), "patch")
    far_last(("ff", 0))
    g_norm = g_norm + steps.swap(g_norm, OUTER)
    g_norm = jnp.moveaxis(g_norm.reshape(14, 2, -1, rows), 0, 2)
    g_norm = g_norm[0] + steps.swap(g_norm[1], low)
    g_head = halves(g_head, swap(g_head, INNER))
    steps.next()
    far_last(("attn", 0), "patch")
    g_norm = g_norm.reshape((2,) * len(high) + (14, rows))
    for bit in high[::-1]:
        g_norm = g_norm[0] + steps.swap(g_norm[1], bit)
    g_norm = g_norm.reshape(7, 2, rows)
    done[0] = finish(g["attn", 0], g["ff", 0], g_patch)
    g_patch = g["patch"][0].astype(F32) + g["patch"][1].astype(F32)

    grads = tuple(jnp.stack([layer[i] for layer in done]) for i in range(4)) + (g_patch.T, g_head, g_norm)
    first_model = (lax.axis_index("mp") == 0).astype(F32)
    squares = sum(layer[4][0, 0] for layer in done) + jnp.sum(g_patch * g_patch) + first_model * (
        jnp.sum(g_head * g_head) + jnp.sum(g_norm * g_norm)
    )
    sums = jnp.stack([squares, loss_local * (outer >= 0)])
    sums = sums + swap(sums, INNER)
    sums = sums + swap(sums, OUTER)
    if len(high) == 2:
        (axis, a), (_, b) = high
        sums = sums + swap(sums, low)
        sums = (sums + swap(sums, (axis, a))) + (swap(sums, (axis, b)) + swap(sums, (axis, a | b)))
    else:
        for bit in bits:
            sums = sums + swap(sums, bit)
    loss = sums[1]
    grad_norm = jnp.sqrt(sums[0])
    clip = jnp.minimum(1.0, CLIP / grad_norm)
    results = []
    for kind in range(7):
        results.append(
            adam(masters[kind], grads[kind] * clip, firsts[kind], seconds[kind], RATES[kind], DECAYS[kind])
        )
    return (loss, grad_norm) + tuple(r[i] for i in range(3) for r in results)


def solution(mesh):
    weights = (
        P(None, None, "dp", "mp"),
        P(None, "mp", "dp"),
        P(None, "dp", "mp"),
        P(None, "mp", "dp"),
        P("mp", "dp"),
        P("dp", None),
        P(None, None, "dp"),
    )
    placed = (P("dp", "mp"), P("dp", None), P("dp"), P("dp", None), P()) + weights * 3
    return jax.shard_map(
        body, mesh=mesh, in_specs=placed, out_specs=(P(), P()) + weights * 3, check_vma=False
    )
```

```python
import functools

import jax
import jax.numpy as jnp
from jax import lax
from jax.experimental import pallas as pl
from jax.experimental.pallas import tpu as pltpu
from jax.sharding import PartitionSpec as P

HEAD_DIM = 64
LAYERS = 3
STEP = 10
MOST = 576
FF_BLOCK = 256

EPSILON = 1e-06
MASKED = -30000.0
CLIP = 0.005
BETA_ONE = 0.9
BETA_TWO = 0.999
ADAM_EPS = 1e-08
RATES = (0.02, 0.06, 0.02, 0.02, 0.02, 0.02, 0.5)
DECAYS = (0.05, 0.05, 0.05, 0.05, 0.05, 0.05, 0.0)
SQRT_HALF = 0.7071067811865476
INV_ROOT = 0.3989422804014327
HIGH = lax.Precision.HIGHEST
BF = jnp.bfloat16
F32 = jnp.float32

AXES = ("dp", "mp")
INNER = ("mp", 1)
OUTER = ("mp", 2)
LOW = ("dp", 1)
FIRST = (LOW, OUTER)
SECOND = (OUTER, LOW)


def swap(value, bit):
    n_dp, n_mp = (lax.axis_size(axis) for axis in AXES)
    pairs = []
    for dp in range(n_dp):
        for mp in range(n_mp):
            axis, mask = bit if isinstance(bit[0], str) else bit[mp % 2]
            to = (dp ^ mask) * n_mp + mp if axis == "dp" else dp * n_mp + (mp ^ mask)
            pairs.append((dp * n_mp + mp, to))
    return lax.ppermute(value, AXES, pairs)


class Steps:
    def __init__(self):
        self.before = []
        self.made = []

    def next(self):
        self.before, self.made = self.made, []

    def tie(self, value):
        if not self.before:
            return value
        return lax.optimization_barrier((value, *self.before))[0]

    def add(self, value):
        self.made.append(value)
        return value

    def swap(self, value, bit):
        return self.add(swap(self.tie(value), bit))


def dp_bits():
    size = lax.axis_size("dp")
    bits = []
    mask = 1
    while mask < size:
        bits.append(("dp", mask))
        mask *= 2
    return bits


def both(part):
    return part + swap(part.astype(BF), INNER).astype(F32)


def dot(left, right, contract):
    return lax.dot_general(left, right, ((contract[0:1], contract[1:2]), ((), ())), preferred_element_type=F32)


def nn(left, right):
    return dot(left, right, (1, 0))


def nt(left, right):
    return dot(left, right, (1, 1))


def tn(left, right):
    return dot(left, right, (0, 0))


def norm_stats(value):
    centred = value - jnp.mean(value, -1, keepdims=True)
    variance = jnp.mean(centred * centred, -1, keepdims=True)
    rstd = lax.rsqrt(variance + EPSILON)
    return centred * rstd, rstd


def layer_norm(value, norm):
    return norm_stats(value)[0] * norm[0:1] + norm[1:2]


def norm_back(value, norm, d_out):
    hat, rstd = norm_stats(value)
    d_hat = d_out * norm[0:1]
    d_value = rstd * (
        d_hat - jnp.mean(d_hat, -1, keepdims=True) - hat * jnp.mean(d_hat * hat, -1, keepdims=True)
    )
    return d_value, jnp.concatenate([jnp.sum(d_out * hat, 0, keepdims=True), jnp.sum(d_out, 0, keepdims=True)], 0)


def load_weight(w, flag, own, near, across, both_ways):
    outer = pl.program_id(0) % 2
    rows = w.shape[0] // 2

    @pl.when(outer == 0)
    def _():
        w[:rows] = own[...]

    @pl.when(outer == 1)
    def _():
        w[rows:] = both_ways[...]

    @pl.when((outer == 0) & (flag[0] == 0))
    def _():
        w[rows:] = across[...]

    @pl.when((outer == 0) & (flag[0] == 1))
    def _():
        w[rows:] = near[...]

    @pl.when((outer == 1) & (flag[0] == 0))
    def _():
        w[:rows] = near[...]

    @pl.when((outer == 1) & (flag[0] == 1))
    def _():
        w[:rows] = across[...]


def store_grad(parts, flag, own, near, across, both_ways):
    outer = pl.program_id(0) % 2

    def put(target, top):
        at = 0
        for part in parts:
            rows = part.shape[0] // 2
            value = part[:rows] if top else part[rows:]
            target[:, at : at + part.shape[1]] = value.astype(BF)
            at += part.shape[1]

    @pl.when(outer == 0)
    def _():
        put(own, True)

    @pl.when(outer == 1)
    def _():
        put(both_ways, False)

    @pl.when((outer == 0) & (flag[0] == 0))
    def _():
        put(across, False)

    @pl.when((outer == 0) & (flag[0] == 1))
    def _():
        put(near, False)

    @pl.when((outer == 1) & (flag[0] == 0))
    def _():
        put(near, True)

    @pl.when((outer == 1) & (flag[0] == 1))
    def _():
        put(across, True)


def quarter_specs(weight, columns):
    steps = 2 * (weight.shape[1] // columns)
    return steps, [pl.BlockSpec((weight.shape[0], columns), lambda i: (0, i // 2))] * 4


def full(value):
    return pl.BlockSpec(value.shape, lambda i: (0,) * len(value.shape))


def spec_of(shape):
    return pl.BlockSpec(shape, lambda i: (0,) * len(shape))


FLAG = pl.BlockSpec(memory_space=pltpu.SMEM)
NO_COST = pl.CostEstimate(flops=10**6, bytes_accessed=10**4, transcendentals=0)


def params():
    return pltpu.CompilerParams(dimension_semantics=("arbitrary",), vmem_limit_bytes=56 * 1024 * 1024)


def masked_probs(scaled_query, key, keep):
    scores = jnp.where(keep, nt(scaled_query, key), MASKED)
    weight = jnp.exp(scores - jnp.max(scores, -1, keepdims=True))
    return weight * (1.0 / jnp.sum(weight, -1, keepdims=True))


def attn_fwd_kernel(count, *refs):
    flag = refs[0]
    adds = refs[1 : count + 1]
    norm, segq, segk, *weight, x_ref, mix_ref, part_ref, normed, w, acc = refs[count + 1 :]
    step = pl.program_id(0)

    @pl.when(step == 0)
    def _():
        x = adds[0][...]
        for other in adds[1:]:
            x = x + other[...].astype(F32)
        x_ref[...] = x
        normed[...] = layer_norm(x, norm[...]).astype(BF)
        acc[...] = jnp.zeros_like(acc)

    load_weight(w, flag, *weight)
    mixed = nn(normed[...], w[...]).astype(BF)
    c = HEAD_DIM
    width = w.shape[1] // 4
    keep = segq[...] == segk[...]
    outs = []
    for at in range(0, width, c):
        probs = masked_probs(mixed[:, at : at + c] * c ** (-0.5), mixed[:, width + at : width + at + c], keep)
        outs.append(nn(probs.astype(BF), mixed[:, 2 * width + at : 2 * width + at + c]).astype(BF))
    out = jnp.concatenate(outs, 1)
    mix_ref[0] = jnp.concatenate([mixed[:, : 3 * width], out], 1)
    acc[...] += nt(jnp.concatenate([jnp.zeros_like(outs[0]), out], 1), w[:, 3 * width - c :])

    @pl.when(step == pl.num_programs(0) - 1)
    def _():
        part_ref[...] = acc[...].astype(BF)


def attn_forward(adds, norm, segq, segk, pieces, flag):
    tokens, width = adds[0].shape
    columns = pieces[0].shape[1]
    steps, quarters = quarter_specs(pieces[0], columns)
    return pl.pallas_call(
        functools.partial(attn_fwd_kernel, len(adds)),
        grid=(steps,),
        in_specs=[FLAG] + [full(v) for v in adds] + [full(norm), full(segq), full(segk)] + quarters,
        out_specs=[
            spec_of((tokens, width)),
            pl.BlockSpec((1, tokens, columns), lambda i: (i, 0, 0)),
            spec_of((tokens, width)),
        ],
        out_shape=[
            jax.ShapeDtypeStruct((tokens, width), F32),
            jax.ShapeDtypeStruct((steps, tokens, columns), BF),
            jax.ShapeDtypeStruct((tokens, width), BF),
        ],
        scratch_shapes=[
            pltpu.VMEM((tokens, width), BF),
            pltpu.VMEM((width, columns), BF),
            pltpu.VMEM((tokens, width), F32),
        ],
        compiler_params=params(),
        cost_estimate=NO_COST,
        name="attn_forward",
    )(flag, *adds, norm, segq, segk, *pieces)


def ff_fwd_kernel(count, *refs):
    flag = refs[0]
    adds = refs[1 : count + 1]
    norm, *weight, x_ref, part_ref, normed, w, acc = refs[count + 1 :]
    step = pl.program_id(0)

    @pl.when(step == 0)
    def _():
        x = adds[0][...]
        for other in adds[1:]:
            x = x + other[...].astype(F32)
        x_ref[...] = x
        normed[...] = layer_norm(x, norm[...]).astype(BF)
        acc[...] = jnp.zeros_like(acc)

    load_weight(w, flag, *weight)
    columns = w.shape[1] // 2
    up = nn(normed[...], w[:, :columns])
    active = (0.5 * up * (1.0 + lax.erf(up * SQRT_HALF))).astype(BF)
    acc[...] += nt(active, w[:, columns:])

    @pl.when(step == pl.num_programs(0) - 1)
    def _():
        part_ref[...] = acc[...].astype(BF)


def ff_forward(adds, norm, pieces, flag):
    tokens, width = adds[0].shape
    columns = FF_BLOCK * 2
    steps, quarters = quarter_specs(pieces[0], columns)
    return pl.pallas_call(
        functools.partial(ff_fwd_kernel, len(adds)),
        grid=(steps,),
        in_specs=[FLAG] + [full(v) for v in adds] + [full(norm)] + quarters,
        out_specs=[spec_of((tokens, width)), spec_of((tokens, width))],
        out_shape=[
            jax.ShapeDtypeStruct((tokens, width), F32),
            jax.ShapeDtypeStruct((tokens, width), BF),
        ],
        scratch_shapes=[
            pltpu.VMEM((tokens, width), BF),
            pltpu.VMEM((width, columns), BF),
            pltpu.VMEM((tokens, width), F32),
        ],
        compiler_params=params(),
        cost_estimate=NO_COST,
        name="ff_forward",
    )(flag, *adds, norm, *pieces)


def back_prologue(back, d_ref, g_ref):
    d_base = back[0][...]
    if len(back) == 1:
        d_ref[...] = d_base
        return d_base
    value, norm, own, other = back[1:]
    d_value, g_ref[...] = norm_back(value[...], norm[...], own[...].astype(F32) + other[...].astype(F32))
    d_all = d_base + d_value
    d_ref[...] = d_all
    return d_all


def ff_back_kernel(count, *refs):
    flag = refs[0]
    back = refs[1 : count + 1]
    value, norm = refs[count + 1 : count + 3]
    weight, d_ref, grad = refs[count + 3 : count + 7], refs[count + 7], refs[count + 8 : count + 12]
    part_ref, g_ref, normed, normed_t, dz, dz_t, w, acc = refs[count + 12 :]
    step = pl.program_id(0)

    @pl.when(step == 0)
    def _():
        d_all = back_prologue(back, d_ref, g_ref)
        dz[...] = d_all.astype(BF)
        dz_t[...] = d_all.T.astype(BF)
        here = layer_norm(value[...], norm[...])
        normed[...] = here.astype(BF)
        normed_t[...] = here.T.astype(BF)
        acc[...] = jnp.zeros_like(acc)

    load_weight(w, flag, *weight)
    columns = w.shape[1] // 2
    up = nn(normed[...], w[:, :columns])
    phi = 0.5 * (1.0 + lax.erf(up * SQRT_HALF))
    active = (up * phi).astype(BF)
    slope = phi + up * jnp.exp(-0.5 * up * up) * INV_ROOT
    d_up = (nn(dz[...], w[:, columns:]) * slope).astype(BF)
    acc[...] += nt(d_up, w[:, :columns])
    store_grad([nn(normed_t[...], d_up), nn(dz_t[...], active)], flag, *grad)

    @pl.when(step == pl.num_programs(0) - 1)
    def _():
        part_ref[...] = acc[...].astype(BF)


def back_out(tokens, width, pieces, quarters):
    specs = [spec_of((tokens, width))] + quarters + [spec_of((tokens, width)), spec_of((2, width))]
    shapes = [
        jax.ShapeDtypeStruct((tokens, width), F32),
        *[jax.ShapeDtypeStruct(piece.shape, BF) for piece in pieces],
        jax.ShapeDtypeStruct((tokens, width), BF),
        jax.ShapeDtypeStruct((2, width), F32),
    ]
    return specs, shapes


def ff_backward(back, value, norm, pieces, flag):
    tokens, width = value.shape
    columns = FF_BLOCK * 2
    steps, quarters = quarter_specs(pieces[0], columns)
    specs, shapes = back_out(tokens, width, pieces, quarters)
    return pl.pallas_call(
        functools.partial(ff_back_kernel, len(back)),
        grid=(steps,),
        in_specs=[FLAG] + [full(v) for v in back] + [full(value), full(norm)] + quarters,
        out_specs=specs,
        out_shape=shapes,
        scratch_shapes=[
            pltpu.VMEM((tokens, width), BF),
            pltpu.VMEM((width, tokens), BF),
            pltpu.VMEM((tokens, width), BF),
            pltpu.VMEM((width, tokens), BF),
            pltpu.VMEM((width, columns), BF),
            pltpu.VMEM((tokens, width), F32),
        ],
        compiler_params=params(),
        cost_estimate=NO_COST,
        name="ff_backward",
    )(flag, *back, value, norm, *pieces)


def attn_back_kernel(count, *refs):
    flag = refs[0]
    back = refs[1 : count + 1]
    value, norm, segq, segk, mix_ref = refs[count + 1 : count + 6]
    weight, d_ref, grad = refs[count + 6 : count + 10], refs[count + 10], refs[count + 11 : count + 15]
    part_ref, g_ref, normed_t, dy, dy_t, w, acc, d_mix = refs[count + 15 :]
    step = pl.program_id(0)

    @pl.when(step == 0)
    def _():
        d_all = back_prologue(back, d_ref, g_ref)
        dy[...] = d_all.astype(BF)
        dy_t[...] = d_all.T.astype(BF)
        normed_t[...] = layer_norm(value[...], norm[...]).T.astype(BF)
        d_mix[...] = jnp.zeros_like(d_mix)
        acc[...] = jnp.zeros_like(acc)

    load_weight(w, flag, *weight)
    c = HEAD_DIM
    scale = HEAD_DIM ** (-0.5)
    width = w.shape[1] // 4
    tokens = dy.shape[0]
    d_outs = nn(dy[...], w[:, 3 * width - c :])[:, c:].astype(BF)
    keep = segq[...] == segk[...]
    for at in range(0, width, c):
        query = mix_ref[0, :, at : at + c] * scale
        key = mix_ref[0, :, width + at : width + at + c]
        val = mix_ref[0, :, 2 * width + at : 2 * width + at + c]
        d_out = d_outs[:, at : at + c]
        probs = masked_probs(query, key, keep)
        d_probs = nt(d_out, val)
        delta = jnp.sum(probs * d_probs, -1, keepdims=True)
        d_scores = jnp.where(keep, probs * (d_probs - delta), 0.0).astype(BF)
        d_mix[:, at : at + c] = (nn(d_scores, key) * scale).astype(BF)
        d_mix[:, width + at : width + at + c] = nn(query.T, d_scores).T.astype(BF)
        d_mix[:, 2 * width + at : 2 * width + at + c] = nn(d_out.T, probs.astype(BF)).T.astype(BF)
    acc[...] += nt(d_mix[...], w[...])
    wide = 4 * width - (3 * width - c)
    out = jnp.concatenate([jnp.zeros((tokens, c), BF), mix_ref[0, :, 3 * width :]], 1)
    left = nn(normed_t[...], d_mix[:, : 4 * width - wide])
    right = nn(normed_t[...], d_mix[:, 4 * width - wide :]) + nn(dy_t[...], out)
    store_grad([left, right], flag, *grad)

    @pl.when(step == pl.num_programs(0) - 1)
    def _():
        part_ref[...] = acc[...].astype(BF)


def attn_backward(back, value, norm, segq, segk, mix, pieces, flag):
    tokens, width = value.shape
    columns = pieces[0].shape[1]
    steps, quarters = quarter_specs(pieces[0], columns)
    specs, shapes = back_out(tokens, width, pieces, quarters)
    return pl.pallas_call(
        functools.partial(attn_back_kernel, len(back)),
        grid=(steps,),
        in_specs=[FLAG] + [full(v) for v in back]
        + [full(value), full(norm), full(segq), full(segk)]
        + [pl.BlockSpec((1, tokens, columns), lambda i: (i, 0, 0))]
        + quarters,
        out_specs=specs,
        out_shape=shapes,
        scratch_shapes=[
            pltpu.VMEM((width, tokens), BF),
            pltpu.VMEM((tokens, width), BF),
            pltpu.VMEM((width, tokens), BF),
            pltpu.VMEM((width, columns), BF),
            pltpu.VMEM((tokens, width), F32),
            pltpu.VMEM((tokens, columns), BF),
        ],
        compiler_params=params(),
        cost_estimate=NO_COST,
        name="attn_backward",
    )(flag, *back, value, norm, segq, segk, mix, *pieces)


def last_kernel(base, value, norm, own, other, d_ref, g_ref):
    d_value, g_ref[...] = norm_back(value[...], norm[...], own[...].astype(F32) + other[...].astype(F32))
    d_ref[...] = (base[...] + d_value).astype(BF)


def input_gradient(back):
    tokens, width = back[0].shape
    return pl.pallas_call(
        last_kernel,
        grid=(1,),
        in_specs=[full(v) for v in back],
        out_specs=[spec_of((tokens, width)), spec_of((2, width))],
        out_shape=[
            jax.ShapeDtypeStruct((tokens, width), BF),
            jax.ShapeDtypeStruct((2, width), F32),
        ],
        compiler_params=params(),
        cost_estimate=NO_COST,
        name="input_gradient",
    )(*back)


def finish_kernel(count, *refs):
    a_keep, a_got, f_keep, f_got, into, out, up, down, square = refs[1 + count :]
    g = a_keep[...].astype(F32) + a_got[...].astype(F32)
    total = jnp.sum(g * g, 0, keepdims=True).sum(1, keepdims=True)
    width = g.shape[1] // 4
    for j in range(3):
        into[j] = g[:, j * width : (j + 1) * width]
    out[...] = g[:, 3 * width :].T
    g = f_keep[...].astype(F32) + f_got[...].astype(F32)
    total = total + jnp.sum(g * g, 0, keepdims=True).sum(1, keepdims=True)
    for i in range(g.shape[1] // (2 * FF_BLOCK)):
        here = slice(i * FF_BLOCK, (i + 1) * FF_BLOCK)
        up[:, here] = g[:, 2 * i * FF_BLOCK : (2 * i + 1) * FF_BLOCK]
        down[:, here] = g[:, (2 * i + 1) * FF_BLOCK : (2 * i + 2) * FF_BLOCK]
    square[...] = total


def finish(l, before, a_pair, f_pair, token):
    rows, width = a_pair[0].shape
    hidden = f_pair[0].shape[1] // 2
    values = (*a_pair, *f_pair)
    outs = [(3, rows, width // 4), (width // 4, rows), (rows, hidden), (rows, hidden)]

    def layer_spec(o):
        return pl.BlockSpec((None, *o), lambda i: (l,) + (0,) * len(o))

    anywhere = pl.BlockSpec(memory_space=pl.ANY)
    return pl.pallas_call(
        functools.partial(finish_kernel, len(before)),
        grid=(1,),
        in_specs=[anywhere] * (1 + len(before)) + [full(v) for v in values],
        out_specs=[layer_spec(o) for o in outs] + [spec_of((1, 1))],
        out_shape=[jax.ShapeDtypeStruct((LAYERS, *o), F32) for o in outs] + [jax.ShapeDtypeStruct((1, 1), F32)],
        input_output_aliases={1 + i: i for i in range(len(before))},
        compiler_params=params(),
        cost_estimate=NO_COST,
        name="finish",
    )(token, *before, *values)


def adam_kernel(clip_ref, *refs):
    clip = clip_ref[0]
    for kind in range(7):
        weight, grad, first, second = (refs[i * 7 + kind] for i in range(4))
        new_first, new_second, new_weight = (refs[28 + i * 7 + kind] for i in range(3))

        def update():
            g = grad[...] * clip
            new_first[...], new_second[...], new_weight[...] = adam(
                weight[...], g, first[...], second[...], RATES[kind], DECAYS[kind]
            )

        if kind < 4:
            update()
        else:
            pl.when(pl.program_id(0) == 0)(update)


def adam_all(clip, masters, grads, firsts, seconds):
    def spec(value, kind):
        if kind < 4:
            rest = value.shape[1:]
            return pl.BlockSpec((None, *rest), lambda i: (i,) + (0,) * len(rest))
        return full(value)

    specs = [spec(value, kind) for kind, value in enumerate(masters)]
    outs = pl.pallas_call(
        adam_kernel,
        grid=(LAYERS,),
        in_specs=[FLAG] + specs * 4,
        out_specs=specs * 3,
        out_shape=[jax.ShapeDtypeStruct(v.shape, F32) for v in masters] * 3,
        compiler_params=params(),
        name="adam",
    )(clip.reshape(1), *masters, *grads, *firsts, *seconds)
    return tuple(outs)


def adam(weight, grad, first, second, rate, decay):
    first = BETA_ONE * first + (1.0 - BETA_ONE) * grad
    second = BETA_TWO * second + (1.0 - BETA_TWO) * grad * grad
    update = first / (1.0 - BETA_ONE**STEP) / (jnp.sqrt(second / (1.0 - BETA_TWO**STEP)) + ADAM_EPS)
    return (first, second, weight - rate * (update + decay * weight))


def body(pixels, lengths, valid_mask, teacher_logits, teacher_map, *state):
    masters, firsts, seconds = state[:7], state[7:14], state[14:]
    attend_in, attend_out, hidden_up, hidden_down, patch_embed, class_head, norm_params = masters
    bits = dp_bits()
    low, high = bits[0], bits[1:]
    steps = Steps()
    rows = patch_embed.shape[1]
    inner = lax.axis_index("mp") % 2
    outer = lax.axis_index("mp") // 2
    images = lengths.shape[1]
    tokens = pixels.shape[0]
    total_images = images * lax.axis_size("dp")

    hidden = hidden_up.shape[2]
    width = attend_out.shape[2] * lax.axis_size("dp")

    def attn_unit(l):
        return jnp.concatenate([attend_in[l, j].astype(BF) for j in range(3)] + [attend_out[l].astype(BF).T], 1)

    def ff_unit(l):
        up = hidden_up[l].astype(BF).reshape(rows, -1, 1, FF_BLOCK)
        down = hidden_down[l].T.astype(BF).reshape(rows, -1, 1, FF_BLOCK)
        return jnp.concatenate([up, down], 2).reshape(rows, -1)

    half = class_head.shape[1] // 2
    head_unit = lax.dynamic_slice_in_dim(class_head.astype(BF), inner * half, half, 1)
    teach = jax.nn.log_softmax(teacher_logits, -1)
    teach = lax.dynamic_slice_in_dim(teach, inner * half, half, 1)
    upper = lax.optimization_barrier(teach.astype(BF))
    head_unit = jnp.concatenate([head_unit, upper, (teach - upper.astype(F32)).astype(BF)], 0)

    flag = inner.reshape(1)

    def over(unit, bits):
        for bit in bits:
            unit = jnp.stack([unit, steps.swap(unit, bit)])
        return unit

    def over_high(unit):
        if len(high) != 2:
            return over(unit, high)
        (axis, a), (_, b) = high
        return jnp.stack([unit] + [steps.swap(unit, (axis, mask)) for mask in (a, b, a | b)])

    def near(own):
        return [own, steps.swap(own, SECOND), steps.swap(own, FIRST)]

    def across(held):
        return held + [steps.swap(held[1], FIRST)]

    def far(unit):
        unit = over_high(unit)
        return unit.reshape(-1, unit.shape[-1])

    row = lengths[0]
    ends = jnp.cumsum(row)
    longest = jnp.argmax(row)
    start = ends[longest] - row[longest]
    place = jnp.arange(MOST, dtype=jnp.int32)

    def mine(value, which):
        twice = jnp.concatenate([value, value], 0)
        return lax.dynamic_slice_in_dim(twice, start + MOST * which, MOST, 0)

    pix = [mine(pixels, outer), mine(pixels, 1 - outer)]
    held = jnp.where(outer == 0, MOST, tokens - MOST)
    position = (start + MOST * outer + place) % tokens
    segment = jnp.sum((position[:, None] >= ends[None, :]).astype(jnp.int32), 1)
    valid = jnp.where(place < held, mine(valid_mask, outer), 0) > 0
    segq = segment[:, None]
    segk = jnp.where(valid, segment, -1)[None, :]
    image_ids = jnp.arange(images, dtype=jnp.int32)
    member = ((segment[None, :] == image_ids[:, None]) & valid[None, :]).astype(F32)
    owned = ((image_ids == longest) == (outer == 0)).astype(F32)[:, None]
    count = jnp.sum(member, 1)

    mid = width // 2

    def of_inner(value, which):
        return jnp.where(which == 0, value[..., :mid], value[..., mid:])

    def halves(own, other):
        return jnp.where(inner == 0, jnp.concatenate([own, other], 1), jnp.concatenate([other, own], 1))

    dp_order = high + [low]
    attn = [attn_unit(l) for l in range(LAYERS)]
    ff = [ff_unit(l) for l in range(LAYERS)]

    one, two = high[:1], high[1:]

    def flat(unit):
        return unit.reshape(-1, unit.shape[-1])

    for unit in attn + ff + [head_unit]:
        steps.add(unit)
    pixel_count = patch_embed.shape[0]
    patch = jnp.concatenate([patch_embed.astype(BF), norm_params.astype(BF).reshape(-1, rows)], 0).T
    patch = far(patch)
    attn[0] = over(attn[0], one)
    steps.next()
    attn[0] = flat(over(attn[0], two))
    ff[0] = over(ff[0], one)
    patch = over(patch, [low]).reshape(width, -1)
    steps.next()
    ff[0] = flat(over(ff[0], two))
    attn[1] = over(attn[1], one)
    attn[0] = near(attn[0])
    patch = steps.tie(patch)
    norms = patch[:, pixel_count:].T.astype(F32).reshape(7, 2, width)
    part = nt(jnp.concatenate(pix, 0), patch[:, :pixel_count]).astype(BF)
    part = of_inner(part, inner).astype(F32) + swap(of_inner(part, 1 - inner), INNER).astype(F32)
    part, theirs = part[:MOST], steps.swap(part[MOST:].astype(BF), OUTER)
    steps.next()
    part = steps.tie(part) + theirs.astype(F32)
    attn[0] = across(attn[0])
    ff[0] = near(ff[0])
    attn[1] = flat(over(attn[1], two))
    ff[1] = over(ff[1], one)
    x = steps.add(halves(part, swap(part, INNER)))
    steps.next()
    xs, middles, mixes = [], [], []

    def run_attn(l, adds):
        x, mix, own = attn_forward([steps.tie(adds[0])] + adds[1:], norms[2 * l], segq, segk, attn[l], flag)
        xs.append(x)
        mixes.append(mix)
        steps.add(own)
        return [x, own, swap(own, INNER)]

    def run_ff(l, adds):
        middle, own = ff_forward([steps.tie(adds[0])] + adds[1:], norms[2 * l + 1], ff[l], flag)
        middles.append(middle)
        steps.add(own)
        return [middle, own, swap(own, INNER)]

    ff[0] = across(ff[0])
    attn[1] = near(attn[1])
    ff[1] = flat(over(ff[1], two))
    attn[2] = over(attn[2], one)
    adds = run_attn(0, [x])
    steps.next()
    attn[1] = across(attn[1])
    ff[1] = near(ff[1])
    attn[2] = flat(over(attn[2], two))
    ff[2] = over(ff[2], one)
    adds = run_ff(0, adds)
    steps.next()
    ff[1] = across(ff[1])
    attn[2] = near(attn[2])
    ff[2] = flat(over(ff[2], two))
    head = over(head_unit, one)
    adds = run_attn(1, adds)
    steps.next()
    attn[2] = across(attn[2])
    ff[2] = near(ff[2])
    head = over(head, two)
    adds = run_ff(1, adds)
    steps.next()
    ff[2] = across(ff[2])
    head = over(head, [low]).reshape(-1, rows + 2 * images, half)
    adds = run_attn(2, adds)
    steps.next()
    teach = head[:, rows : rows + images].astype(F32) + head[:, rows + images :].astype(F32)
    head = head[:, :rows].reshape(width, half)
    adds = run_ff(2, adds)
    x = sum(v.astype(F32) for v in adds)

    teach = jnp.swapaxes(teach.reshape((2, -1, images, half)), 0, 1).reshape(-1, images, half)
    me = lax.axis_index("dp")
    source = jnp.sum(jnp.where(teacher_map == me, jnp.arange(teacher_map.shape[0], dtype=jnp.int32), 0))
    teach_log = lax.dynamic_index_in_dim(teach, jnp.bitwise_xor(source, me), 0, False)

    divisor = jnp.maximum(count, 1.0)[:, None]
    pooled = jnp.dot(member, x, precision=HIGH) / divisor
    pooled_normed = layer_norm(pooled, norms[-1]).astype(BF)
    logits = nn(pooled_normed, head)
    theirs = swap(logits, INNER)
    peak = jnp.maximum(jnp.max(logits, -1, keepdims=True), jnp.max(theirs, -1, keepdims=True))
    total = jnp.sum(jnp.exp(logits - peak), -1, keepdims=True) + jnp.sum(jnp.exp(theirs - peak), -1, keepdims=True)
    student_log = logits - peak - jnp.log(total)
    loss_local = jnp.sum(owned * jnp.exp(teach_log) * (teach_log - student_log))
    d_logits = (owned * (jnp.exp(student_log) - jnp.exp(teach_log)) / total_images).astype(BF)
    g_head = tn(pooled_normed, d_logits).astype(BF)
    d_pooled, g_final = norm_back(pooled, norms[-1], both(nt(d_logits, head)))
    d_x = lax.dot_general(member, d_pooled / divisor, (((0,), (0,)), ((), ())), precision=HIGH)

    steps = Steps()
    g, g_norms = {}, {}

    def near(name):
        own, near, across, both_ways = g[name]
        near = near.astype(F32) + steps.swap(both_ways, FIRST).astype(F32)
        g[name] = own, near.astype(BF), steps.swap(across, FIRST)

    def blocks_of(value):
        value = value.astype(BF).reshape((-1, rows, value.shape[-1]))
        return [value[i] for i in range(value.shape[0])]

    def near_last(name):
        own, near, received = g[name]
        value = own.astype(F32) + received.astype(F32) + steps.swap(near, SECOND).astype(F32)
        g[name] = blocks_of(value)

    def near_low(name):
        keep, send = g[name]
        g[name] = blocks_of(keep.astype(F32) + steps.swap(send, low).astype(F32))

    def far_first(*names):
        for bit in high[:0:-1]:
            half = len(g[names[0]]) // 2
            got = steps.swap(jnp.stack([v for name in names for v in g[name][half:]]), bit)
            for k, name in enumerate(names):
                g[name] = [
                    (g[name][i].astype(F32) + got[k * half + i].astype(F32)).astype(BF) for i in range(half)
                ]

    def far_last(*names):
        got = steps.swap(jnp.stack([g[name][1] for name in names]), high[0])
        for k, name in enumerate(names):
            g[name] = (g[name][0], got[k])

    def back_ff(l, back):
        back = [steps.tie(back[0])] + back[1:]
        d_x, *grad, own, g_above = ff_backward(back, middles[l], norms[2 * l + 1], ff[l], flag)
        g["ff", l] = grad
        if l < LAYERS - 1:
            g_norms[2 * l + 2] = g_above
        steps.add(own)
        return [d_x, middles[l], norms[2 * l + 1], own, swap(own, INNER)]

    def back_attn(l, back):
        back = [steps.tie(back[0])] + back[1:]
        d_mid, *grad, own, g_above = attn_backward(
            back, xs[l], norms[2 * l], segq, segk, mixes[l], attn[l], flag
        )
        g["attn", l] = grad
        g_norms[2 * l + 1] = g_above
        steps.add(own)
        return [d_mid, xs[l], norms[2 * l], own, swap(own, INNER)]

    g["head"] = (g_head[:mid], g_head[mid:])
    near_low("head")
    back = back_ff(2, [d_x])
    steps.next()
    near(("ff", 2))
    far_first("head")
    back = back_attn(2, back)
    steps.next()
    near(("attn", 2))
    near_last(("ff", 2))
    far_last("head")
    back = back_ff(1, back)
    steps.next()
    near(("ff", 1))
    near_last(("attn", 2))
    far_first(("ff", 2))
    back = back_attn(1, back)
    steps.next()
    near(("attn", 1))
    near_last(("ff", 1))
    far_first(("attn", 2))
    far_last(("ff", 2))
    back = back_ff(0, back)
    steps.next()
    near(("ff", 0))
    near_last(("attn", 1))
    far_first(("ff", 1))
    far_last(("attn", 2))
    back = back_attn(0, back)
    steps.next()
    d_x0, g_norms[0] = input_gradient([steps.tie(back[0])] + back[1:])
    theirs = steps.swap(of_inner(d_x0, inner), OUTER)
    near(("attn", 0))
    near_last(("ff", 0))
    far_first(("attn", 1))
    far_last(("ff", 1))
    theirs = halves(theirs, swap(theirs, INNER))
    g_patch = tn(jnp.concatenate([d_x0, theirs], 0), jnp.concatenate(pix, 0)).astype(BF)
    steps.add(g_patch)
    g["patch"] = (g_patch[:mid], g_patch[mid:])
    token = g_norms[0]
    *done, square_two = finish(2, [], g["attn", 2], g["ff", 2], token)
    steps.next()
    near_low("patch")
    near_last(("attn", 0))
    far_first(("ff", 0))
    far_last(("attn", 1))
    g_head = steps.tie(g["head"][0]).astype(F32) + g["head"][1].astype(F32)
    g_head = g_head + steps.swap(g_head, OUTER)
    g_norm = steps.tie(jnp.concatenate([g_norms[i] for i in range(6)] + [g_final], 0))
    g_norm = 0.5 * (g_norm + swap(g_norm, INNER))
    *done, square_one = finish(1, done, g["attn", 1], g["ff", 1], g_patch)
    steps.next()
    far_first(("attn", 0), "patch")
    far_last(("ff", 0))
    g_norm = g_norm + steps.swap(g_norm, OUTER)
    g_norm = jnp.moveaxis(g_norm.reshape(14, 2, -1, rows), 0, 2)
    g_norm = g_norm[0] + steps.swap(g_norm[1], low)
    g_head = halves(g_head, swap(g_head, INNER))
    steps.next()
    far_last(("attn", 0), "patch")
    g_norm = g_norm.reshape((2,) * len(high) + (14, rows))
    for bit in high[::-1]:
        g_norm = g_norm[0] + steps.swap(g_norm[1], bit)
    g_norm = g_norm.reshape(7, 2, rows)
    *done, square_zero = finish(0, done, g["attn", 0], g["ff", 0], g_patch)
    g_patch = g["patch"][0].astype(F32) + g["patch"][1].astype(F32)

    grads = (*done, g_patch, g_head, g_norm)
    first_model = (lax.axis_index("mp") == 0).astype(F32)
    squares = (square_two + square_one + square_zero)[0, 0] + jnp.sum(g_patch * g_patch) + first_model * (
        jnp.sum(g_head * g_head) + jnp.sum(g_norm * g_norm)
    )
    sums = jnp.stack([squares, loss_local * (outer >= 0)])
    sums = sums + swap(sums, INNER)
    sums = sums + swap(sums, OUTER)
    if len(high) == 2:
        (axis, a), (_, b) = high
        sums = sums + swap(sums, low)
        sums = (sums + swap(sums, (axis, a))) + (swap(sums, (axis, b)) + swap(sums, (axis, a | b)))
    else:
        for bit in bits:
            sums = sums + swap(sums, bit)
    loss = sums[1]
    grad_norm = jnp.sqrt(sums[0])
    clip = jnp.minimum(1.0, CLIP / grad_norm)

    def turned(values):
        return (*values[:3], values[3].swapaxes(1, 2), values[4].T, *values[5:])

    masters, firsts, seconds = turned(masters), turned(firsts), turned(seconds)
    outs = adam_all(clip, masters, grads, firsts, seconds)
    return (loss, grad_norm) + turned(outs[:7]) + turned(outs[7:14]) + turned(outs[14:])


def solution(mesh):
    weights = (
        P(None, None, "dp", "mp"),
        P(None, "mp", "dp"),
        P(None, "dp", "mp"),
        P(None, "mp", "dp"),
        P("mp", "dp"),
        P("dp", None),
        P(None, None, "dp"),
    )
    placed = (P("dp", "mp"), P("dp", None), P("dp"), P("dp", None), P()) + weights * 3
    return jax.shard_map(
        body, mesh=mesh, in_specs=placed, out_specs=(P(), P()) + weights * 3, check_vma=False
    )
```

```python
import functools

import jax
import jax.numpy as jnp
from jax import lax
from jax.experimental import pallas as pl
from jax.experimental.pallas import tpu as pltpu
from jax.sharding import PartitionSpec as P

HEAD_DIM = 64
LAYERS = 3
STEP = 10
MOST = 576
EXTRA = 16
NEVER = -1e30
FF_BLOCK = 256

EPSILON = 1e-06
MASKED = -30000.0
CLIP = 0.005
BETA_ONE = 0.9
BETA_TWO = 0.999
ADAM_EPS = 1e-08
RATES = (0.02, 0.06, 0.02, 0.02, 0.02, 0.02, 0.5)
DECAYS = (0.05, 0.05, 0.05, 0.05, 0.05, 0.05, 0.0)
SQRT_HALF = 0.7071067811865476
INV_ROOT = 0.3989422804014327
HIGH = lax.Precision.HIGHEST
BF = jnp.bfloat16
F32 = jnp.float32

AXES = ("dp", "mp")
INNER = ("mp", 1)
OUTER = ("mp", 2)
DIAGONAL = ("mp", 3)
LOW = ("dp", 1)
FIRST = (LOW, OUTER)
SECOND = (OUTER, LOW)


def swap(value, bit):
    n_dp, n_mp = (lax.axis_size(axis) for axis in AXES)
    pairs = []
    for dp in range(n_dp):
        for mp in range(n_mp):
            axis, mask = bit if isinstance(bit[0], str) else bit[mp % 2]
            to = (dp ^ mask) * n_mp + mp if axis == "dp" else dp * n_mp + (mp ^ mask)
            pairs.append((dp * n_mp + mp, to))
    return lax.ppermute(value, AXES, pairs)


class Steps:
    def __init__(self):
        self.before = []
        self.made = []

    def next(self):
        self.before, self.made = self.made, []

    def tie(self, value):
        if not self.before:
            return value
        return lax.optimization_barrier((value, *self.before))[0]

    def add(self, value):
        self.made.append(value)
        return value

    def swap(self, value, bit):
        return self.add(swap(self.tie(value), bit))


def dp_bits():
    size = lax.axis_size("dp")
    bits = []
    mask = 1
    while mask < size:
        bits.append(("dp", mask))
        mask *= 2
    return bits


def both(part):
    return part + swap(part.astype(BF), INNER).astype(F32)


def dot(left, right, contract):
    return lax.dot_general(left, right, ((contract[0:1], contract[1:2]), ((), ())), preferred_element_type=F32)


def nn(left, right):
    return dot(left, right, (1, 0))


def nt(left, right):
    return dot(left, right, (1, 1))


def tn(left, right):
    return dot(left, right, (0, 0))


def norm_stats(value):
    centred = value - jnp.mean(value, -1, keepdims=True)
    variance = jnp.mean(centred * centred, -1, keepdims=True)
    rstd = lax.rsqrt(variance + EPSILON)
    return centred * rstd, rstd


def layer_norm(value, norm):
    return norm_stats(value)[0] * norm[0:1] + norm[1:2]


def norm_back(value, norm, d_out):
    hat, rstd = norm_stats(value)
    d_hat = d_out * norm[0:1]
    d_value = rstd * (
        d_hat - jnp.mean(d_hat, -1, keepdims=True) - hat * jnp.mean(d_hat * hat, -1, keepdims=True)
    )
    return d_value, jnp.concatenate([jnp.sum(d_out * hat, 0, keepdims=True), jnp.sum(d_out, 0, keepdims=True)], 0)


def load_weight(w, flag, own, near, across, both_ways):
    outer = pl.program_id(0) % 2
    rows = w.shape[0] // 2

    @pl.when(outer == 0)
    def _():
        w[:rows] = own[...]

    @pl.when(outer == 1)
    def _():
        w[rows:] = both_ways[...]

    @pl.when((outer == 0) & (flag[0] == 0))
    def _():
        w[rows:] = across[...]

    @pl.when((outer == 0) & (flag[0] == 1))
    def _():
        w[rows:] = near[...]

    @pl.when((outer == 1) & (flag[0] == 0))
    def _():
        w[:rows] = near[...]

    @pl.when((outer == 1) & (flag[0] == 1))
    def _():
        w[:rows] = across[...]


def store_grad(parts, flag, own, near, across, both_ways):
    outer = pl.program_id(0) % 2

    def put(target, top):
        at = 0
        for part in parts:
            rows = part.shape[0] // 2
            value = part[:rows] if top else part[rows:]
            target[:, at : at + part.shape[1]] = value.astype(BF)
            at += part.shape[1]

    @pl.when(outer == 0)
    def _():
        put(own, True)

    @pl.when(outer == 1)
    def _():
        put(both_ways, False)

    @pl.when((outer == 0) & (flag[0] == 0))
    def _():
        put(across, False)

    @pl.when((outer == 0) & (flag[0] == 1))
    def _():
        put(near, False)

    @pl.when((outer == 1) & (flag[0] == 0))
    def _():
        put(near, True)

    @pl.when((outer == 1) & (flag[0] == 1))
    def _():
        put(across, True)


def quarter_specs(weight, columns):
    steps = 2 * (weight.shape[1] // columns)
    return steps, [pl.BlockSpec((weight.shape[0], columns), lambda i: (0, i // 2))] * 4


def full(value):
    return pl.BlockSpec(value.shape, lambda i: (0,) * len(value.shape))


def spec_of(shape):
    return pl.BlockSpec(shape, lambda i: (0,) * len(shape))


FLAG = pl.BlockSpec(memory_space=pltpu.SMEM)
NO_COST = pl.CostEstimate(flops=10**6, bytes_accessed=10**4, transcendentals=0)


def params():
    return pltpu.CompilerParams(dimension_semantics=("arbitrary",), vmem_limit_bytes=56 * 1024 * 1024)


def masked_probs(scaled_query, key, keep, base, away):
    scores = jnp.where(keep, nt(scaled_query, key), base)
    top = jnp.maximum(jnp.max(scores, -1, keepdims=True), MASKED)
    weight = jnp.exp(scores - top)
    far = jnp.exp(MASKED - top)
    part = 1.0 / (jnp.sum(weight, -1, keepdims=True) + away * far)
    return weight * part, far * part


def prepare_kernel(count, *refs):
    adds = refs[:count]
    norm, real, x_ref, normed_ref, sum_ref = refs[count:]
    x = adds[0][...]
    for other in adds[1:]:
        x = x + other[...].astype(F32)
    x_ref[...] = x
    normed = layer_norm(x, norm[...]).astype(BF)
    normed_ref[...] = normed
    sum_ref[...] = jnp.sum(normed.astype(F32) * real[...], 0, keepdims=True)


def prepare(adds, norm, real):
    tokens, width = adds[0].shape
    return pl.pallas_call(
        functools.partial(prepare_kernel, len(adds)),
        grid=(1,),
        in_specs=[full(v) for v in adds] + [full(norm), full(real)],
        out_specs=[spec_of((tokens, width)), spec_of((tokens, width)), spec_of((1, width))],
        out_shape=[
            jax.ShapeDtypeStruct((tokens, width), F32),
            jax.ShapeDtypeStruct((tokens, width), BF),
            jax.ShapeDtypeStruct((1, width), F32),
        ],
        compiler_params=params(),
        cost_estimate=NO_COST,
        name="prepare",
    )(*adds, norm, real)


def below(rows, count=EXTRA):
    return jnp.concatenate([rows, jnp.zeros((count - rows.shape[0], rows.shape[1]), rows.dtype)], 0)


def attn_fwd_kernel(flag, away, normed, others, segq, segk, base, *refs):
    *weight, mix_ref, part_ref, normed_all, w, acc = refs
    step = pl.program_id(0)
    tokens = normed.shape[0]

    @pl.when(step == 0)
    def _():
        normed_all[:tokens] = normed[...]
        normed_all[tokens:] = below(others[...]).astype(BF)
        acc[...] = jnp.zeros_like(acc)

    load_weight(w, flag, *weight)
    wide = nn(normed_all[...], w[...])
    mixed = wide.astype(BF)
    c = HEAD_DIM
    width = w.shape[1] // 4
    keep = segq[...] == segk[...]
    outs = []
    for at in range(0, width, c):
        query = mixed[:tokens, at : at + c] * c ** (-0.5)
        key = mixed[:tokens, width + at : width + at + c]
        here = slice(2 * width + at, 2 * width + at + c)
        probs, far = masked_probs(query, key, keep, base[...], away[0])
        out = nn(probs.astype(BF), mixed[:tokens, here]) + far.astype(BF).astype(F32) * wide[tokens : tokens + 1, here]
        outs.append(out.astype(BF))
    out = jnp.concatenate(outs, 1)
    mix_ref[0, :, : 3 * width] = mixed[:, : 3 * width]
    mix_ref[0, :tokens, 3 * width :] = out
    mix_ref[0, tokens:, 3 * width :] = jnp.zeros((EXTRA, width), BF)
    acc[...] += nt(jnp.concatenate([jnp.zeros_like(outs[0]), out], 1), w[:, 3 * width - c :])

    @pl.when(step == pl.num_programs(0) - 1)
    def _():
        part_ref[...] = acc[...].astype(BF)


def attn_forward(normed, others, segq, segk, base, away, pieces, flag):
    tokens, width = normed.shape
    columns = pieces[0].shape[1]
    steps, quarters = quarter_specs(pieces[0], columns)
    values = (normed, others, segq, segk, base)
    return pl.pallas_call(
        attn_fwd_kernel,
        grid=(steps,),
        in_specs=[FLAG, FLAG] + [full(v) for v in values] + quarters,
        out_specs=[
            pl.BlockSpec((1, tokens + EXTRA, columns), lambda i: (i, 0, 0)),
            spec_of((tokens, width)),
        ],
        out_shape=[
            jax.ShapeDtypeStruct((steps, tokens + EXTRA, columns), BF),
            jax.ShapeDtypeStruct((tokens, width), BF),
        ],
        scratch_shapes=[
            pltpu.VMEM((tokens + EXTRA, width), BF),
            pltpu.VMEM((width, columns), BF),
            pltpu.VMEM((tokens, width), F32),
        ],
        compiler_params=params(),
        cost_estimate=NO_COST,
        name="attn_forward",
    )(flag, away, *values, *pieces)


def ff_fwd_kernel(count, *refs):
    flag = refs[0]
    adds = refs[1 : count + 1]
    norm, *weight, x_ref, part_ref, normed, w, acc = refs[count + 1 :]
    step = pl.program_id(0)

    @pl.when(step == 0)
    def _():
        x = adds[0][...]
        for other in adds[1:]:
            x = x + other[...].astype(F32)
        x_ref[...] = x
        normed[...] = layer_norm(x, norm[...]).astype(BF)
        acc[...] = jnp.zeros_like(acc)

    load_weight(w, flag, *weight)
    columns = w.shape[1] // 2
    up = nn(normed[...], w[:, :columns])
    active = (0.5 * up * (1.0 + lax.erf(up * SQRT_HALF))).astype(BF)
    acc[...] += nt(active, w[:, columns:])

    @pl.when(step == pl.num_programs(0) - 1)
    def _():
        part_ref[...] = acc[...].astype(BF)


def ff_forward(adds, norm, pieces, flag):
    tokens, width = adds[0].shape
    columns = FF_BLOCK * 2
    steps, quarters = quarter_specs(pieces[0], columns)
    return pl.pallas_call(
        functools.partial(ff_fwd_kernel, len(adds)),
        grid=(steps,),
        in_specs=[FLAG] + [full(v) for v in adds] + [full(norm)] + quarters,
        out_specs=[spec_of((tokens, width)), spec_of((tokens, width))],
        out_shape=[
            jax.ShapeDtypeStruct((tokens, width), F32),
            jax.ShapeDtypeStruct((tokens, width), BF),
        ],
        scratch_shapes=[
            pltpu.VMEM((tokens, width), BF),
            pltpu.VMEM((width, columns), BF),
            pltpu.VMEM((tokens, width), F32),
        ],
        compiler_params=params(),
        cost_estimate=NO_COST,
        name="ff_forward",
    )(flag, *adds, norm, *pieces)


def past_norm(own, other, *rest):
    total = own[...].astype(F32) + other[...].astype(F32)
    if rest:
        one, two, real = rest
        total = total + real[...] * (one[:1] + two[:1])
    return total


def back_prologue(back, d_ref, g_ref):
    d_base = back[0][...]
    if len(back) == 1:
        d_ref[...] = d_base
        return d_base
    d_value, g_ref[...] = norm_back(back[1][...], back[2][...], past_norm(*back[3:]))
    d_all = d_base + d_value
    d_ref[...] = d_all
    return d_all


def ff_back_kernel(count, *refs):
    flag = refs[0]
    back = refs[1 : count + 1]
    value, norm = refs[count + 1 : count + 3]
    weight, d_ref, grad = refs[count + 3 : count + 7], refs[count + 7], refs[count + 8 : count + 12]
    part_ref, g_ref, normed, normed_t, dz, dz_t, w, acc = refs[count + 12 :]
    step = pl.program_id(0)

    @pl.when(step == 0)
    def _():
        d_all = back_prologue(back, d_ref, g_ref)
        dz[...] = d_all.astype(BF)
        dz_t[...] = d_all.T.astype(BF)
        here = layer_norm(value[...], norm[...])
        normed[...] = here.astype(BF)
        normed_t[...] = here.T.astype(BF)
        acc[...] = jnp.zeros_like(acc)

    load_weight(w, flag, *weight)
    columns = w.shape[1] // 2
    up = nn(normed[...], w[:, :columns])
    phi = 0.5 * (1.0 + lax.erf(up * SQRT_HALF))
    active = (up * phi).astype(BF)
    slope = phi + up * jnp.exp(-0.5 * up * up) * INV_ROOT
    d_up = (nn(dz[...], w[:, columns:]) * slope).astype(BF)
    acc[...] += nt(d_up, w[:, :columns])
    store_grad([nn(normed_t[...], d_up), nn(dz_t[...], active)], flag, *grad)

    @pl.when(step == pl.num_programs(0) - 1)
    def _():
        part_ref[...] = acc[...].astype(BF)


def back_out(tokens, width, pieces, quarters):
    specs = [spec_of((tokens, width))] + quarters + [spec_of((tokens, width)), spec_of((2, width))]
    shapes = [
        jax.ShapeDtypeStruct((tokens, width), F32),
        *[jax.ShapeDtypeStruct(piece.shape, BF) for piece in pieces],
        jax.ShapeDtypeStruct((tokens, width), BF),
        jax.ShapeDtypeStruct((2, width), F32),
    ]
    return specs, shapes


def ff_backward(back, value, norm, pieces, flag):
    tokens, width = value.shape
    columns = FF_BLOCK * 2
    steps, quarters = quarter_specs(pieces[0], columns)
    specs, shapes = back_out(tokens, width, pieces, quarters)
    return pl.pallas_call(
        functools.partial(ff_back_kernel, len(back)),
        grid=(steps,),
        in_specs=[FLAG] + [full(v) for v in back] + [full(value), full(norm)] + quarters,
        out_specs=specs,
        out_shape=shapes,
        scratch_shapes=[
            pltpu.VMEM((tokens, width), BF),
            pltpu.VMEM((width, tokens), BF),
            pltpu.VMEM((tokens, width), BF),
            pltpu.VMEM((width, tokens), BF),
            pltpu.VMEM((width, columns), BF),
            pltpu.VMEM((tokens, width), F32),
        ],
        compiler_params=params(),
        cost_estimate=NO_COST,
        name="ff_backward",
    )(flag, *back, value, norm, *pieces)


def attn_back_kernel(count, *refs):
    flag, away = refs[:2]
    back = refs[2 : count + 2]
    value, norm, others, segq, segk, base, mix_ref = refs[count + 2 : count + 9]
    weight, d_ref, grad = refs[count + 9 : count + 13], refs[count + 13], refs[count + 14 : count + 18]
    part_ref, g_ref, row_ref, normed_t, dy, dy_t, w, acc, d_mix = refs[count + 18 :]
    step = pl.program_id(0)
    tokens = dy.shape[0]

    @pl.when(step == 0)
    def _():
        d_all = back_prologue(back, d_ref, g_ref)
        dy[...] = d_all.astype(BF)
        dy_t[...] = d_all.T.astype(BF)
        here = jnp.concatenate([layer_norm(value[...], norm[...]), below(others[...])], 0)
        normed_t[...] = here.T.astype(BF)
        d_mix[...] = jnp.zeros_like(d_mix)
        acc[...] = jnp.zeros_like(acc)

    load_weight(w, flag, *weight)
    c = HEAD_DIM
    scale = HEAD_DIM ** (-0.5)
    width = w.shape[1] // 4
    d_outs = nn(dy[...], w[:, 3 * width - c :])[:, c:].astype(BF)
    keep = segq[...] == segk[...]
    for at in range(0, width, c):
        query = mix_ref[0, :tokens, at : at + c] * scale
        key = mix_ref[0, :tokens, width + at : width + at + c]
        here = slice(2 * width + at, 2 * width + at + c)
        val = mix_ref[0, :tokens, here]
        val_sum = mix_ref[0, tokens:, here][:1].astype(F32)
        d_out = d_outs[:, at : at + c]
        d_wide = d_out.astype(F32)
        probs, far = masked_probs(query, key, keep, base[...], away[0])
        d_probs = nt(d_out, val)
        delta = jnp.sum(probs * d_probs, -1, keepdims=True) + far * jnp.sum(d_wide * val_sum, -1, keepdims=True)
        d_scores = jnp.where(keep, probs * (d_probs - delta), 0.0).astype(BF)
        d_mix[:tokens, at : at + c] = (nn(d_scores, key) * scale).astype(BF)
        d_mix[:tokens, width + at : width + at + c] = nn(query.T, d_scores).T.astype(BF)
        d_mix[:tokens, here] = nn(d_out.T, probs.astype(BF)).T.astype(BF)
        row = jnp.sum(far.astype(BF).astype(F32) * d_wide, 0, keepdims=True)
        d_mix[tokens:, here] = below(row).astype(BF)
    acc[...] += nt(d_mix[...], w[...])
    wide = 4 * width - (3 * width - c)
    out = jnp.concatenate([jnp.zeros((tokens, c), BF), mix_ref[0, :tokens, 3 * width :]], 1)
    left = nn(normed_t[...], d_mix[:, : 4 * width - wide])
    right = nn(normed_t[...], d_mix[:, 4 * width - wide :]) + nn(dy_t[...], out)
    store_grad([left, right], flag, *grad)

    @pl.when(step == pl.num_programs(0) - 1)
    def _():
        part_ref[...] = acc[:tokens].astype(BF)
        row_ref[...] = acc[tokens:]


def attn_backward(back, value, norm, others, segq, segk, base, away, mix, pieces, flag):
    tokens, width = value.shape
    columns = pieces[0].shape[1]
    steps, quarters = quarter_specs(pieces[0], columns)
    specs, shapes = back_out(tokens, width, pieces, quarters)
    values = (*back, value, norm, others, segq, segk, base)
    return pl.pallas_call(
        functools.partial(attn_back_kernel, len(back)),
        grid=(steps,),
        in_specs=[FLAG, FLAG]
        + [full(v) for v in values]
        + [pl.BlockSpec((1, tokens + EXTRA, columns), lambda i: (i, 0, 0))]
        + quarters,
        out_specs=specs + [spec_of((EXTRA, width))],
        out_shape=shapes + [jax.ShapeDtypeStruct((EXTRA, width), F32)],
        scratch_shapes=[
            pltpu.VMEM((width, tokens + EXTRA), BF),
            pltpu.VMEM((tokens, width), BF),
            pltpu.VMEM((width, tokens), BF),
            pltpu.VMEM((width, columns), BF),
            pltpu.VMEM((tokens + EXTRA, width), F32),
            pltpu.VMEM((tokens + EXTRA, columns), BF),
        ],
        compiler_params=params(),
        cost_estimate=NO_COST,
        name="attn_backward",
    )(flag, away, *values, mix, *pieces)


def last_kernel(base, value, norm, *refs):
    *parts, d_ref, g_ref = refs
    d_value, g_ref[...] = norm_back(value[...], norm[...], past_norm(*parts))
    d_ref[...] = (base[...] + d_value).astype(BF)


def input_gradient(back):
    tokens, width = back[0].shape
    return pl.pallas_call(
        last_kernel,
        grid=(1,),
        in_specs=[full(v) for v in back],
        out_specs=[spec_of((tokens, width)), spec_of((2, width))],
        out_shape=[
            jax.ShapeDtypeStruct((tokens, width), BF),
            jax.ShapeDtypeStruct((2, width), F32),
        ],
        compiler_params=params(),
        cost_estimate=NO_COST,
        name="input_gradient",
    )(*back)


def finish_kernel(count, *refs):
    a_keep, a_got, f_keep, f_got, into, out, up, down, square = refs[1 + count :]
    g = a_keep[...].astype(F32) + a_got[...].astype(F32)
    total = jnp.sum(g * g, 0, keepdims=True).sum(1, keepdims=True)
    width = g.shape[1] // 4
    for j in range(3):
        into[j] = g[:, j * width : (j + 1) * width]
    out[...] = g[:, 3 * width :].T
    g = f_keep[...].astype(F32) + f_got[...].astype(F32)
    total = total + jnp.sum(g * g, 0, keepdims=True).sum(1, keepdims=True)
    for i in range(g.shape[1] // (2 * FF_BLOCK)):
        here = slice(i * FF_BLOCK, (i + 1) * FF_BLOCK)
        up[:, here] = g[:, 2 * i * FF_BLOCK : (2 * i + 1) * FF_BLOCK]
        down[:, here] = g[:, (2 * i + 1) * FF_BLOCK : (2 * i + 2) * FF_BLOCK]
    square[...] = total


def finish(l, before, a_pair, f_pair, token):
    rows, width = a_pair[0].shape
    hidden = f_pair[0].shape[1] // 2
    values = (*a_pair, *f_pair)
    outs = [(3, rows, width // 4), (width // 4, rows), (rows, hidden), (rows, hidden)]

    def layer_spec(o):
        return pl.BlockSpec((None, *o), lambda i: (l,) + (0,) * len(o))

    anywhere = pl.BlockSpec(memory_space=pl.ANY)
    return pl.pallas_call(
        functools.partial(finish_kernel, len(before)),
        grid=(1,),
        in_specs=[anywhere] * (1 + len(before)) + [full(v) for v in values],
        out_specs=[layer_spec(o) for o in outs] + [spec_of((1, 1))],
        out_shape=[jax.ShapeDtypeStruct((LAYERS, *o), F32) for o in outs] + [jax.ShapeDtypeStruct((1, 1), F32)],
        input_output_aliases={1 + i: i for i in range(len(before))},
        compiler_params=params(),
        cost_estimate=NO_COST,
        name="finish",
    )(token, *before, *values)


def adam_kernel(clip_ref, *refs):
    clip = clip_ref[0]
    for kind in range(7):
        weight, grad, first, second = (refs[i * 7 + kind] for i in range(4))
        new_first, new_second, new_weight = (refs[28 + i * 7 + kind] for i in range(3))

        def update():
            g = grad[...] * clip
            new_first[...], new_second[...], new_weight[...] = adam(
                weight[...], g, first[...], second[...], RATES[kind], DECAYS[kind]
            )

        if kind < 4:
            update()
        else:
            pl.when(pl.program_id(0) == 0)(update)


def adam_all(clip, masters, grads, firsts, seconds):
    def spec(value, kind):
        if kind < 4:
            rest = value.shape[1:]
            return pl.BlockSpec((None, *rest), lambda i: (i,) + (0,) * len(rest))
        return full(value)

    specs = [spec(value, kind) for kind, value in enumerate(masters)]
    outs = pl.pallas_call(
        adam_kernel,
        grid=(LAYERS,),
        in_specs=[FLAG] + specs * 4,
        out_specs=specs * 3,
        out_shape=[jax.ShapeDtypeStruct(v.shape, F32) for v in masters] * 3,
        compiler_params=params(),
        name="adam",
    )(clip.reshape(1), *masters, *grads, *firsts, *seconds)
    return tuple(outs)


def adam(weight, grad, first, second, rate, decay):
    first = BETA_ONE * first + (1.0 - BETA_ONE) * grad
    second = BETA_TWO * second + (1.0 - BETA_TWO) * grad * grad
    update = first / (1.0 - BETA_ONE**STEP) / (jnp.sqrt(second / (1.0 - BETA_TWO**STEP)) + ADAM_EPS)
    return (first, second, weight - rate * (update + decay * weight))


def body(pixels, lengths, valid_mask, teacher_logits, teacher_map, *state):
    masters, firsts, seconds = state[:7], state[7:14], state[14:]
    attend_in, attend_out, hidden_up, hidden_down, patch_embed, class_head, norm_params = masters
    bits = dp_bits()
    low, high = bits[0], bits[1:]
    steps = Steps()
    rows = patch_embed.shape[1]
    inner = lax.axis_index("mp") % 2
    outer = lax.axis_index("mp") // 2
    images = lengths.shape[1]
    tokens = pixels.shape[0]
    total_images = images * lax.axis_size("dp")

    hidden = hidden_up.shape[2]
    width = attend_out.shape[2] * lax.axis_size("dp")

    def attn_unit(l):
        return jnp.concatenate([attend_in[l, j].astype(BF) for j in range(3)] + [attend_out[l].astype(BF).T], 1)

    def ff_unit(l):
        up = hidden_up[l].astype(BF).reshape(rows, -1, 1, FF_BLOCK)
        down = hidden_down[l].T.astype(BF).reshape(rows, -1, 1, FF_BLOCK)
        return jnp.concatenate([up, down], 2).reshape(rows, -1)

    half = class_head.shape[1] // 2
    head_unit = lax.dynamic_slice_in_dim(class_head.astype(BF), inner * half, half, 1)
    teach = jax.nn.log_softmax(teacher_logits, -1)
    teach = lax.dynamic_slice_in_dim(teach, inner * half, half, 1)
    upper = lax.optimization_barrier(teach.astype(BF))
    head_unit = jnp.concatenate([head_unit, upper, (teach - upper.astype(F32)).astype(BF)], 0)

    flag = inner.reshape(1)

    def over(unit, bits):
        for bit in bits:
            unit = jnp.stack([unit, steps.swap(unit, bit)])
        return unit

    def over_high(unit):
        if len(high) != 2:
            return over(unit, high)
        (axis, a), (_, b) = high
        return jnp.stack([unit] + [steps.swap(unit, (axis, mask)) for mask in (a, b, a | b)])

    def near(own):
        return [own, steps.swap(own, SECOND), steps.swap(own, FIRST)]

    def across(held):
        return held + [steps.swap(held[1], FIRST)]

    def far(unit):
        unit = over_high(unit)
        return unit.reshape(-1, unit.shape[-1])

    row = lengths[0]
    ends = jnp.cumsum(row)
    longest = jnp.argmax(row)
    start = ends[longest] - row[longest]
    place = jnp.arange(MOST, dtype=jnp.int32)

    def mine(value, which):
        twice = jnp.concatenate([value, value], 0)
        return lax.dynamic_slice_in_dim(twice, start + MOST * which, MOST, 0)

    pix = [mine(pixels, outer), mine(pixels, 1 - outer)]
    held = jnp.where(outer == 0, MOST, tokens - MOST)
    position = (start + MOST * outer + place) % tokens
    segment = jnp.sum((position[:, None] >= ends[None, :]).astype(jnp.int32), 1)
    valid = jnp.where(place < held, mine(valid_mask, outer), 0) > 0
    segq = segment[:, None]
    segk = jnp.where(valid, segment, -1)[None, :]
    real = (place < held).astype(F32)[:, None]
    base = jnp.where(place < held, MASKED, NEVER)[None, :]
    away = (tokens - held).astype(F32).reshape(1)
    image_ids = jnp.arange(images, dtype=jnp.int32)
    member = ((segment[None, :] == image_ids[:, None]) & valid[None, :]).astype(F32)
    owned = ((image_ids == longest) == (outer == 0)).astype(F32)[:, None]
    count = jnp.sum(member, 1)

    mid = width // 2

    def of_inner(value, which):
        return jnp.where(which == 0, value[..., :mid], value[..., mid:])

    def halves(own, other):
        return jnp.where(inner == 0, jnp.concatenate([own, other], 1), jnp.concatenate([other, own], 1))

    dp_order = high + [low]
    attn = [attn_unit(l) for l in range(LAYERS)]
    ff = [ff_unit(l) for l in range(LAYERS)]

    one, two = high[:1], high[1:]

    def together(*units):
        got = steps.swap(jnp.stack(units), high[0])
        return [jnp.stack([unit, got[i]]) for i, unit in enumerate(units)]

    def flat(unit):
        return unit.reshape(-1, unit.shape[-1])

    xs, middles, mixes, others = [], [], [], []

    def run_prepare(l, adds):
        x, normed, total = prepare(adds, norms[2 * l], real)
        xs.append(x)
        others.append(steps.swap(total, OUTER))
        return x, steps.add(normed)

    def run_attn(l, x, normed):
        mix, own = attn_forward(steps.tie(normed), others[l], segq, segk, base, away, attn[l], flag)
        mixes.append(mix)
        steps.add(own)
        return [x, own, swap(own, INNER)]

    def run_ff(l, adds):
        middle, own = ff_forward([steps.tie(adds[0])] + adds[1:], norms[2 * l + 1], ff[l], flag)
        middles.append(middle)
        steps.add(own)
        return [middle, own, swap(own, INNER)]

    for unit in attn + ff + [head_unit]:
        steps.add(unit)
    pixel_count = patch_embed.shape[0]
    patch = jnp.concatenate([patch_embed.astype(BF), norm_params.astype(BF).reshape(-1, rows)], 0).T
    patch = far(patch)
    attn[0] = over(attn[0], one)
    steps.next()
    attn[0] = flat(over(attn[0], two))
    ff[0] = over(ff[0], one)
    attn[1], attn[2] = together(attn[1], attn[2])
    patch = over(patch, [low]).reshape(width, -1)
    steps.next()
    ff[0] = flat(over(ff[0], two))
    ff[1], ff[2] = together(ff[1], ff[2])
    attn[0] = near(attn[0])
    patch = steps.tie(patch)
    norms = patch[:, pixel_count:].T.astype(F32).reshape(7, 2, width)
    part = nt(jnp.concatenate(pix, 0), patch[:, :pixel_count]).astype(BF)
    part = of_inner(part, inner).astype(F32) + swap(of_inner(part, 1 - inner), INNER).astype(F32)
    part, theirs = part[:MOST], steps.swap(part[MOST:].astype(BF), OUTER)
    steps.next()
    part = steps.tie(part) + theirs.astype(F32)
    attn[0] = across(attn[0])
    ff[0] = near(ff[0])
    attn[1] = flat(over(attn[1], two))
    prepared = run_prepare(0, [halves(part, swap(part, INNER))])
    steps.next()
    ff[0] = across(ff[0])
    attn[1] = near(attn[1])
    ff[1] = flat(over(ff[1], two))
    adds = run_attn(0, *prepared)
    steps.next()
    attn[1] = across(attn[1])
    ff[1] = near(ff[1])
    attn[2] = flat(over(attn[2], two))
    prepared = run_prepare(1, run_ff(0, adds))
    steps.next()
    ff[1] = across(ff[1])
    attn[2] = near(attn[2])
    ff[2] = flat(over(ff[2], two))
    adds = run_attn(1, *prepared)
    steps.next()
    attn[2] = across(attn[2])
    ff[2] = near(ff[2])
    head = over(head_unit, one)
    prepared = run_prepare(2, run_ff(1, adds))
    steps.next()
    ff[2] = across(ff[2])
    head = over(head, two)
    adds = run_attn(2, *prepared)
    steps.next()
    head = over(head, [low]).reshape(-1, rows + 2 * images, half)
    teach = head[:, rows : rows + images].astype(F32) + head[:, rows + images :].astype(F32)
    head = head[:, :rows].reshape(width, half)
    adds = run_ff(2, adds)
    x = sum(v.astype(F32) for v in adds)

    teach = jnp.swapaxes(teach.reshape((2, -1, images, half)), 0, 1).reshape(-1, images, half)
    me = lax.axis_index("dp")
    source = jnp.sum(jnp.where(teacher_map == me, jnp.arange(teacher_map.shape[0], dtype=jnp.int32), 0))
    teach_log = lax.dynamic_index_in_dim(teach, jnp.bitwise_xor(source, me), 0, False)

    divisor = jnp.maximum(count, 1.0)[:, None]
    pooled = jnp.dot(member, x, precision=HIGH) / divisor
    pooled_normed = layer_norm(pooled, norms[-1]).astype(BF)
    logits = nn(pooled_normed, head)
    theirs = swap(logits, INNER)
    peak = jnp.maximum(jnp.max(logits, -1, keepdims=True), jnp.max(theirs, -1, keepdims=True))
    total = jnp.sum(jnp.exp(logits - peak), -1, keepdims=True) + jnp.sum(jnp.exp(theirs - peak), -1, keepdims=True)
    student_log = logits - peak - jnp.log(total)
    loss_local = jnp.sum(owned * jnp.exp(teach_log) * (teach_log - student_log))
    d_logits = (owned * (jnp.exp(student_log) - jnp.exp(teach_log)) / total_images).astype(BF)
    g_head = tn(pooled_normed, d_logits).astype(BF)
    d_pooled, g_final = norm_back(pooled, norms[-1], both(nt(d_logits, head)))
    d_x = lax.dot_general(member, d_pooled / divisor, (((0,), (0,)), ((), ())), precision=HIGH)

    steps = Steps()
    g, g_norms = {}, {}

    def near(name):
        own, near, across, both_ways = g[name]
        near = near.astype(F32) + steps.swap(both_ways, FIRST).astype(F32)
        g[name] = own, near.astype(BF), steps.swap(across, FIRST)

    def blocks_of(value):
        value = value.astype(BF).reshape((-1, rows, value.shape[-1]))
        return [value[i] for i in range(value.shape[0])]

    def near_last(name):
        own, near, received = g[name]
        value = own.astype(F32) + received.astype(F32) + steps.swap(near, SECOND).astype(F32)
        g[name] = blocks_of(value)

    def near_low(name):
        keep, send = g[name]
        g[name] = blocks_of(keep.astype(F32) + steps.swap(send, low).astype(F32))

    def far_first(*names):
        for bit in high[:0:-1]:
            half = len(g[names[0]]) // 2
            got = steps.swap(jnp.stack([v for name in names for v in g[name][half:]]), bit)
            for k, name in enumerate(names):
                g[name] = [
                    (g[name][i].astype(F32) + got[k * half + i].astype(F32)).astype(BF) for i in range(half)
                ]

    def far_last(*names):
        got = steps.swap(jnp.stack([g[name][1] for name in names]), high[0])
        for k, name in enumerate(names):
            g[name] = (g[name][0], got[k])

    def back_ff(l, back):
        back = [steps.tie(back[0])] + back[1:]
        d_x, *grad, own, g_above = ff_backward(back, middles[l], norms[2 * l + 1], ff[l], flag)
        g["ff", l] = grad
        if l < LAYERS - 1:
            g_norms[2 * l + 2] = g_above
        steps.add(own)
        return [d_x, middles[l], norms[2 * l + 1], own, swap(own, INNER)]

    def back_attn(l, back):
        back = [steps.tie(back[0])] + back[1:]
        d_mid, *grad, own, g_above, row = attn_backward(
            back, xs[l], norms[2 * l], others[l], segq, segk, base, away, mixes[l], attn[l], flag
        )
        g["attn", l] = grad
        g_norms[2 * l + 1] = g_above
        steps.add(own)
        row = row[:8]
        rows_in = [steps.add(swap(row, OUTER)), steps.add(swap(row, DIAGONAL))]
        return [d_mid, xs[l], norms[2 * l], own, swap(own, INNER), *rows_in, real]

    g["head"] = (g_head[:mid], g_head[mid:])
    near_low("head")
    back = back_ff(2, [d_x])
    steps.next()
    near(("ff", 2))
    far_first("head")
    back = back_attn(2, back)
    steps.next()
    near(("attn", 2))
    near_last(("ff", 2))
    far_last("head")
    back = back_ff(1, back)
    steps.next()
    near(("ff", 1))
    near_last(("attn", 2))
    far_first(("ff", 2))
    back = back_attn(1, back)
    steps.next()
    near(("attn", 1))
    near_last(("ff", 1))
    far_first(("attn", 2))
    far_last(("ff", 2))
    back = back_ff(0, back)
    steps.next()
    near(("ff", 0))
    near_last(("attn", 1))
    far_first(("ff", 1))
    far_last(("attn", 2))
    back = back_attn(0, back)
    steps.next()
    d_x0, g_norms[0] = input_gradient([steps.tie(back[0])] + back[1:])
    theirs = steps.swap(of_inner(d_x0, inner), OUTER)
    near(("attn", 0))
    near_last(("ff", 0))
    far_first(("attn", 1))
    far_last(("ff", 1))
    theirs = halves(theirs, swap(theirs, INNER))
    g_patch = tn(jnp.concatenate([d_x0, theirs], 0), jnp.concatenate(pix, 0)).astype(BF)
    steps.add(g_patch)
    g["patch"] = (g_patch[:mid], g_patch[mid:])
    token = g_norms[0]
    *done, square_two = finish(2, [], g["attn", 2], g["ff", 2], token)
    steps.next()
    near_low("patch")
    near_last(("attn", 0))
    far_first(("ff", 0))
    far_last(("attn", 1))
    g_head = steps.tie(g["head"][0]).astype(F32) + g["head"][1].astype(F32)
    g_head = g_head + steps.swap(g_head, OUTER)
    g_norm = steps.tie(jnp.concatenate([g_norms[i] for i in range(6)] + [g_final], 0))
    g_norm = 0.5 * (g_norm + swap(g_norm, INNER))
    *done, square_one = finish(1, done, g["attn", 1], g["ff", 1], g_patch)
    steps.next()
    far_first(("attn", 0), "patch")
    far_last(("ff", 0))
    g_norm = g_norm + steps.swap(g_norm, OUTER)
    g_norm = jnp.moveaxis(g_norm.reshape(14, 2, -1, rows), 0, 2)
    g_norm = g_norm[0] + steps.swap(g_norm[1], low)
    g_head = halves(g_head, swap(g_head, INNER))
    steps.next()
    far_last(("attn", 0), "patch")
    g_norm = g_norm.reshape((2,) * len(high) + (14, rows))
    for bit in high[::-1]:
        g_norm = g_norm[0] + steps.swap(g_norm[1], bit)
    g_norm = g_norm.reshape(7, 2, rows)
    *done, square_zero = finish(0, done, g["attn", 0], g["ff", 0], g_patch)
    g_patch = g["patch"][0].astype(F32) + g["patch"][1].astype(F32)

    grads = (*done, g_patch, g_head, g_norm)
    first_model = (lax.axis_index("mp") == 0).astype(F32)
    squares = (square_two + square_one + square_zero)[0, 0] + jnp.sum(g_patch * g_patch) + first_model * (
        jnp.sum(g_head * g_head) + jnp.sum(g_norm * g_norm)
    )
    sums = jnp.stack([squares, loss_local * (outer >= 0)])
    sums = sums + swap(sums, INNER)
    sums = sums + swap(sums, OUTER)
    if len(high) == 2:
        (axis, a), (_, b) = high
        sums = sums + swap(sums, low)
        sums = (sums + swap(sums, (axis, a))) + (swap(sums, (axis, b)) + swap(sums, (axis, a | b)))
    else:
        for bit in bits:
            sums = sums + swap(sums, bit)
    loss = sums[1]
    grad_norm = jnp.sqrt(sums[0])
    clip = jnp.minimum(1.0, CLIP / grad_norm)

    def turned(values):
        return (*values[:3], values[3].swapaxes(1, 2), values[4].T, *values[5:])

    masters, firsts, seconds = turned(masters), turned(firsts), turned(seconds)
    outs = adam_all(clip, masters, grads, firsts, seconds)
    return (loss, grad_norm) + turned(outs[:7]) + turned(outs[7:14]) + turned(outs[14:])


def solution(mesh):
    weights = (
        P(None, None, "dp", "mp"),
        P(None, "mp", "dp"),
        P(None, "dp", "mp"),
        P(None, "mp", "dp"),
        P("mp", "dp"),
        P("dp", None),
        P(None, None, "dp"),
    )
    placed = (P("dp", "mp"), P("dp", None), P("dp"), P("dp", None), P()) + weights * 3
    return jax.shard_map(
        body, mesh=mesh, in_specs=placed, out_specs=(P(), P()) + weights * 3, check_vma=False
    )
```

```python
import functools

import jax
import jax.numpy as jnp
from jax import lax
from jax.experimental import pallas as pl
from jax.experimental.pallas import tpu as pltpu
from jax.sharding import PartitionSpec as P

HEAD_DIM = 64
LAYERS = 3
STEP = 10
MOST = 576
EXTRA = 16
NEVER = -1e30
FF_BLOCK = 256

EPSILON = 1e-06
MASKED = -30000.0
CLIP = 0.005
BETA_ONE = 0.9
BETA_TWO = 0.999
ADAM_EPS = 1e-08
RATES = (0.02, 0.06, 0.02, 0.02, 0.02, 0.02, 0.5)
DECAYS = (0.05, 0.05, 0.05, 0.05, 0.05, 0.05, 0.0)
SQRT_HALF = 0.7071067811865476
INV_ROOT = 0.3989422804014327
HIGH = lax.Precision.HIGHEST
BF = jnp.bfloat16
F32 = jnp.float32

AXES = ("dp", "mp")
INNER = ("mp", 1)
OUTER = ("mp", 2)
DIAGONAL = ("mp", 3)
LOW = ("dp", 1)
FIRST = (LOW, OUTER)
SECOND = (OUTER, LOW)


def swap(value, bit):
    n_dp, n_mp = (lax.axis_size(axis) for axis in AXES)
    pairs = []
    for dp in range(n_dp):
        for mp in range(n_mp):
            axis, mask = bit if isinstance(bit[0], str) else bit[mp % 2]
            to = (dp ^ mask) * n_mp + mp if axis == "dp" else dp * n_mp + (mp ^ mask)
            pairs.append((dp * n_mp + mp, to))
    return lax.ppermute(value, AXES, pairs)


class Steps:
    def __init__(self):
        self.before = []
        self.made = []

    def next(self):
        self.before, self.made = self.made, []

    def tie(self, value):
        if not self.before:
            return value
        return lax.optimization_barrier((value, *self.before))[0]

    def add(self, value):
        self.made.append(value)
        return value

    def swap(self, value, bit):
        return self.add(swap(self.tie(value), bit))


def dp_bits():
    size = lax.axis_size("dp")
    bits = []
    mask = 1
    while mask < size:
        bits.append(("dp", mask))
        mask *= 2
    return bits


def both(part):
    return part + swap(part.astype(BF), INNER).astype(F32)


def dot(left, right, contract):
    return lax.dot_general(left, right, ((contract[0:1], contract[1:2]), ((), ())), preferred_element_type=F32)


def nn(left, right):
    return dot(left, right, (1, 0))


def nt(left, right):
    return dot(left, right, (1, 1))


def tn(left, right):
    return dot(left, right, (0, 0))


def norm_stats(value):
    centred = value - jnp.mean(value, -1, keepdims=True)
    variance = jnp.mean(centred * centred, -1, keepdims=True)
    rstd = lax.rsqrt(variance + EPSILON)
    return centred * rstd, rstd


def layer_norm(value, norm):
    return norm_stats(value)[0] * norm[0:1] + norm[1:2]


def norm_back(value, norm, d_out):
    hat, rstd = norm_stats(value)
    d_hat = d_out * norm[0:1]
    d_value = rstd * (
        d_hat - jnp.mean(d_hat, -1, keepdims=True) - hat * jnp.mean(d_hat * hat, -1, keepdims=True)
    )
    return d_value, jnp.concatenate([jnp.sum(d_out * hat, 0, keepdims=True), jnp.sum(d_out, 0, keepdims=True)], 0)


def load_weight(w, flag, own, near, across, both_ways):
    outer = pl.program_id(0) % 2
    rows = w.shape[0] // 2

    @pl.when(outer == 0)
    def _():
        w[:rows] = own[...]

    @pl.when(outer == 1)
    def _():
        w[rows:] = both_ways[...]

    @pl.when((outer == 0) & (flag[0] == 0))
    def _():
        w[rows:] = across[...]

    @pl.when((outer == 0) & (flag[0] == 1))
    def _():
        w[rows:] = near[...]

    @pl.when((outer == 1) & (flag[0] == 0))
    def _():
        w[:rows] = near[...]

    @pl.when((outer == 1) & (flag[0] == 1))
    def _():
        w[:rows] = across[...]


def store_grad(parts, flag, own, near, across, both_ways):
    outer = pl.program_id(0) % 2

    def put(target, top):
        at = 0
        for part in parts:
            rows = part.shape[0] // 2
            value = part[:rows] if top else part[rows:]
            target[:, at : at + part.shape[1]] = value.astype(BF)
            at += part.shape[1]

    @pl.when(outer == 0)
    def _():
        put(own, True)

    @pl.when(outer == 1)
    def _():
        put(both_ways, False)

    @pl.when((outer == 0) & (flag[0] == 0))
    def _():
        put(across, False)

    @pl.when((outer == 0) & (flag[0] == 1))
    def _():
        put(near, False)

    @pl.when((outer == 1) & (flag[0] == 0))
    def _():
        put(near, True)

    @pl.when((outer == 1) & (flag[0] == 1))
    def _():
        put(across, True)


def quarter_specs(weight, columns):
    steps = 2 * (weight.shape[1] // columns)
    return steps, [pl.BlockSpec((weight.shape[0], columns), lambda i: (0, i // 2))] * 4


def full(value):
    return pl.BlockSpec(value.shape, lambda i: (0,) * len(value.shape))


def spec_of(shape):
    return pl.BlockSpec(shape, lambda i: (0,) * len(shape))


FLAG = pl.BlockSpec(memory_space=pltpu.SMEM)
NO_COST = pl.CostEstimate(flops=10**6, bytes_accessed=10**4, transcendentals=0)


def params():
    return pltpu.CompilerParams(dimension_semantics=("arbitrary",), vmem_limit_bytes=56 * 1024 * 1024)


def masked_probs(scaled_query, key, keep, base, away):
    scores = jnp.where(keep, nt(scaled_query, key), base)
    top = jnp.maximum(jnp.max(scores, -1, keepdims=True), MASKED)
    weight = jnp.exp(scores - top)
    far = jnp.exp(MASKED - top)
    part = 1.0 / (jnp.sum(weight, -1, keepdims=True) + away * far)
    return weight * part, far * part


def prepare_kernel(count, *refs):
    adds = refs[:count]
    norm, real, x_ref, normed_ref, sum_ref = refs[count:]
    x = adds[0][...]
    for other in adds[1:]:
        x = x + other[...].astype(F32)
    x_ref[...] = x
    normed = layer_norm(x, norm[...]).astype(BF)
    normed_ref[...] = normed
    sum_ref[...] = jnp.sum(normed.astype(F32) * real[...], 0, keepdims=True)


def prepare(adds, norm, real):
    tokens, width = adds[0].shape
    return pl.pallas_call(
        functools.partial(prepare_kernel, len(adds)),
        grid=(1,),
        in_specs=[full(v) for v in adds] + [full(norm), full(real)],
        out_specs=[spec_of((tokens, width)), spec_of((tokens, width)), spec_of((1, width))],
        out_shape=[
            jax.ShapeDtypeStruct((tokens, width), F32),
            jax.ShapeDtypeStruct((tokens, width), BF),
            jax.ShapeDtypeStruct((1, width), F32),
        ],
        compiler_params=params(),
        cost_estimate=NO_COST,
        name="prepare",
    )(*adds, norm, real)


def below(rows, count=EXTRA):
    return jnp.concatenate([rows, jnp.zeros((count - rows.shape[0], rows.shape[1]), rows.dtype)], 0)


def attn_fwd_kernel(flag, away, normed, others, segq, segk, base, *refs):
    *weight, mix_ref, part_ref, normed_all, w, acc = refs
    step = pl.program_id(0)
    tokens = normed.shape[0]

    @pl.when(step == 0)
    def _():
        normed_all[:tokens] = normed[...]
        normed_all[tokens:] = below(others[...]).astype(BF)
        acc[...] = jnp.zeros_like(acc)

    load_weight(w, flag, *weight)
    wide = nn(normed_all[...], w[...])
    mixed = wide.astype(BF)
    c = HEAD_DIM
    width = w.shape[1] // 4
    keep = segq[...] == segk[...]
    outs = []
    for at in range(0, width, c):
        query = mixed[:tokens, at : at + c] * c ** (-0.5)
        key = mixed[:tokens, width + at : width + at + c]
        here = slice(2 * width + at, 2 * width + at + c)
        probs, far = masked_probs(query, key, keep, base[...], away[0])
        out = nn(probs.astype(BF), mixed[:tokens, here]) + far.astype(BF).astype(F32) * wide[tokens : tokens + 1, here]
        outs.append(out.astype(BF))
    out = jnp.concatenate(outs, 1)
    mix_ref[0, :, : 3 * width] = mixed[:, : 3 * width]
    mix_ref[0, :tokens, 3 * width :] = out
    mix_ref[0, tokens:, 3 * width :] = jnp.zeros((EXTRA, width), BF)
    acc[...] += nt(jnp.concatenate([jnp.zeros_like(outs[0]), out], 1), w[:, 3 * width - c :])

    @pl.when(step == pl.num_programs(0) - 1)
    def _():
        part_ref[...] = acc[...].astype(BF)


def attn_forward(normed, others, segq, segk, base, away, pieces, flag):
    tokens, width = normed.shape
    columns = pieces[0].shape[1]
    steps, quarters = quarter_specs(pieces[0], columns)
    values = (normed, others, segq, segk, base)
    return pl.pallas_call(
        attn_fwd_kernel,
        grid=(steps,),
        in_specs=[FLAG, FLAG] + [full(v) for v in values] + quarters,
        out_specs=[
            pl.BlockSpec((1, tokens + EXTRA, columns), lambda i: (i, 0, 0)),
            spec_of((tokens, width)),
        ],
        out_shape=[
            jax.ShapeDtypeStruct((steps, tokens + EXTRA, columns), BF),
            jax.ShapeDtypeStruct((tokens, width), BF),
        ],
        scratch_shapes=[
            pltpu.VMEM((tokens + EXTRA, width), BF),
            pltpu.VMEM((width, columns), BF),
            pltpu.VMEM((tokens, width), F32),
        ],
        compiler_params=params(),
        cost_estimate=NO_COST,
        name="attn_forward",
    )(flag, away, *values, *pieces)


def ff_fwd_kernel(count, *refs):
    flag = refs[0]
    adds = refs[1 : count + 1]
    norm, *weight, x_ref, part_ref, normed, w, acc = refs[count + 1 :]
    step = pl.program_id(0)

    @pl.when(step == 0)
    def _():
        x = adds[0][...]
        for other in adds[1:]:
            x = x + other[...].astype(F32)
        x_ref[...] = x
        normed[...] = layer_norm(x, norm[...]).astype(BF)
        acc[...] = jnp.zeros_like(acc)

    load_weight(w, flag, *weight)
    columns = w.shape[1] // 2
    up = nn(normed[...], w[:, :columns])
    active = (0.5 * up * (1.0 + lax.erf(up * SQRT_HALF))).astype(BF)
    acc[...] += nt(active, w[:, columns:])

    @pl.when(step == pl.num_programs(0) - 1)
    def _():
        part_ref[...] = acc[...].astype(BF)


def ff_forward(adds, norm, pieces, flag):
    tokens, width = adds[0].shape
    columns = FF_BLOCK * 2
    steps, quarters = quarter_specs(pieces[0], columns)
    return pl.pallas_call(
        functools.partial(ff_fwd_kernel, len(adds)),
        grid=(steps,),
        in_specs=[FLAG] + [full(v) for v in adds] + [full(norm)] + quarters,
        out_specs=[spec_of((tokens, width)), spec_of((tokens, width))],
        out_shape=[
            jax.ShapeDtypeStruct((tokens, width), F32),
            jax.ShapeDtypeStruct((tokens, width), BF),
        ],
        scratch_shapes=[
            pltpu.VMEM((tokens, width), BF),
            pltpu.VMEM((width, columns), BF),
            pltpu.VMEM((tokens, width), F32),
        ],
        compiler_params=params(),
        cost_estimate=NO_COST,
        name="ff_forward",
    )(flag, *adds, norm, *pieces)


def past_norm(own, other, *rest):
    total = own[...].astype(F32) + other[...].astype(F32)
    if rest:
        one, two, real = rest
        total = total + real[...] * (one[:1] + two[:1])
    return total


def back_prologue(back, d_ref, g_ref):
    d_base = back[0][...]
    if len(back) == 1:
        d_ref[...] = d_base
        return d_base
    d_value, g_ref[...] = norm_back(back[1][...], back[2][...], past_norm(*back[3:]))
    d_all = d_base + d_value
    d_ref[...] = d_all
    return d_all


def ff_back_kernel(count, *refs):
    flag = refs[0]
    back = refs[1 : count + 1]
    value, norm = refs[count + 1 : count + 3]
    weight, d_ref, grad = refs[count + 3 : count + 7], refs[count + 7], refs[count + 8 : count + 12]
    part_ref, g_ref, normed, normed_t, dz, dz_t, w, acc = refs[count + 12 :]
    step = pl.program_id(0)

    @pl.when(step == 0)
    def _():
        d_all = back_prologue(back, d_ref, g_ref)
        dz[...] = d_all.astype(BF)
        dz_t[...] = d_all.T.astype(BF)
        here = layer_norm(value[...], norm[...])
        normed[...] = here.astype(BF)
        normed_t[...] = here.T.astype(BF)
        acc[...] = jnp.zeros_like(acc)

    load_weight(w, flag, *weight)
    columns = w.shape[1] // 2
    up = nn(normed[...], w[:, :columns])
    phi = 0.5 * (1.0 + lax.erf(up * SQRT_HALF))
    active = (up * phi).astype(BF)
    slope = phi + up * jnp.exp(-0.5 * up * up) * INV_ROOT
    d_up = (nn(dz[...], w[:, columns:]) * slope).astype(BF)
    acc[...] += nt(d_up, w[:, :columns])
    store_grad([nn(normed_t[...], d_up), nn(dz_t[...], active)], flag, *grad)

    @pl.when(step == pl.num_programs(0) - 1)
    def _():
        part_ref[...] = acc[...].astype(BF)


def back_out(tokens, width, pieces, quarters):
    specs = [spec_of((tokens, width))] + quarters + [spec_of((tokens, width)), spec_of((2, width))]
    shapes = [
        jax.ShapeDtypeStruct((tokens, width), F32),
        *[jax.ShapeDtypeStruct(piece.shape, BF) for piece in pieces],
        jax.ShapeDtypeStruct((tokens, width), BF),
        jax.ShapeDtypeStruct((2, width), F32),
    ]
    return specs, shapes


def ff_backward(back, value, norm, pieces, flag):
    tokens, width = value.shape
    columns = FF_BLOCK * 2
    steps, quarters = quarter_specs(pieces[0], columns)
    specs, shapes = back_out(tokens, width, pieces, quarters)
    return pl.pallas_call(
        functools.partial(ff_back_kernel, len(back)),
        grid=(steps,),
        in_specs=[FLAG] + [full(v) for v in back] + [full(value), full(norm)] + quarters,
        out_specs=specs,
        out_shape=shapes,
        scratch_shapes=[
            pltpu.VMEM((tokens, width), BF),
            pltpu.VMEM((width, tokens), BF),
            pltpu.VMEM((tokens, width), BF),
            pltpu.VMEM((width, tokens), BF),
            pltpu.VMEM((width, columns), BF),
            pltpu.VMEM((tokens, width), F32),
        ],
        compiler_params=params(),
        cost_estimate=NO_COST,
        name="ff_backward",
    )(flag, *back, value, norm, *pieces)


def attn_back_kernel(count, *refs):
    flag, away = refs[:2]
    back = refs[2 : count + 2]
    value, norm, others, segq, segk, base, mix_ref = refs[count + 2 : count + 9]
    weight, d_ref, grad = refs[count + 9 : count + 13], refs[count + 13], refs[count + 14 : count + 18]
    part_ref, g_ref, row_ref, normed_t, dy, dy_t, w, acc, d_mix = refs[count + 18 :]
    step = pl.program_id(0)
    tokens = dy.shape[0]

    @pl.when(step == 0)
    def _():
        d_all = back_prologue(back, d_ref, g_ref)
        dy[...] = d_all.astype(BF)
        dy_t[...] = d_all.T.astype(BF)
        here = jnp.concatenate([layer_norm(value[...], norm[...]), below(others[...])], 0)
        normed_t[...] = here.T.astype(BF)
        d_mix[...] = jnp.zeros_like(d_mix)
        acc[...] = jnp.zeros_like(acc)

    load_weight(w, flag, *weight)
    c = HEAD_DIM
    scale = HEAD_DIM ** (-0.5)
    width = w.shape[1] // 4
    d_outs = nn(dy[...], w[:, 3 * width - c :])[:, c:].astype(BF)
    keep = segq[...] == segk[...]
    for at in range(0, width, c):
        query = mix_ref[0, :tokens, at : at + c] * scale
        key = mix_ref[0, :tokens, width + at : width + at + c]
        here = slice(2 * width + at, 2 * width + at + c)
        val = mix_ref[0, :tokens, here]
        val_sum = mix_ref[0, tokens:, here][:1].astype(F32)
        d_out = d_outs[:, at : at + c]
        d_wide = d_out.astype(F32)
        probs, far = masked_probs(query, key, keep, base[...], away[0])
        d_probs = nt(d_out, val)
        delta = jnp.sum(probs * d_probs, -1, keepdims=True) + far * jnp.sum(d_wide * val_sum, -1, keepdims=True)
        d_scores = jnp.where(keep, probs * (d_probs - delta), 0.0).astype(BF)
        d_mix[:tokens, at : at + c] = (nn(d_scores, key) * scale).astype(BF)
        d_mix[:tokens, width + at : width + at + c] = nn(query.T, d_scores).T.astype(BF)
        d_mix[:tokens, here] = nn(d_out.T, probs.astype(BF)).T.astype(BF)
        row = jnp.sum(far.astype(BF).astype(F32) * d_wide, 0, keepdims=True)
        d_mix[tokens:, here] = below(row).astype(BF)
    acc[...] += nt(d_mix[...], w[...])
    wide = 4 * width - (3 * width - c)
    out = jnp.concatenate([jnp.zeros((tokens, c), BF), mix_ref[0, :tokens, 3 * width :]], 1)
    left = nn(normed_t[...], d_mix[:, : 4 * width - wide])
    right = nn(normed_t[...], d_mix[:, 4 * width - wide :]) + nn(dy_t[...], out)
    store_grad([left, right], flag, *grad)

    @pl.when(step == pl.num_programs(0) - 1)
    def _():
        part_ref[...] = acc[:tokens].astype(BF)
        row_ref[...] = acc[tokens:]


def attn_backward(back, value, norm, others, segq, segk, base, away, mix, pieces, flag):
    tokens, width = value.shape
    columns = pieces[0].shape[1]
    steps, quarters = quarter_specs(pieces[0], columns)
    specs, shapes = back_out(tokens, width, pieces, quarters)
    values = (*back, value, norm, others, segq, segk, base)
    return pl.pallas_call(
        functools.partial(attn_back_kernel, len(back)),
        grid=(steps,),
        in_specs=[FLAG, FLAG]
        + [full(v) for v in values]
        + [pl.BlockSpec((1, tokens + EXTRA, columns), lambda i: (i, 0, 0))]
        + quarters,
        out_specs=specs + [spec_of((EXTRA, width))],
        out_shape=shapes + [jax.ShapeDtypeStruct((EXTRA, width), F32)],
        scratch_shapes=[
            pltpu.VMEM((width, tokens + EXTRA), BF),
            pltpu.VMEM((tokens, width), BF),
            pltpu.VMEM((width, tokens), BF),
            pltpu.VMEM((width, columns), BF),
            pltpu.VMEM((tokens + EXTRA, width), F32),
            pltpu.VMEM((tokens + EXTRA, columns), BF),
        ],
        compiler_params=params(),
        cost_estimate=NO_COST,
        name="attn_backward",
    )(flag, away, *values, mix, *pieces)


def last_kernel(base, value, norm, *refs):
    *parts, d_ref, g_ref = refs
    d_value, g_ref[...] = norm_back(value[...], norm[...], past_norm(*parts))
    d_ref[...] = (base[...] + d_value).astype(BF)


def input_gradient(back):
    tokens, width = back[0].shape
    return pl.pallas_call(
        last_kernel,
        grid=(1,),
        in_specs=[full(v) for v in back],
        out_specs=[spec_of((tokens, width)), spec_of((2, width))],
        out_shape=[
            jax.ShapeDtypeStruct((tokens, width), BF),
            jax.ShapeDtypeStruct((2, width), F32),
        ],
        compiler_params=params(),
        cost_estimate=NO_COST,
        name="input_gradient",
    )(*back)


def finish_kernel(count, *refs):
    a_keep, a_got, f_keep, f_got, into, out, up, down, square = refs[1 + count :]
    g = a_keep[...].astype(F32) + a_got[...].astype(F32)
    total = jnp.sum(g * g, 0, keepdims=True).sum(1, keepdims=True)
    width = g.shape[1] // 4
    for j in range(3):
        into[j] = g[:, j * width : (j + 1) * width]
    out[...] = g[:, 3 * width :].T
    g = f_keep[...].astype(F32) + f_got[...].astype(F32)
    total = total + jnp.sum(g * g, 0, keepdims=True).sum(1, keepdims=True)
    for i in range(g.shape[1] // (2 * FF_BLOCK)):
        here = slice(i * FF_BLOCK, (i + 1) * FF_BLOCK)
        up[:, here] = g[:, 2 * i * FF_BLOCK : (2 * i + 1) * FF_BLOCK]
        down[:, here] = g[:, (2 * i + 1) * FF_BLOCK : (2 * i + 2) * FF_BLOCK]
    square[...] = total


def finish(l, before, a_pair, f_pair, token):
    rows, width = a_pair[0].shape
    hidden = f_pair[0].shape[1] // 2
    values = (*a_pair, *f_pair)
    outs = [(3, rows, width // 4), (width // 4, rows), (rows, hidden), (rows, hidden)]

    def layer_spec(o):
        return pl.BlockSpec((None, *o), lambda i: (l,) + (0,) * len(o))

    anywhere = pl.BlockSpec(memory_space=pl.ANY)
    return pl.pallas_call(
        functools.partial(finish_kernel, len(before)),
        grid=(1,),
        in_specs=[anywhere] * (1 + len(before)) + [full(v) for v in values],
        out_specs=[layer_spec(o) for o in outs] + [spec_of((1, 1))],
        out_shape=[jax.ShapeDtypeStruct((LAYERS, *o), F32) for o in outs] + [jax.ShapeDtypeStruct((1, 1), F32)],
        input_output_aliases={1 + i: i for i in range(len(before))},
        compiler_params=params(),
        cost_estimate=NO_COST,
        name="finish",
    )(token, *before, *values)


def adam_kernel(clip_ref, *refs):
    clip = clip_ref[0]
    for kind in range(7):
        weight, grad, first, second = (refs[i * 7 + kind] for i in range(4))
        new_first, new_second, new_weight = (refs[28 + i * 7 + kind] for i in range(3))

        def update():
            g = grad[...] * clip
            new_first[...], new_second[...], new_weight[...] = adam(
                weight[...], g, first[...], second[...], RATES[kind], DECAYS[kind]
            )

        if kind < 4:
            update()
        else:
            pl.when(pl.program_id(0) == 0)(update)


def adam_all(clip, masters, grads, firsts, seconds):
    def spec(value, kind):
        if kind < 4:
            rest = value.shape[1:]
            return pl.BlockSpec((None, *rest), lambda i: (i,) + (0,) * len(rest))
        return full(value)

    specs = [spec(value, kind) for kind, value in enumerate(masters)]
    outs = pl.pallas_call(
        adam_kernel,
        grid=(LAYERS,),
        in_specs=[FLAG] + specs * 4,
        out_specs=specs * 3,
        out_shape=[jax.ShapeDtypeStruct(v.shape, F32) for v in masters] * 3,
        compiler_params=params(),
        name="adam",
    )(clip.reshape(1), *masters, *grads, *firsts, *seconds)
    return tuple(outs)


def adam(weight, grad, first, second, rate, decay):
    first = BETA_ONE * first + (1.0 - BETA_ONE) * grad
    second = BETA_TWO * second + (1.0 - BETA_TWO) * grad * grad
    update = first / (1.0 - BETA_ONE**STEP) / (jnp.sqrt(second / (1.0 - BETA_TWO**STEP)) + ADAM_EPS)
    return (first, second, weight - rate * (update + decay * weight))


def body(pixels, lengths, valid_mask, teacher_logits, teacher_map, *state):
    masters, firsts, seconds = state[:7], state[7:14], state[14:]
    attend_in, attend_out, hidden_up, hidden_down, patch_embed, class_head, norm_params = masters
    bits = dp_bits()
    low, high = bits[0], bits[1:]
    steps = Steps()
    rows = patch_embed.shape[1]
    inner = lax.axis_index("mp") % 2
    outer = lax.axis_index("mp") // 2
    images = lengths.shape[1]
    tokens = pixels.shape[0]
    total_images = images * lax.axis_size("dp")

    hidden = hidden_up.shape[2]
    width = attend_out.shape[2] * lax.axis_size("dp")

    def attn_unit(l):
        return jnp.concatenate([attend_in[l, j].astype(BF) for j in range(3)] + [attend_out[l].astype(BF).T], 1)

    def ff_unit(l):
        up = hidden_up[l].astype(BF).reshape(rows, -1, 1, FF_BLOCK)
        down = hidden_down[l].T.astype(BF).reshape(rows, -1, 1, FF_BLOCK)
        return jnp.concatenate([up, down], 2).reshape(rows, -1)

    half = class_head.shape[1] // 2
    head_unit = lax.dynamic_slice_in_dim(class_head.astype(BF), inner * half, half, 1)
    teach = jax.nn.log_softmax(teacher_logits, -1)
    teach = lax.dynamic_slice_in_dim(teach, inner * half, half, 1)
    upper = lax.optimization_barrier(teach.astype(BF))
    head_unit = jnp.concatenate([head_unit, upper, (teach - upper.astype(F32)).astype(BF)], 0)

    flag = inner.reshape(1)

    def over(unit, bits):
        for bit in bits:
            unit = jnp.stack([unit, steps.swap(unit, bit)])
        return unit

    def over_high(unit):
        if len(high) != 2:
            return over(unit, high)
        (axis, a), (_, b) = high
        return jnp.stack([unit] + [steps.swap(unit, (axis, mask)) for mask in (a, b, a | b)])

    def near(own):
        return [own, steps.swap(own, SECOND), steps.swap(own, FIRST)]

    def across(held):
        return held + [steps.swap(held[1], FIRST)]

    def far(unit):
        unit = over_high(unit)
        return unit.reshape(-1, unit.shape[-1])

    row = lengths[0]
    ends = jnp.cumsum(row)
    longest = jnp.argmax(row)
    start = ends[longest] - row[longest]
    place = jnp.arange(MOST, dtype=jnp.int32)

    def mine(value, which):
        twice = jnp.concatenate([value, value], 0)
        return lax.dynamic_slice_in_dim(twice, start + MOST * which, MOST, 0)

    pix = [mine(pixels, outer), mine(pixels, 1 - outer)]
    held = jnp.where(outer == 0, MOST, tokens - MOST)
    position = (start + MOST * outer + place) % tokens
    segment = jnp.sum((position[:, None] >= ends[None, :]).astype(jnp.int32), 1)
    valid = jnp.where(place < held, mine(valid_mask, outer), 0) > 0
    segq = segment[:, None]
    segk = jnp.where(valid, segment, -1)[None, :]
    real = (place < held).astype(F32)[:, None]
    base = jnp.where(place < held, MASKED, NEVER)[None, :]
    away = (tokens - held).astype(F32).reshape(1)
    image_ids = jnp.arange(images, dtype=jnp.int32)
    member = ((segment[None, :] == image_ids[:, None]) & valid[None, :]).astype(F32)
    owned = ((image_ids == longest) == (outer == 0)).astype(F32)[:, None]
    count = jnp.sum(member, 1)

    mid = width // 2

    def of_inner(value, which):
        return jnp.where(which == 0, value[..., :mid], value[..., mid:])

    def halves(own, other):
        return jnp.where(inner == 0, jnp.concatenate([own, other], 1), jnp.concatenate([other, own], 1))

    dp_order = high + [low]
    attn = [attn_unit(l) for l in range(LAYERS)]
    ff = [ff_unit(l) for l in range(LAYERS)]

    one, two = high[:1], high[1:]

    def together(*units):
        got = steps.swap(jnp.stack(units), high[0])
        return [jnp.stack([unit, got[i]]) for i, unit in enumerate(units)]

    def flat(unit):
        return unit.reshape(-1, unit.shape[-1])

    xs, middles, mixes, others = [], [], [], []

    def run_prepare(l, adds):
        x, normed, total = prepare(adds, norms[2 * l], real)
        xs.append(x)
        others.append(steps.swap(total, OUTER))
        return x, steps.add(normed)

    def run_attn(l, x, normed):
        mix, own = attn_forward(steps.tie(normed), others[l], segq, segk, base, away, attn[l], flag)
        mixes.append(mix)
        steps.add(own)
        return [x, own, swap(own, INNER)]

    def run_ff(l, adds):
        middle, own = ff_forward([steps.tie(adds[0])] + adds[1:], norms[2 * l + 1], ff[l], flag)
        middles.append(middle)
        steps.add(own)
        return [middle, own, swap(own, INNER)]

    for unit in attn + ff + [head_unit]:
        steps.add(unit)
    pixel_count = patch_embed.shape[0]
    patch = jnp.concatenate([patch_embed.astype(BF), norm_params.astype(BF).reshape(-1, rows)], 0).T
    patch = far(patch)
    attn[0] = over(attn[0], one)
    attn[1], attn[2] = together(attn[1], attn[2])
    steps.next()
    attn[0] = flat(over(attn[0], two))
    ff[0] = over(ff[0], one)
    head = over(head_unit, one)
    patch = over(patch, [low]).reshape(width, -1)
    steps.next()
    ff[0] = flat(over(ff[0], two))
    ff[1], ff[2] = together(ff[1], ff[2])
    attn[0] = near(attn[0])
    patch = steps.tie(patch)
    norms = patch[:, pixel_count:].T.astype(F32).reshape(7, 2, width)
    part = nt(jnp.concatenate(pix, 0), patch[:, :pixel_count]).astype(BF)
    part = of_inner(part, inner).astype(F32) + swap(of_inner(part, 1 - inner), INNER).astype(F32)
    part, theirs = part[:MOST], steps.swap(part[MOST:].astype(BF), OUTER)
    steps.next()
    part = steps.tie(part) + theirs.astype(F32)
    attn[0] = across(attn[0])
    ff[0] = near(ff[0])
    attn[1] = flat(over(attn[1], two))
    prepared = run_prepare(0, [halves(part, swap(part, INNER))])
    steps.next()
    ff[0] = across(ff[0])
    attn[1] = near(attn[1])
    ff[1] = flat(over(ff[1], two))
    adds = run_attn(0, *prepared)
    steps.next()
    attn[1] = across(attn[1])
    ff[1] = near(ff[1])
    attn[2] = flat(over(attn[2], two))
    prepared = run_prepare(1, run_ff(0, adds))
    steps.next()
    ff[1] = across(ff[1])
    attn[2] = near(attn[2])
    ff[2] = flat(over(ff[2], two))
    adds = run_attn(1, *prepared)
    steps.next()
    attn[2] = across(attn[2])
    ff[2] = near(ff[2])
    head = over(head, two)
    prepared = run_prepare(2, run_ff(1, adds))
    steps.next()
    ff[2] = across(ff[2])
    head = over(head, [low]).reshape(-1, rows + 2 * images, half)
    adds = run_attn(2, *prepared)
    steps.next()
    teach = head[:, rows : rows + images].astype(F32) + head[:, rows + images :].astype(F32)
    head = head[:, :rows].reshape(width, half)
    adds = run_ff(2, adds)
    x = sum(v.astype(F32) for v in adds)

    teach = jnp.swapaxes(teach.reshape((2, -1, images, half)), 0, 1).reshape(-1, images, half)
    me = lax.axis_index("dp")
    source = jnp.sum(jnp.where(teacher_map == me, jnp.arange(teacher_map.shape[0], dtype=jnp.int32), 0))
    teach_log = lax.dynamic_index_in_dim(teach, jnp.bitwise_xor(source, me), 0, False)

    divisor = jnp.maximum(count, 1.0)[:, None]
    pooled = jnp.dot(member, x, precision=HIGH) / divisor
    pooled_normed = layer_norm(pooled, norms[-1]).astype(BF)
    logits = nn(pooled_normed, head)
    theirs = swap(logits, INNER)
    peak = jnp.maximum(jnp.max(logits, -1, keepdims=True), jnp.max(theirs, -1, keepdims=True))
    total = jnp.sum(jnp.exp(logits - peak), -1, keepdims=True) + jnp.sum(jnp.exp(theirs - peak), -1, keepdims=True)
    student_log = logits - peak - jnp.log(total)
    loss_local = jnp.sum(owned * jnp.exp(teach_log) * (teach_log - student_log))
    d_logits = (owned * (jnp.exp(student_log) - jnp.exp(teach_log)) / total_images).astype(BF)
    g_head = tn(pooled_normed, d_logits).astype(BF)
    d_pooled, g_final = norm_back(pooled, norms[-1], both(nt(d_logits, head)))
    d_x = lax.dot_general(member, d_pooled / divisor, (((0,), (0,)), ((), ())), precision=HIGH)

    steps = Steps()
    g, g_norms = {}, {}

    def near(name):
        own, near, across, both_ways = g[name]
        near = near.astype(F32) + steps.swap(both_ways, FIRST).astype(F32)
        g[name] = own, near.astype(BF), steps.swap(across, FIRST)

    def blocks_of(value):
        value = value.astype(BF).reshape((-1, rows, value.shape[-1]))
        return [value[i] for i in range(value.shape[0])]

    def near_last(name):
        own, near, received = g[name]
        value = own.astype(F32) + received.astype(F32) + steps.swap(near, SECOND).astype(F32)
        g[name] = blocks_of(value)

    def near_low(name):
        keep, send = g[name]
        g[name] = blocks_of(keep.astype(F32) + steps.swap(send, low).astype(F32))

    def far_first(*names):
        for bit in high[:0:-1]:
            half = len(g[names[0]]) // 2
            got = steps.swap(jnp.stack([v for name in names for v in g[name][half:]]), bit)
            for k, name in enumerate(names):
                g[name] = [
                    (g[name][i].astype(F32) + got[k * half + i].astype(F32)).astype(BF) for i in range(half)
                ]

    def far_last(*names):
        got = steps.swap(jnp.stack([g[name][1] for name in names]), high[0])
        for k, name in enumerate(names):
            g[name] = (g[name][0], got[k])

    def back_ff(l, back):
        back = [steps.tie(back[0])] + back[1:]
        d_x, *grad, own, g_above = ff_backward(back, middles[l], norms[2 * l + 1], ff[l], flag)
        g["ff", l] = grad
        if l < LAYERS - 1:
            g_norms[2 * l + 2] = g_above
        steps.add(own)
        return [d_x, middles[l], norms[2 * l + 1], own, swap(own, INNER)]

    def back_attn(l, back):
        back = [steps.tie(back[0])] + back[1:]
        d_mid, *grad, own, g_above, row = attn_backward(
            back, xs[l], norms[2 * l], others[l], segq, segk, base, away, mixes[l], attn[l], flag
        )
        g["attn", l] = grad
        g_norms[2 * l + 1] = g_above
        steps.add(own)
        row = row[:8]
        rows_in = [steps.add(swap(row, OUTER)), steps.add(swap(row, DIAGONAL))]
        return [d_mid, xs[l], norms[2 * l], own, swap(own, INNER), *rows_in, real]

    g["head"] = (g_head[:mid], g_head[mid:])
    near_low("head")
    back = back_ff(2, [d_x])
    steps.next()
    near(("ff", 2))
    far_first("head")
    back = back_attn(2, back)
    steps.next()
    near(("attn", 2))
    near_last(("ff", 2))
    far_last("head")
    back = back_ff(1, back)
    steps.next()
    near(("ff", 1))
    near_last(("attn", 2))
    far_first(("ff", 2))
    back = back_attn(1, back)
    steps.next()
    near(("attn", 1))
    near_last(("ff", 1))
    far_first(("attn", 2))
    far_last(("ff", 2))
    back = back_ff(0, back)
    steps.next()
    near(("ff", 0))
    near_last(("attn", 1))
    far_first(("ff", 1))
    far_last(("attn", 2))
    back = back_attn(0, back)
    steps.next()
    d_x0, g_norms[0] = input_gradient([steps.tie(back[0])] + back[1:])
    theirs = steps.swap(of_inner(d_x0, inner), OUTER)
    near(("attn", 0))
    near_last(("ff", 0))
    far_first(("attn", 1))
    far_last(("ff", 1))
    theirs = halves(theirs, swap(theirs, INNER))
    g_patch = tn(jnp.concatenate([d_x0, theirs], 0), jnp.concatenate(pix, 0)).astype(BF)
    steps.add(g_patch)
    g["patch"] = (g_patch[:mid], g_patch[mid:])
    token = g_norms[0]
    *done, square_two = finish(2, [], g["attn", 2], g["ff", 2], token)
    steps.next()
    near_low("patch")
    near_last(("attn", 0))
    far_first(("ff", 0))
    far_last(("attn", 1))
    g_head = steps.tie(g["head"][0]).astype(F32) + g["head"][1].astype(F32)
    g_head = g_head + steps.swap(g_head, OUTER)
    g_norm = steps.tie(jnp.concatenate([g_norms[i] for i in range(6)] + [g_final], 0))
    g_norm = 0.5 * (g_norm + swap(g_norm, INNER))
    *done, square_one = finish(1, done, g["attn", 1], g["ff", 1], g_patch)
    steps.next()
    far_first(("attn", 0), "patch")
    far_last(("ff", 0))
    g_norm = g_norm + steps.swap(g_norm, OUTER)
    g_norm = jnp.moveaxis(g_norm.reshape(14, 2, -1, rows), 0, 2)
    g_norm = g_norm[0] + steps.swap(g_norm[1], low)
    g_head = halves(g_head, swap(g_head, INNER))
    steps.next()
    far_last(("attn", 0), "patch")
    g_norm = g_norm.reshape((2,) * len(high) + (14, rows))
    for bit in high[::-1]:
        g_norm = g_norm[0] + steps.swap(g_norm[1], bit)
    g_norm = g_norm.reshape(7, 2, rows)
    *done, square_zero = finish(0, done, g["attn", 0], g["ff", 0], g_patch)
    g_patch = g["patch"][0].astype(F32) + g["patch"][1].astype(F32)

    grads = (*done, g_patch, g_head, g_norm)
    first_model = (lax.axis_index("mp") == 0).astype(F32)
    squares = (square_two + square_one + square_zero)[0, 0] + jnp.sum(g_patch * g_patch) + first_model * (
        jnp.sum(g_head * g_head) + jnp.sum(g_norm * g_norm)
    )
    sums = jnp.stack([squares, loss_local * (outer >= 0)])
    sums = sums + swap(sums, INNER)
    sums = sums + swap(sums, OUTER)
    if len(high) == 2:
        (axis, a), (_, b) = high
        sums = sums + swap(sums, low)
        sums = (sums + swap(sums, (axis, a))) + (swap(sums, (axis, b)) + swap(sums, (axis, a | b)))
    else:
        for bit in bits:
            sums = sums + swap(sums, bit)
    loss = sums[1]
    grad_norm = jnp.sqrt(sums[0])
    clip = jnp.minimum(1.0, CLIP / grad_norm)

    def turned(values):
        return (*values[:3], values[3].swapaxes(1, 2), values[4].T, *values[5:])

    masters, firsts, seconds = turned(masters), turned(firsts), turned(seconds)
    outs = adam_all(clip, masters, grads, firsts, seconds)
    return (loss, grad_norm) + turned(outs[:7]) + turned(outs[7:14]) + turned(outs[14:])


def solution(mesh):
    weights = (
        P(None, None, "dp", "mp"),
        P(None, "mp", "dp"),
        P(None, "dp", "mp"),
        P(None, "mp", "dp"),
        P("mp", "dp"),
        P("dp", None),
        P(None, None, "dp"),
    )
    placed = (P("dp", "mp"), P("dp", None), P("dp"), P("dp", None), P()) + weights * 3
    return jax.shard_map(
        body, mesh=mesh, in_specs=placed, out_specs=(P(), P()) + weights * 3, check_vma=False
    )
```

```python
import functools

import jax
import jax.numpy as jnp
from jax import lax
from jax.experimental import pallas as pl
from jax.experimental.pallas import tpu as pltpu
from jax.sharding import PartitionSpec as P

HEAD_DIM = 64
LAYERS = 3
STEP = 10
MOST = 576
EXTRA = 16
NEVER = -1e30
FF_BLOCK = 256

EPSILON = 1e-06
MASKED = -30000.0
CLIP = 0.005
BETA_ONE = 0.9
BETA_TWO = 0.999
ADAM_EPS = 1e-08
RATES = (0.02, 0.06, 0.02, 0.02, 0.02, 0.02, 0.5)
DECAYS = (0.05, 0.05, 0.05, 0.05, 0.05, 0.05, 0.0)
SQRT_HALF = 0.7071067811865476
INV_ROOT = 0.3989422804014327
HIGH = lax.Precision.HIGHEST
BF = jnp.bfloat16
F32 = jnp.float32

AXES = ("dp", "mp")
INNER = ("mp", 1)
OUTER = ("mp", 2)
LOW = ("dp", 1)
FIRST = (LOW, OUTER)
SECOND = (OUTER, LOW)


def swap(value, bit):
    n_dp, n_mp = (lax.axis_size(axis) for axis in AXES)
    pairs = []
    for dp in range(n_dp):
        for mp in range(n_mp):
            axis, mask = bit if isinstance(bit[0], str) else bit[mp % 2]
            to = (dp ^ mask) * n_mp + mp if axis == "dp" else dp * n_mp + (mp ^ mask)
            pairs.append((dp * n_mp + mp, to))
    return lax.ppermute(value, AXES, pairs)


class Steps:
    def __init__(self):
        self.before = []
        self.made = []

    def next(self):
        self.before, self.made = self.made, []

    def tie(self, value):
        if not self.before:
            return value
        return lax.optimization_barrier((value, *self.before))[0]

    def add(self, value):
        self.made.append(value)
        return value

    def swap(self, value, bit):
        return self.add(swap(self.tie(value), bit))


def dp_bits():
    size = lax.axis_size("dp")
    bits = []
    mask = 1
    while mask < size:
        bits.append(("dp", mask))
        mask *= 2
    return bits


def both(part):
    return part + swap(part.astype(BF), INNER).astype(F32)


def dot(left, right, contract):
    return lax.dot_general(left, right, ((contract[0:1], contract[1:2]), ((), ())), preferred_element_type=F32)


def nn(left, right):
    return dot(left, right, (1, 0))


def nt(left, right):
    return dot(left, right, (1, 1))


def tn(left, right):
    return dot(left, right, (0, 0))


def norm_stats(value):
    centred = value - jnp.mean(value, -1, keepdims=True)
    variance = jnp.mean(centred * centred, -1, keepdims=True)
    rstd = lax.rsqrt(variance + EPSILON)
    return centred * rstd, rstd


def layer_norm(value, norm):
    return norm_stats(value)[0] * norm[0:1] + norm[1:2]


def norm_back(value, norm, d_out):
    hat, rstd = norm_stats(value)
    d_hat = d_out * norm[0:1]
    d_value = rstd * (
        d_hat - jnp.mean(d_hat, -1, keepdims=True) - hat * jnp.mean(d_hat * hat, -1, keepdims=True)
    )
    return d_value, jnp.concatenate([jnp.sum(d_out * hat, 0, keepdims=True), jnp.sum(d_out, 0, keepdims=True)], 0)


def load_weight(w, flag, own, near, across, both_ways):
    outer = pl.program_id(0) % 2
    rows = w.shape[0] // 2

    @pl.when(outer == 0)
    def _():
        w[:rows] = own[...]

    @pl.when(outer == 1)
    def _():
        w[rows:] = both_ways[...]

    @pl.when((outer == 0) & (flag[0] == 0))
    def _():
        w[rows:] = across[...]

    @pl.when((outer == 0) & (flag[0] == 1))
    def _():
        w[rows:] = near[...]

    @pl.when((outer == 1) & (flag[0] == 0))
    def _():
        w[:rows] = near[...]

    @pl.when((outer == 1) & (flag[0] == 1))
    def _():
        w[:rows] = across[...]


def store_grad(parts, flag, own, near, across, both_ways):
    outer = pl.program_id(0) % 2

    def put(target, top):
        at = 0
        for part in parts:
            rows = part.shape[0] // 2
            value = part[:rows] if top else part[rows:]
            target[:, at : at + part.shape[1]] = value.astype(BF)
            at += part.shape[1]

    @pl.when(outer == 0)
    def _():
        put(own, True)

    @pl.when(outer == 1)
    def _():
        put(both_ways, False)

    @pl.when((outer == 0) & (flag[0] == 0))
    def _():
        put(across, False)

    @pl.when((outer == 0) & (flag[0] == 1))
    def _():
        put(near, False)

    @pl.when((outer == 1) & (flag[0] == 0))
    def _():
        put(near, True)

    @pl.when((outer == 1) & (flag[0] == 1))
    def _():
        put(across, True)


def quarter_specs(weight, columns):
    steps = 2 * (weight.shape[1] // columns)
    return steps, [pl.BlockSpec((weight.shape[0], columns), lambda i: (0, i // 2))] * 4


def full(value):
    return pl.BlockSpec(value.shape, lambda i: (0,) * len(value.shape))


def spec_of(shape):
    return pl.BlockSpec(shape, lambda i: (0,) * len(shape))


FLAG = pl.BlockSpec(memory_space=pltpu.SMEM)
NO_COST = pl.CostEstimate(flops=10**6, bytes_accessed=10**4, transcendentals=0)


def params():
    return pltpu.CompilerParams(dimension_semantics=("arbitrary",), vmem_limit_bytes=56 * 1024 * 1024)


def masked_probs(scaled_query, key, keep, base, away):
    scores = jnp.where(keep, nt(scaled_query, key), base)
    top = jnp.maximum(jnp.max(scores, -1, keepdims=True), MASKED)
    weight = jnp.exp(scores - top)
    far = jnp.exp(MASKED - top)
    part = 1.0 / (jnp.sum(weight, -1, keepdims=True) + away * far)
    return weight * part, far * part


def prepare_kernel(count, *refs):
    adds = refs[:count]
    norm, real, x_ref, normed_ref, sum_ref = refs[count:]
    x = adds[0][...]
    for other in adds[1:]:
        x = x + other[...].astype(F32)
    x_ref[...] = x
    normed = layer_norm(x, norm[...]).astype(BF)
    normed_ref[...] = normed
    sum_ref[...] = jnp.sum(normed.astype(F32) * real[...], 0, keepdims=True)


def prepare(adds, norm, real):
    tokens, width = adds[0].shape
    return pl.pallas_call(
        functools.partial(prepare_kernel, len(adds)),
        grid=(1,),
        in_specs=[full(v) for v in adds] + [full(norm), full(real)],
        out_specs=[spec_of((tokens, width)), spec_of((tokens, width)), spec_of((1, width))],
        out_shape=[
            jax.ShapeDtypeStruct((tokens, width), F32),
            jax.ShapeDtypeStruct((tokens, width), BF),
            jax.ShapeDtypeStruct((1, width), F32),
        ],
        compiler_params=params(),
        cost_estimate=NO_COST,
        name="prepare",
    )(*adds, norm, real)


def below(rows, count=EXTRA):
    return jnp.concatenate([rows, jnp.zeros((count - rows.shape[0], rows.shape[1]), rows.dtype)], 0)


def attn_fwd_kernel(flag, away, normed, others, segq, segk, base, *refs):
    *weight, mix_ref, part_ref, normed_all, w, acc = refs
    step = pl.program_id(0)
    tokens = normed.shape[0]

    @pl.when(step == 0)
    def _():
        normed_all[:tokens] = normed[...]
        normed_all[tokens:] = below(others[...]).astype(BF)
        acc[...] = jnp.zeros_like(acc)

    load_weight(w, flag, *weight)
    wide = nn(normed_all[...], w[...])
    mixed = wide.astype(BF)
    c = HEAD_DIM
    width = w.shape[1] // 4
    keep = segq[...] == segk[...]
    outs = []
    for at in range(0, width, c):
        query = mixed[:tokens, at : at + c] * c ** (-0.5)
        key = mixed[:tokens, width + at : width + at + c]
        here = slice(2 * width + at, 2 * width + at + c)
        probs, far = masked_probs(query, key, keep, base[...], away[0])
        out = nn(probs.astype(BF), mixed[:tokens, here]) + far.astype(BF).astype(F32) * wide[tokens : tokens + 1, here]
        outs.append(out.astype(BF))
    out = jnp.concatenate(outs, 1)
    mix_ref[0, :, : 3 * width] = mixed[:, : 3 * width]
    mix_ref[0, :tokens, 3 * width :] = out
    mix_ref[0, tokens:, 3 * width :] = jnp.zeros((EXTRA, width), BF)
    acc[...] += nt(jnp.concatenate([jnp.zeros_like(outs[0]), out], 1), w[:, 3 * width - c :])

    @pl.when(step == pl.num_programs(0) - 1)
    def _():
        part_ref[...] = acc[...].astype(BF)


def attn_forward(normed, others, segq, segk, base, away, pieces, flag):
    tokens, width = normed.shape
    columns = pieces[0].shape[1]
    steps, quarters = quarter_specs(pieces[0], columns)
    values = (normed, others, segq, segk, base)
    return pl.pallas_call(
        attn_fwd_kernel,
        grid=(steps,),
        in_specs=[FLAG, FLAG] + [full(v) for v in values] + quarters,
        out_specs=[
            pl.BlockSpec((1, tokens + EXTRA, columns), lambda i: (i, 0, 0)),
            spec_of((tokens, width)),
        ],
        out_shape=[
            jax.ShapeDtypeStruct((steps, tokens + EXTRA, columns), BF),
            jax.ShapeDtypeStruct((tokens, width), BF),
        ],
        scratch_shapes=[
            pltpu.VMEM((tokens + EXTRA, width), BF),
            pltpu.VMEM((width, columns), BF),
            pltpu.VMEM((tokens, width), F32),
        ],
        compiler_params=params(),
        cost_estimate=NO_COST,
        name="attn_forward",
    )(flag, away, *values, *pieces)


def ff_fwd_kernel(count, *refs):
    flag = refs[0]
    adds = refs[1 : count + 1]
    norm, *weight, x_ref, part_ref, normed, w, acc = refs[count + 1 :]
    step = pl.program_id(0)

    @pl.when(step == 0)
    def _():
        x = adds[0][...]
        for other in adds[1:]:
            x = x + other[...].astype(F32)
        x_ref[...] = x
        normed[...] = layer_norm(x, norm[...]).astype(BF)
        acc[...] = jnp.zeros_like(acc)

    load_weight(w, flag, *weight)
    columns = w.shape[1] // 2
    up = nn(normed[...], w[:, :columns])
    active = (0.5 * up * (1.0 + lax.erf(up * SQRT_HALF))).astype(BF)
    acc[...] += nt(active, w[:, columns:])

    @pl.when(step == pl.num_programs(0) - 1)
    def _():
        part_ref[...] = acc[...].astype(BF)


def ff_forward(adds, norm, pieces, flag):
    tokens, width = adds[0].shape
    columns = FF_BLOCK * 2
    steps, quarters = quarter_specs(pieces[0], columns)
    return pl.pallas_call(
        functools.partial(ff_fwd_kernel, len(adds)),
        grid=(steps,),
        in_specs=[FLAG] + [full(v) for v in adds] + [full(norm)] + quarters,
        out_specs=[spec_of((tokens, width)), spec_of((tokens, width))],
        out_shape=[
            jax.ShapeDtypeStruct((tokens, width), F32),
            jax.ShapeDtypeStruct((tokens, width), BF),
        ],
        scratch_shapes=[
            pltpu.VMEM((tokens, width), BF),
            pltpu.VMEM((width, columns), BF),
            pltpu.VMEM((tokens, width), F32),
        ],
        compiler_params=params(),
        cost_estimate=NO_COST,
        name="ff_forward",
    )(flag, *adds, norm, *pieces)


def past_norm(own, other, *rest):
    total = own[...].astype(F32) + other[...].astype(F32)
    if rest:
        one, two, real = rest
        total = total + real[...] * (one[:1] + two[:1])
    return total


def back_prologue(back, d_ref, g_ref):
    d_base = back[0][...]
    if len(back) == 1:
        d_ref[...] = d_base
        return d_base
    d_value, g_ref[...] = norm_back(back[1][...], back[2][...], past_norm(*back[3:]))
    d_all = d_base + d_value
    d_ref[...] = d_all
    return d_all


def ff_back_kernel(count, *refs):
    flag = refs[0]
    back = refs[1 : count + 1]
    value, norm = refs[count + 1 : count + 3]
    weight, d_ref, grad = refs[count + 3 : count + 7], refs[count + 7], refs[count + 8 : count + 12]
    part_ref, g_ref, normed, normed_t, dz, dz_t, w, acc = refs[count + 12 :]
    step = pl.program_id(0)

    @pl.when(step == 0)
    def _():
        d_all = back_prologue(back, d_ref, g_ref)
        dz[...] = d_all.astype(BF)
        dz_t[...] = d_all.T.astype(BF)
        here = layer_norm(value[...], norm[...])
        normed[...] = here.astype(BF)
        normed_t[...] = here.T.astype(BF)
        acc[...] = jnp.zeros_like(acc)

    load_weight(w, flag, *weight)
    columns = w.shape[1] // 2
    up = nn(normed[...], w[:, :columns])
    phi = 0.5 * (1.0 + lax.erf(up * SQRT_HALF))
    active = (up * phi).astype(BF)
    slope = phi + up * jnp.exp(-0.5 * up * up) * INV_ROOT
    d_up = (nn(dz[...], w[:, columns:]) * slope).astype(BF)
    acc[...] += nt(d_up, w[:, :columns])
    store_grad([nn(normed_t[...], d_up), nn(dz_t[...], active)], flag, *grad)

    @pl.when(step == pl.num_programs(0) - 1)
    def _():
        part_ref[...] = acc[...].astype(BF)


def back_out(tokens, width, pieces, quarters):
    specs = [spec_of((tokens, width))] + quarters + [spec_of((tokens, width)), spec_of((2, width))]
    shapes = [
        jax.ShapeDtypeStruct((tokens, width), F32),
        *[jax.ShapeDtypeStruct(piece.shape, BF) for piece in pieces],
        jax.ShapeDtypeStruct((tokens, width), BF),
        jax.ShapeDtypeStruct((2, width), F32),
    ]
    return specs, shapes


def ff_backward(back, value, norm, pieces, flag):
    tokens, width = value.shape
    columns = FF_BLOCK * 2
    steps, quarters = quarter_specs(pieces[0], columns)
    specs, shapes = back_out(tokens, width, pieces, quarters)
    return pl.pallas_call(
        functools.partial(ff_back_kernel, len(back)),
        grid=(steps,),
        in_specs=[FLAG] + [full(v) for v in back] + [full(value), full(norm)] + quarters,
        out_specs=specs,
        out_shape=shapes,
        scratch_shapes=[
            pltpu.VMEM((tokens, width), BF),
            pltpu.VMEM((width, tokens), BF),
            pltpu.VMEM((tokens, width), BF),
            pltpu.VMEM((width, tokens), BF),
            pltpu.VMEM((width, columns), BF),
            pltpu.VMEM((tokens, width), F32),
        ],
        compiler_params=params(),
        cost_estimate=NO_COST,
        name="ff_backward",
    )(flag, *back, value, norm, *pieces)


def attn_back_kernel(count, *refs):
    flag, away = refs[:2]
    back = refs[2 : count + 2]
    value, norm, others, segq, segk, base, mix_ref = refs[count + 2 : count + 9]
    weight, d_ref, grad = refs[count + 9 : count + 13], refs[count + 13], refs[count + 14 : count + 18]
    part_ref, g_ref, row_ref, normed_t, dy, dy_t, w, acc, d_mix = refs[count + 18 :]
    step = pl.program_id(0)
    tokens = dy.shape[0]

    @pl.when(step == 0)
    def _():
        d_all = back_prologue(back, d_ref, g_ref)
        dy[...] = d_all.astype(BF)
        dy_t[...] = d_all.T.astype(BF)
        here = jnp.concatenate([layer_norm(value[...], norm[...]), below(others[...])], 0)
        normed_t[...] = here.T.astype(BF)
        d_mix[...] = jnp.zeros_like(d_mix)
        acc[...] = jnp.zeros_like(acc)

    load_weight(w, flag, *weight)
    c = HEAD_DIM
    scale = HEAD_DIM ** (-0.5)
    width = w.shape[1] // 4
    d_outs = nn(dy[...], w[:, 3 * width - c :])[:, c:].astype(BF)
    keep = segq[...] == segk[...]
    for at in range(0, width, c):
        query = mix_ref[0, :tokens, at : at + c] * scale
        key = mix_ref[0, :tokens, width + at : width + at + c]
        here = slice(2 * width + at, 2 * width + at + c)
        val = mix_ref[0, :tokens, here]
        val_sum = mix_ref[0, tokens:, here][:1].astype(F32)
        d_out = d_outs[:, at : at + c]
        d_wide = d_out.astype(F32)
        probs, far = masked_probs(query, key, keep, base[...], away[0])
        d_probs = nt(d_out, val)
        delta = jnp.sum(probs * d_probs, -1, keepdims=True) + far * jnp.sum(d_wide * val_sum, -1, keepdims=True)
        d_scores = jnp.where(keep, probs * (d_probs - delta), 0.0).astype(BF)
        d_mix[:tokens, at : at + c] = (nn(d_scores, key) * scale).astype(BF)
        d_mix[:tokens, width + at : width + at + c] = nn(query.T, d_scores).T.astype(BF)
        d_mix[:tokens, here] = nn(d_out.T, probs.astype(BF)).T.astype(BF)
        row = jnp.sum(far.astype(BF).astype(F32) * d_wide, 0, keepdims=True)
        d_mix[tokens:, here] = below(row).astype(BF)
    acc[...] += nt(d_mix[...], w[...])
    wide = 4 * width - (3 * width - c)
    out = jnp.concatenate([jnp.zeros((tokens, c), BF), mix_ref[0, :tokens, 3 * width :]], 1)
    left = nn(normed_t[...], d_mix[:, : 4 * width - wide])
    right = nn(normed_t[...], d_mix[:, 4 * width - wide :]) + nn(dy_t[...], out)
    store_grad([left, right], flag, *grad)

    @pl.when(step == pl.num_programs(0) - 1)
    def _():
        part_ref[...] = acc[:tokens].astype(BF)
        row_ref[...] = acc[tokens:]


def attn_backward(back, value, norm, others, segq, segk, base, away, mix, pieces, flag):
    tokens, width = value.shape
    columns = pieces[0].shape[1]
    steps, quarters = quarter_specs(pieces[0], columns)
    specs, shapes = back_out(tokens, width, pieces, quarters)
    values = (*back, value, norm, others, segq, segk, base)
    return pl.pallas_call(
        functools.partial(attn_back_kernel, len(back)),
        grid=(steps,),
        in_specs=[FLAG, FLAG]
        + [full(v) for v in values]
        + [pl.BlockSpec((1, tokens + EXTRA, columns), lambda i: (i, 0, 0))]
        + quarters,
        out_specs=specs + [spec_of((EXTRA, width))],
        out_shape=shapes + [jax.ShapeDtypeStruct((EXTRA, width), F32)],
        scratch_shapes=[
            pltpu.VMEM((width, tokens + EXTRA), BF),
            pltpu.VMEM((tokens, width), BF),
            pltpu.VMEM((width, tokens), BF),
            pltpu.VMEM((width, columns), BF),
            pltpu.VMEM((tokens + EXTRA, width), F32),
            pltpu.VMEM((tokens + EXTRA, columns), BF),
        ],
        compiler_params=params(),
        cost_estimate=NO_COST,
        name="attn_backward",
    )(flag, away, *values, mix, *pieces)


def last_kernel(base, value, norm, *refs):
    *parts, d_ref, g_ref = refs
    d_value, g_ref[...] = norm_back(value[...], norm[...], past_norm(*parts))
    d_ref[...] = (base[...] + d_value).astype(BF)


def input_gradient(back):
    tokens, width = back[0].shape
    return pl.pallas_call(
        last_kernel,
        grid=(1,),
        in_specs=[full(v) for v in back],
        out_specs=[spec_of((tokens, width)), spec_of((2, width))],
        out_shape=[
            jax.ShapeDtypeStruct((tokens, width), BF),
            jax.ShapeDtypeStruct((2, width), F32),
        ],
        compiler_params=params(),
        cost_estimate=NO_COST,
        name="input_gradient",
    )(*back)


def finish_kernel(count, *refs):
    a_keep, a_got, f_keep, f_got, into, out, up, down, square = refs[1 + count :]
    g = a_keep[...].astype(F32) + a_got[...].astype(F32)
    total = jnp.sum(g * g, 0, keepdims=True).sum(1, keepdims=True)
    width = g.shape[1] // 4
    for j in range(3):
        into[j] = g[:, j * width : (j + 1) * width]
    out[...] = g[:, 3 * width :].T
    g = f_keep[...].astype(F32) + f_got[...].astype(F32)
    total = total + jnp.sum(g * g, 0, keepdims=True).sum(1, keepdims=True)
    for i in range(g.shape[1] // (2 * FF_BLOCK)):
        here = slice(i * FF_BLOCK, (i + 1) * FF_BLOCK)
        up[:, here] = g[:, 2 * i * FF_BLOCK : (2 * i + 1) * FF_BLOCK]
        down[:, here] = g[:, (2 * i + 1) * FF_BLOCK : (2 * i + 2) * FF_BLOCK]
    square[...] = total


def finish(l, before, a_pair, f_pair, token):
    rows, width = a_pair[0].shape
    hidden = f_pair[0].shape[1] // 2
    values = (*a_pair, *f_pair)
    outs = [(3, rows, width // 4), (width // 4, rows), (rows, hidden), (rows, hidden)]

    def layer_spec(o):
        return pl.BlockSpec((None, *o), lambda i: (l,) + (0,) * len(o))

    anywhere = pl.BlockSpec(memory_space=pl.ANY)
    return pl.pallas_call(
        functools.partial(finish_kernel, len(before)),
        grid=(1,),
        in_specs=[anywhere] * (1 + len(before)) + [full(v) for v in values],
        out_specs=[layer_spec(o) for o in outs] + [spec_of((1, 1))],
        out_shape=[jax.ShapeDtypeStruct((LAYERS, *o), F32) for o in outs] + [jax.ShapeDtypeStruct((1, 1), F32)],
        input_output_aliases={1 + i: i for i in range(len(before))},
        compiler_params=params(),
        cost_estimate=NO_COST,
        name="finish",
    )(token, *before, *values)


def adam_kernel(clip_ref, *refs):
    clip = clip_ref[0]
    for kind in range(7):
        weight, grad, first, second = (refs[i * 7 + kind] for i in range(4))
        new_first, new_second, new_weight = (refs[28 + i * 7 + kind] for i in range(3))

        def update():
            g = grad[...] * clip
            new_first[...], new_second[...], new_weight[...] = adam(
                weight[...], g, first[...], second[...], RATES[kind], DECAYS[kind]
            )

        if kind < 4:
            update()
        else:
            pl.when(pl.program_id(0) == 0)(update)


def adam_all(clip, masters, grads, firsts, seconds):
    def spec(value, kind):
        if kind < 4:
            rest = value.shape[1:]
            return pl.BlockSpec((None, *rest), lambda i: (i,) + (0,) * len(rest))
        return full(value)

    specs = [spec(value, kind) for kind, value in enumerate(masters)]
    outs = pl.pallas_call(
        adam_kernel,
        grid=(LAYERS,),
        in_specs=[FLAG] + specs * 4,
        out_specs=specs * 3,
        out_shape=[jax.ShapeDtypeStruct(v.shape, F32) for v in masters] * 3,
        compiler_params=params(),
        name="adam",
    )(clip.reshape(1), *masters, *grads, *firsts, *seconds)
    return tuple(outs)


def adam(weight, grad, first, second, rate, decay):
    first = BETA_ONE * first + (1.0 - BETA_ONE) * grad
    second = BETA_TWO * second + (1.0 - BETA_TWO) * grad * grad
    update = first / (1.0 - BETA_ONE**STEP) / (jnp.sqrt(second / (1.0 - BETA_TWO**STEP)) + ADAM_EPS)
    return (first, second, weight - rate * (update + decay * weight))


def body(pixels, lengths, valid_mask, teacher_logits, teacher_map, *state):
    masters, firsts, seconds = state[:7], state[7:14], state[14:]
    attend_in, attend_out, hidden_up, hidden_down, patch_embed, class_head, norm_params = masters
    bits = dp_bits()
    low, high = bits[0], bits[1:]
    steps = Steps()
    rows = patch_embed.shape[1]
    inner = lax.axis_index("mp") % 2
    outer = lax.axis_index("mp") // 2
    images = lengths.shape[1]
    tokens = pixels.shape[0]
    total_images = images * lax.axis_size("dp")

    hidden = hidden_up.shape[2]
    width = attend_out.shape[2] * lax.axis_size("dp")

    def attn_unit(l):
        return jnp.concatenate([attend_in[l, j].astype(BF) for j in range(3)] + [attend_out[l].astype(BF).T], 1)

    def ff_unit(l):
        up = hidden_up[l].astype(BF).reshape(rows, -1, 1, FF_BLOCK)
        down = hidden_down[l].T.astype(BF).reshape(rows, -1, 1, FF_BLOCK)
        return jnp.concatenate([up, down], 2).reshape(rows, -1)

    half = class_head.shape[1] // 2
    head_unit = lax.dynamic_slice_in_dim(class_head.astype(BF), inner * half, half, 1)
    teach = jax.nn.log_softmax(teacher_logits, -1)
    teach = lax.dynamic_slice_in_dim(teach, inner * half, half, 1)
    upper = lax.optimization_barrier(teach.astype(BF))
    head_unit = jnp.concatenate([head_unit, upper, (teach - upper.astype(F32)).astype(BF)], 0)

    flag = inner.reshape(1)

    def over(unit, bits):
        for bit in bits:
            unit = jnp.stack([unit, steps.swap(unit, bit)])
        return unit

    def over_high(unit):
        if len(high) != 2:
            return over(unit, high)
        (axis, a), (_, b) = high
        return jnp.stack([unit] + [steps.swap(unit, (axis, mask)) for mask in (a, b, a | b)])

    def near(own):
        return [own, steps.swap(own, SECOND), steps.swap(own, FIRST)]

    def across(held):
        return held + [steps.swap(held[1], FIRST)]

    def far(unit):
        unit = over_high(unit)
        return unit.reshape(-1, unit.shape[-1])

    row = lengths[0]
    ends = jnp.cumsum(row)
    longest = jnp.argmax(row)
    start = ends[longest] - row[longest]
    place = jnp.arange(MOST, dtype=jnp.int32)

    def mine(value, which):
        twice = jnp.concatenate([value, value], 0)
        return lax.dynamic_slice_in_dim(twice, start + MOST * which, MOST, 0)

    pix = [mine(pixels, outer), mine(pixels, 1 - outer)]
    held = jnp.where(outer == 0, MOST, tokens - MOST)
    position = (start + MOST * outer + place) % tokens
    segment = jnp.sum((position[:, None] >= ends[None, :]).astype(jnp.int32), 1)
    valid = jnp.where(place < held, mine(valid_mask, outer), 0) > 0
    segq = segment[:, None]
    segk = jnp.where(valid, segment, -1)[None, :]
    real = (place < held).astype(F32)[:, None]
    base = jnp.where(place < held, MASKED, NEVER)[None, :]
    away = (tokens - held).astype(F32).reshape(1)
    image_ids = jnp.arange(images, dtype=jnp.int32)
    member = ((segment[None, :] == image_ids[:, None]) & valid[None, :]).astype(F32)
    owned = ((image_ids == longest) == (outer == 0)).astype(F32)[:, None]
    count = jnp.sum(member, 1)

    mid = width // 2

    def of_inner(value, which):
        return jnp.where(which == 0, value[..., :mid], value[..., mid:])

    def halves(own, other):
        return jnp.where(inner == 0, jnp.concatenate([own, other], 1), jnp.concatenate([other, own], 1))

    dp_order = high + [low]
    attn = [attn_unit(l) for l in range(LAYERS)]
    ff = [ff_unit(l) for l in range(LAYERS)]

    one, two = high[:1], high[1:]

    def together(*units):
        got = steps.swap(jnp.stack(units), high[0])
        return [jnp.stack([unit, got[i]]) for i, unit in enumerate(units)]

    def flat(unit):
        return unit.reshape(-1, unit.shape[-1])

    xs, middles, mixes, others = [], [], [], []

    def run_prepare(l, adds):
        x, normed, total = prepare(adds, norms[2 * l], real)
        xs.append(x)
        others.append(steps.swap(total, OUTER))
        return x, steps.add(normed)

    def run_attn(l, x, normed):
        mix, own = attn_forward(steps.tie(normed), others[l], segq, segk, base, away, attn[l], flag)
        mixes.append(mix)
        steps.add(own)
        return [x, own, swap(own, INNER)]

    def run_ff(l, adds):
        middle, own = ff_forward([steps.tie(adds[0])] + adds[1:], norms[2 * l + 1], ff[l], flag)
        middles.append(middle)
        steps.add(own)
        return [middle, own, swap(own, INNER)]

    for unit in attn + ff + [head_unit]:
        steps.add(unit)
    pixel_count = patch_embed.shape[0]
    patch = jnp.concatenate([patch_embed.astype(BF), norm_params.astype(BF).reshape(-1, rows)], 0).T
    patch = far(patch)
    attn[0] = over(attn[0], one)
    attn[1], attn[2] = together(attn[1], attn[2])
    steps.next()
    attn[0] = flat(over(attn[0], two))
    ff[0] = over(ff[0], one)
    head = over(head_unit, one)
    patch = over(patch, [low]).reshape(width, -1)
    steps.next()
    ff[0] = flat(over(ff[0], two))
    ff[1], ff[2] = together(ff[1], ff[2])
    attn[0] = near(attn[0])
    patch = steps.tie(patch)
    norms = patch[:, pixel_count:].T.astype(F32).reshape(7, 2, width)
    part = nt(jnp.concatenate(pix, 0), patch[:, :pixel_count]).astype(BF)
    part = of_inner(part, inner).astype(F32) + swap(of_inner(part, 1 - inner), INNER).astype(F32)
    part, theirs = part[:MOST], steps.swap(part[MOST:].astype(BF), OUTER)
    steps.next()
    part = steps.tie(part) + theirs.astype(F32)
    attn[0] = across(attn[0])
    ff[0] = near(ff[0])
    attn[1] = flat(over(attn[1], two))
    prepared = run_prepare(0, [halves(part, swap(part, INNER))])
    steps.next()
    ff[0] = across(ff[0])
    attn[1] = near(attn[1])
    ff[1] = flat(over(ff[1], two))
    adds = run_attn(0, *prepared)
    steps.next()
    attn[1] = across(attn[1])
    ff[1] = near(ff[1])
    attn[2] = flat(over(attn[2], two))
    prepared = run_prepare(1, run_ff(0, adds))
    steps.next()
    ff[1] = across(ff[1])
    attn[2] = near(attn[2])
    ff[2] = flat(over(ff[2], two))
    adds = run_attn(1, *prepared)
    steps.next()
    attn[2] = across(attn[2])
    ff[2] = near(ff[2])
    head = over(head, two)
    prepared = run_prepare(2, run_ff(1, adds))
    steps.next()
    ff[2] = across(ff[2])
    head = over(head, [low]).reshape(-1, rows + 2 * images, half)
    adds = run_attn(2, *prepared)
    steps.next()
    teach = head[:, rows : rows + images].astype(F32) + head[:, rows + images :].astype(F32)
    head = head[:, :rows].reshape(width, half)
    adds = run_ff(2, adds)
    x = sum(v.astype(F32) for v in adds)

    teach = jnp.swapaxes(teach.reshape((2, -1, images, half)), 0, 1).reshape(-1, images, half)
    me = lax.axis_index("dp")
    source = jnp.sum(jnp.where(teacher_map == me, jnp.arange(teacher_map.shape[0], dtype=jnp.int32), 0))
    teach_log = lax.dynamic_index_in_dim(teach, jnp.bitwise_xor(source, me), 0, False)

    divisor = jnp.maximum(count, 1.0)[:, None]
    pooled = jnp.dot(member, x, precision=HIGH) / divisor
    pooled_normed = layer_norm(pooled, norms[-1]).astype(BF)
    logits = nn(pooled_normed, head)
    theirs = swap(logits, INNER)
    peak = jnp.maximum(jnp.max(logits, -1, keepdims=True), jnp.max(theirs, -1, keepdims=True))
    total = jnp.sum(jnp.exp(logits - peak), -1, keepdims=True) + jnp.sum(jnp.exp(theirs - peak), -1, keepdims=True)
    student_log = logits - peak - jnp.log(total)
    loss_local = jnp.sum(owned * jnp.exp(teach_log) * (teach_log - student_log))
    d_logits = (owned * (jnp.exp(student_log) - jnp.exp(teach_log)) / total_images).astype(BF)
    g_head = tn(pooled_normed, d_logits).astype(BF)
    d_pooled, g_final = norm_back(pooled, norms[-1], both(nt(d_logits, head)))
    d_x = lax.dot_general(member, d_pooled / divisor, (((0,), (0,)), ((), ())), precision=HIGH)

    steps = Steps()
    g, g_norms = {}, {}

    def near(name):
        own, near, across, both_ways = g[name]
        near = near.astype(F32) + steps.swap(both_ways, FIRST).astype(F32)
        g[name] = own, near.astype(BF), steps.swap(across, FIRST)

    def blocks_of(value):
        value = value.astype(BF).reshape((-1, rows, value.shape[-1]))
        return [value[i] for i in range(value.shape[0])]

    def near_last(name):
        own, near, received = g[name]
        value = own.astype(F32) + received.astype(F32) + steps.swap(near, SECOND).astype(F32)
        g[name] = blocks_of(value)

    def near_low(name):
        keep, send = g[name]
        g[name] = blocks_of(keep.astype(F32) + steps.swap(send, low).astype(F32))

    def far_first(*names):
        for bit in high[:0:-1]:
            half = len(g[names[0]]) // 2
            got = steps.swap(jnp.stack([v for name in names for v in g[name][half:]]), bit)
            for k, name in enumerate(names):
                g[name] = [
                    (g[name][i].astype(F32) + got[k * half + i].astype(F32)).astype(BF) for i in range(half)
                ]

    def far_last(*names):
        got = steps.swap(jnp.stack([g[name][1] for name in names]), high[0])
        for k, name in enumerate(names):
            g[name] = (g[name][0], got[k])

    def back_ff(l, back):
        back = [steps.tie(back[0])] + back[1:]
        d_x, *grad, own, g_above = ff_backward(back, middles[l], norms[2 * l + 1], ff[l], flag)
        g["ff", l] = grad
        if l < LAYERS - 1:
            g_norms[2 * l + 2] = g_above
        steps.add(own)
        return [d_x, middles[l], norms[2 * l + 1], own, swap(own, INNER)]

    def back_attn(l, back):
        back = [steps.tie(back[0])] + back[1:]
        d_mid, *grad, own, g_above, row = attn_backward(
            back, xs[l], norms[2 * l], others[l], segq, segk, base, away, mixes[l], attn[l], flag
        )
        g["attn", l] = grad
        g_norms[2 * l + 1] = g_above
        steps.add(own)
        row = row[:8]
        got = steps.add(swap(row, OUTER))
        rows_in = [got, swap(got, INNER)]
        return [d_mid, xs[l], norms[2 * l], own, swap(own, INNER), *rows_in, real]

    g["head"] = (g_head[:mid], g_head[mid:])
    near_low("head")
    back = back_ff(2, [d_x])
    steps.next()
    near(("ff", 2))
    far_first("head")
    back = back_attn(2, back)
    steps.next()
    near(("attn", 2))
    near_last(("ff", 2))
    far_last("head")
    back = back_ff(1, back)
    steps.next()
    near(("ff", 1))
    near_last(("attn", 2))
    far_first(("ff", 2))
    back = back_attn(1, back)
    steps.next()
    near(("attn", 1))
    near_last(("ff", 1))
    far_first(("attn", 2))
    far_last(("ff", 2))
    back = back_ff(0, back)
    steps.next()
    near(("ff", 0))
    near_last(("attn", 1))
    far_first(("ff", 1))
    far_last(("attn", 2))
    back = back_attn(0, back)
    steps.next()
    d_x0, g_norms[0] = input_gradient([steps.tie(back[0])] + back[1:])
    theirs = steps.swap(of_inner(d_x0, inner), OUTER)
    near(("attn", 0))
    near_last(("ff", 0))
    far_first(("attn", 1))
    far_last(("ff", 1))
    theirs = halves(theirs, swap(theirs, INNER))
    g_patch = tn(jnp.concatenate([d_x0, theirs], 0), jnp.concatenate(pix, 0)).astype(BF)
    steps.add(g_patch)
    g["patch"] = (g_patch[:mid], g_patch[mid:])
    token = g_norms[0]
    *done, square_two = finish(2, [], g["attn", 2], g["ff", 2], token)
    steps.next()
    near_low("patch")
    near_last(("attn", 0))
    far_first(("ff", 0))
    far_last(("attn", 1))
    g_head = steps.tie(g["head"][0]).astype(F32) + g["head"][1].astype(F32)
    g_head = g_head + steps.swap(g_head, OUTER)
    g_norm = steps.tie(jnp.concatenate([g_norms[i] for i in range(6)] + [g_final], 0))
    g_norm = 0.5 * (g_norm + swap(g_norm, INNER))
    *done, square_one = finish(1, done, g["attn", 1], g["ff", 1], g_patch)
    steps.next()
    far_first(("attn", 0), "patch")
    far_last(("ff", 0))
    g_norm = g_norm + steps.swap(g_norm, OUTER)
    g_norm = jnp.moveaxis(g_norm.reshape(14, 2, -1, rows), 0, 2)
    g_norm = g_norm[0] + steps.swap(g_norm[1], low)
    g_head = halves(g_head, swap(g_head, INNER))
    steps.next()
    far_last(("attn", 0), "patch")
    g_norm = g_norm.reshape((2,) * len(high) + (14, rows))
    for bit in high[::-1]:
        g_norm = g_norm[0] + steps.swap(g_norm[1], bit)
    g_norm = g_norm.reshape(7, 2, rows)
    *done, square_zero = finish(0, done, g["attn", 0], g["ff", 0], g_patch)
    g_patch = g["patch"][0].astype(F32) + g["patch"][1].astype(F32)

    grads = (*done, g_patch, g_head, g_norm)
    first_model = (lax.axis_index("mp") == 0).astype(F32)
    squares = (square_two + square_one + square_zero)[0, 0] + jnp.sum(g_patch * g_patch) + first_model * (
        jnp.sum(g_head * g_head) + jnp.sum(g_norm * g_norm)
    )
    sums = jnp.stack([squares, loss_local * (outer >= 0)])
    sums = sums + swap(sums, INNER)
    sums = sums + swap(sums, OUTER)
    if len(high) == 2:
        (axis, a), (_, b) = high
        sums = sums + swap(sums, low)
        sums = (sums + swap(sums, (axis, a))) + (swap(sums, (axis, b)) + swap(sums, (axis, a | b)))
    else:
        for bit in bits:
            sums = sums + swap(sums, bit)
    loss = sums[1]
    grad_norm = jnp.sqrt(sums[0])
    clip = jnp.minimum(1.0, CLIP / grad_norm)

    def turned(values):
        return (*values[:3], values[3].swapaxes(1, 2), values[4].T, *values[5:])

    masters, firsts, seconds = turned(masters), turned(firsts), turned(seconds)
    outs = adam_all(clip, masters, grads, firsts, seconds)
    return (loss, grad_norm) + turned(outs[:7]) + turned(outs[7:14]) + turned(outs[14:])


def solution(mesh):
    weights = (
        P(None, None, "dp", "mp"),
        P(None, "mp", "dp"),
        P(None, "dp", "mp"),
        P(None, "mp", "dp"),
        P("mp", "dp"),
        P("dp", None),
        P(None, None, "dp"),
    )
    placed = (P("dp", "mp"), P("dp", None), P("dp"), P("dp", None), P()) + weights * 3
    return jax.shard_map(
        body, mesh=mesh, in_specs=placed, out_specs=(P(), P()) + weights * 3, check_vma=False
    )
```
